256 devices in a mesh: dp: 32 (over z, x), grp: 8 (over y, core).
Axes of the slice: x: 4, y: 4, z: 8, core: 2. Of those that a mesh axis runs over, the one named last changes fastest.
Arguments:
- byte_states: bfloat16 [32768, 1280], P('dp'), may hold values from -36 to 36
- norm_gain: float32 [1280], replicated, may hold values from 0.1 to 1.9
- patch_window: int32 [32, 1041], P('dp'), may hold values from -1 to 8192, as said below
- w_query: bfloat16 [1280, 4096], P('dp', 'grp'), may hold values from -0.11320094 to 0.11320094
- w_key: bfloat16 [1280, 4096], P('dp', 'grp'), may hold values from -9.056075 to 9.056075
- w_value: bfloat16 [1280, 4096], P('dp', 'grp'), may hold values from -0.15625 to 0.15625
- w_out: bfloat16 [4096, 4096], P('grp', 'dp'), may hold values from -0.09375 to 0.09375
- cotangent: bfloat16 [8192, 4096], P('dp', 'grp'), may hold values from -6 to 6
Outputs:
- patch_rows: bfloat16 [8192, 4096], P('dp', 'grp')
- grad_attended: float32 [8192, 4096], P('dp', 'grp')
The draws below stay inside these ranges and needn't reach their ends.
Inputs may be any that keep to these rules, and one draw needn't show every extreme that they name: `patch_window`: row d holds the patch numbers of the 1024 bytes of dp index d, preceded by those of the 16 bytes before them (-1 before the stream) and followed by that of the next byte (8192 after the stream). Patch numbers never fall and take every value from 0 to 8191. Between 128 and 640 patches end on the bytes of one dp index, 640 on some index in every draw; those ending on the bytes of dp index d are numbered from (d - 2) * 256 to (d + 3) * 256 - 1. The first patch ending on a device's bytes begins at most 15 bytes before them, exactly so on some device in every draw.
All inputs are finite; a program needn't handle non-finite values.
Results may differ from the reference program's by a relative error of at most 0.025.
Values may be sent and summed in bfloat16 or wider, within the bound.
No kernel may reach another device: no remote copies, remote signals or barrier semaphores. Data moves between devices by JAX's collectives and lax.ppermute only.
A program may use at most 64 MiB of HBM per device.

```python
import math
import jax
import jax.numpy as jnp
from jax import lax

E = 1280
D = 4096
HDIM = 128
MOST = 16
BYTES_DEV = 1024
BYTES = 32768
PATCHES = 8192
N_DP = 32
N_GRP = 8


def shared_weight(key):
    return jnp.clip(jax.random.normal(key, (E, D), jnp.float32), -4.0, 4.0)


def draw_w_query(key, part):
    common = shared_weight(key)
    return (common * E ** (-0.5)).astype(jnp.bfloat16)


def draw_w_key(key, part):
    key = jax.random.fold_in(key, 5)
    private = jnp.clip(jax.random.normal(key, (E, D), jnp.float32), -4.0, 4.0)
    return (private * E ** (-0.5)).astype(jnp.bfloat16)


def draw_byte_states(key, part):
    key = jax.random.fold_in(key, 11)
    subkeys = jax.random.split(key, 3)
    row_scale = jnp.exp(jax.random.uniform(subkeys[0], (BYTES, 1), jnp.float32, math.log(0.3), math.log(3.0)))
    col_scale = jnp.exp(jax.random.uniform(subkeys[1], (1, E), jnp.float32, math.log(0.3), math.log(3.0)))
    raw_values = jnp.clip(jax.random.normal(subkeys[2], (BYTES, E), jnp.float32), -4.0, 4.0)
    return (raw_values * row_scale * col_scale).astype(jnp.bfloat16)


def draw_patch_window(key, part):
    key = jax.random.fold_in(key, 7)
    subkeys = jax.random.split(key, 6)
    quarters = N_DP // 4
    spread = jax.random.randint(subkeys[0], (quarters,), 0, BYTES_DEV // 8 + 1)
    forced = jax.random.randint(subkeys[1], (), 0, quarters)
    spread = jnp.where(jnp.arange(quarters) == forced, BYTES_DEV // 8, spread)
    leader = jax.random.randint(subkeys[2], (quarters,), 0, 4)
    seats = jnp.arange(4)
    changes = jnp.where(seats[None, :] == leader[:, None], 3 * spread[:, None], -spread[:, None])
    counts = (BYTES_DEV // 4 + changes).reshape(N_DP)
    device_rank = jnp.arange(N_DP)
    tail_bytes = jax.random.randint(subkeys[3], (N_DP,), 0, MOST)
    longest = jax.random.randint(subkeys[4], (), 0, N_DP - 1)
    tail_bytes = jnp.where(device_rank == longest, MOST - 1, tail_bytes)
    tail_bytes = jnp.where(device_rank == N_DP - 2, MOST - 1, tail_bytes)
    tail_bytes = jnp.where(device_rank == N_DP - 1, 0, tail_bytes)
    scores = jax.vmap(lambda subkey: jax.random.permutation(subkey, BYTES_DEV))(jax.random.split(subkeys[5], N_DP))
    position = jnp.arange(BYTES_DEV)
    last_end = BYTES_DEV - 1 - tail_bytes
    masked = jnp.where(position[None, :] < last_end[:, None], scores, BYTES_DEV + position[None, :])
    ranking = jnp.argsort(jnp.argsort(masked, axis=1, stable=True), axis=1, stable=True)
    end_flags = (ranking < (counts - 1)[:, None]) | (position[None, :] == last_end[:, None])
    flat_ends = end_flags.reshape(BYTES).astype(jnp.int32)
    patch_ids = (jnp.cumsum(flat_ends) - flat_ends).astype(jnp.int32)
    padded = jnp.concatenate([jnp.full((MOST,), -1, jnp.int32), patch_ids, jnp.full((1,), PATCHES, jnp.int32)])
    indices = device_rank[:, None] * BYTES_DEV + jnp.arange(MOST + BYTES_DEV + 1)[None, :]
    return padded[indices].astype(jnp.int32)


def level_of(rng, dims, shards, low, top_value):
    factor_of = 1.0
    for dim, parts in shards:
        draws = jax.random.uniform(jax.random.fold_in(jax.random.fold_in(rng, 6), dim), (parts,), jnp.float32, low / len(shards), top_value / len(shards))
        factor_of = factor_of * jnp.repeat(jnp.exp(draws), dims[dim] // parts).reshape((-1,) + (1,) * (len(dims) - 1 - dim))
    return factor_of


def bell_draw(key, dims, scale, most, shards=(), kind=jnp.bfloat16):
    factor_of = level_of(key, dims, shards, -0.22, 0.18) if shards else 1.0
    entries = jax.random.normal(key, dims, jnp.float32) * scale * factor_of
    return jnp.minimum(jnp.maximum(entries, -most), most).astype(kind)


def setup_inputs(seed: int = 0) -> dict:
    streams_of = jax.random.split(jax.random.key(seed), 9)
    byte_states = draw_byte_states(jax.random.fold_in(streams_of[8], 71), 0)
    norm_gain = jnp.clip(1.0 + 0.18 * jax.random.normal(streams_of[1], (E,), jnp.float32), 0.1, 1.9)
    patch_window = draw_patch_window(jax.random.fold_in(streams_of[8], 71), 0)
    w_query = draw_w_query(jax.random.fold_in(streams_of[8], 71), 0)
    w_key = draw_w_key(jax.random.fold_in(streams_of[8], 71), 0)
    w_value = bell_draw(streams_of[5], (E, D), E ** -0.5, 0.15625, ((0, 32), (1, 8)))
    w_out = bell_draw(streams_of[6], (D, D), D ** -0.5, 0.09375, ((0, 8), (1, 32)))
    cotangent = bell_draw(streams_of[7], (PATCHES, D), 1.0, 6.0, ((0, 32), (1, 8)))
    return {"byte_states": byte_states, "norm_gain": norm_gain, "patch_window": patch_window, "w_query": w_query, "w_key": w_key, "w_value": w_value, "w_out": w_out, "cotangent": cotangent}


EPSILON = 1e-05
block_columns = 512

def normalize(states, gain):
    as_float = states.astype(jnp.float32)
    mean_square = lax.optimization_barrier(jnp.mean(as_float * as_float, axis=1, keepdims=True))
    return (as_float * lax.rsqrt(mean_square + EPSILON) * gain).astype(jnp.bfloat16)

def reference(byte_states, norm_gain, patch_window, w_query, w_key, w_value, w_out, cotangent):
    patch_ids = patch_window[:, MOST:MOST + BYTES_DEV].reshape(BYTES).astype(jnp.int32)
    normed = normalize(byte_states, norm_gain)
    patch_sizes = jax.ops.segment_sum(jnp.ones((BYTES,), jnp.float32), patch_ids, PATCHES)
    byte_sums = jax.ops.segment_sum(normed.astype(jnp.float32), patch_ids, PATCHES)
    pooled = (byte_sums / patch_sizes[:, None]).astype(jnp.bfloat16)
    queries = jnp.dot(pooled, w_query, preferred_element_type=jnp.float32).astype(jnp.bfloat16)
    width_block = min(block_columns, D)
    head_count = width_block // HDIM

    def head_block(number):
        first_col = number * width_block
        key_rows = jnp.dot(normed, lax.dynamic_slice_in_dim(w_key, first_col, width_block, 1), preferred_element_type=jnp.float32).astype(jnp.bfloat16)
        value_rows = jnp.dot(normed, lax.dynamic_slice_in_dim(w_value, first_col, width_block, 1), preferred_element_type=jnp.float32).astype(jnp.bfloat16)
        query_block = lax.dynamic_slice_in_dim(queries, first_col, width_block, 1)[patch_ids]
        product = query_block.astype(jnp.float32) * key_rows.astype(jnp.float32)
        scores = product.reshape(BYTES, head_count, HDIM).sum(axis=2) * HDIM ** (-0.5)
        highest = jnp.full((PATCHES, head_count), -1e+30, jnp.float32).at[patch_ids].max(scores)
        weights = jnp.exp(scores - highest[patch_ids])
        totals = jax.ops.segment_sum(weights, patch_ids, PATCHES)
        weighted = weights[:, :, None] * value_rows.astype(jnp.float32).reshape(BYTES, head_count, HDIM)
        sums = jax.ops.segment_sum(weighted.reshape(BYTES, width_block), patch_ids, PATCHES)
        result = sums.reshape(PATCHES, head_count, HDIM) / totals[:, :, None]
        return result.reshape(PATCHES, width_block).astype(jnp.bfloat16)
    blocks = lax.map(head_block, jnp.arange(D // width_block, dtype=jnp.int32))
    attended = jnp.transpose(blocks, (1, 0, 2)).reshape(PATCHES, D)
    block_rows = D // N_GRP
    mixed_rows = jnp.zeros((PATCHES, D), jnp.float32)
    for member in range(N_GRP):
        term = jnp.dot(attended[:, member * block_rows:(member + 1) * block_rows], w_out[member * block_rows:(member + 1) * block_rows, :], preferred_element_type=jnp.float32).astype(jnp.bfloat16)
        term = lax.optimization_barrier(term)
        mixed_rows = mixed_rows + term.astype(jnp.float32)
    patch_rows = (queries.astype(jnp.float32) + mixed_rows).astype(jnp.bfloat16)
    grad_attended = jnp.dot(cotangent, w_out.T, preferred_element_type=jnp.float32)
    return (patch_rows, grad_attended)
```

```python
import jax
import jax.numpy as jnp
from jax import lax
from jax.sharding import Mesh, PartitionSpec as P

HDIM = 128
MOST = 16
PAT_DEV = 256
PCAP = 640
EPSILON = 1e-05
DP = ("z", "x")
GRP = ("y", "c")


def ring(value, axis, steps):
    count = lax.axis_size(axis)
    return lax.ppermute(value, axis, [(i, (i + steps) % count) for i in range(count)])


def from_behind(value, steps):
    count = lax.axis_size(DP)
    leading, last = (max(0, -steps), min(count, count - steps))
    return lax.ppermute(value, DP, [(source, source + steps) for source in range(leading, last)])


def normalize(states, gain):
    as_float = states.astype(jnp.float32)
    mean_square = jnp.mean(as_float * as_float, axis=1, keepdims=True)
    return (as_float * lax.rsqrt(mean_square + EPSILON) * gain).astype(jnp.bfloat16)


def place(buffer, block, index, dim):
    return lax.dynamic_update_slice_in_dim(buffer, jnp.expand_dims(block, dim), index, dim)


def gather_x(block):
    me = lax.axis_index("x")
    count = lax.axis_size("x")
    arrived = [ring(block, "x", steps) for steps in range(1, count)]
    out = place(jnp.zeros((count,) + block.shape, block.dtype), block, me, 0)
    for steps, piece in enumerate(arrived, 1):
        out = place(out, piece, (me - steps) % count, 0)
    return out


def gather_z(block):
    me = lax.axis_index("z")
    count = lax.axis_size("z")
    out = place(jnp.zeros((count,) + block.shape, block.dtype), block, me, 0)
    up = down = block
    for steps in range(1, count // 2):
        up = ring(up, "z", 1)
        down = ring(down, "z", -1)
        out = place(out, up, (me - steps) % count, 0)
        out = place(out, down, (me + steps) % count, 0)
    half = block.shape[-1] // 2
    first = ring(up[..., :half], "z", 1)
    second = ring(down[..., half:], "z", -1)
    last = jnp.concatenate([first, second], axis=-1)
    return place(out, last, (me + count // 2) % count, 0)


def per_device(byte_states, norm_gain, patch_window, w_query, w_key, w_value, w_out, cotangent):
    byte_count = byte_states.shape[0]
    columns = w_query.shape[1]
    width = byte_states.shape[1]
    head_count = columns // HDIM
    highest_precision = lax.Precision.HIGHEST
    weight_full = lax.all_gather(w_out.T, DP, axis=0, tiled=True)
    packed = jnp.concatenate([w_query, w_key, w_value], axis=1)
    half = packed.shape[1] // 2
    rows = packed.shape[0]
    left = gather_z(gather_x(packed[:, :half]))
    right = gather_z(packed[:, half:])
    right = gather_x(right).transpose(1, 0, 2, 3)
    left = left.reshape(width, half)
    right = right.reshape(width, half)

    normed = normalize(byte_states, norm_gain)
    before = from_behind(normed[byte_count - MOST :], 1)
    window = jnp.concatenate([before, normed], axis=0)
    span_rows = window.shape[0]
    patch_ids = patch_window[0, :span_rows]
    first_patch = patch_window[0, MOST]
    patch_total = patch_window[0, span_rows] - first_patch
    relative = patch_ids - first_patch
    owned = (relative >= 0) & (relative < patch_total)
    segment = jnp.where(owned, relative, PCAP)
    slot_numbers = jnp.arange(PCAP, dtype=jnp.int32)
    member = segment[None, :] == slot_numbers[:, None]
    member_half = member.astype(jnp.bfloat16)
    member_full = member.astype(jnp.float32)
    patch_sizes = jnp.sum(member_full, axis=1)
    byte_sums = jnp.dot(member_half, window, preferred_element_type=jnp.float32)
    pooled = (byte_sums / jnp.where(patch_sizes > 0, patch_sizes, 1.0)[:, None]).astype(
        jnp.bfloat16
    )
    device_index = lax.axis_index(DP)
    landing = (
        (device_index - 2) * PAT_DEV - first_patch + jnp.arange(5 * PAT_DEV, dtype=jnp.int32)
    )
    chosen = (landing[:, None] == slot_numbers[None, :]).astype(jnp.bfloat16)

    queries = jnp.dot(pooled, left[:, :columns], preferred_element_type=jnp.float32).astype(
        jnp.bfloat16
    )
    key_part = jnp.dot(window, left[:, columns:], preferred_element_type=jnp.float32)
    rest = jnp.dot(window, right, preferred_element_type=jnp.float32)
    split = 2 * columns - half
    key_rows = jnp.concatenate([key_part, rest[:, :split]], axis=1).astype(jnp.bfloat16)
    value_rows = rest[:, split:].astype(jnp.bfloat16)
    query_rows = lax.dot_general(
        member_half, queries, (((0,), (0,)), ((), ())), preferred_element_type=jnp.float32
    )
    product = query_rows * key_rows.astype(jnp.float32)
    scores = product.reshape(span_rows, head_count, HDIM).sum(axis=2) * HDIM ** (-0.5)
    highest = jnp.max(jnp.where(member[:, :, None], scores[None, :, :], -1e30), axis=1)
    highest_rows = lax.dot_general(
        member_full,
        highest,
        (((0,), (0,)), ((), ())),
        precision=highest_precision,
        preferred_element_type=jnp.float32,
    )
    weights = jnp.exp(jnp.where(owned[:, None], scores - highest_rows, -1e30))
    totals = jnp.dot(
        member_full, weights, precision=highest_precision, preferred_element_type=jnp.float32
    )
    weighted = weights[:, :, None] * value_rows.astype(jnp.float32).reshape(
        span_rows, head_count, HDIM
    )
    weighted = weighted.reshape(span_rows, columns)
    high = weighted.astype(jnp.bfloat16)
    low = (weighted - high.astype(jnp.float32)).astype(jnp.bfloat16)
    sums = jnp.dot(member_half, high, preferred_element_type=jnp.float32) + jnp.dot(
        member_half, low, preferred_element_type=jnp.float32
    )
    result = sums.reshape(PCAP, head_count, HDIM) / jnp.where(totals > 0, totals, 1.0)[:, :, None]
    attended = result.reshape(PCAP, columns).astype(jnp.bfloat16)

    def rehome(source):
        spread = jnp.dot(chosen, source, preferred_element_type=jnp.float32).astype(jnp.bfloat16)
        spread = spread.reshape(5, PAT_DEV, columns)
        landed = spread[2].astype(jnp.float32)
        for offset in (-2, -1, 1, 2):
            landed = landed + from_behind(spread[offset + 2], offset).astype(jnp.float32)
        return landed

    attended_home = rehome(attended).astype(jnp.bfloat16)
    queries_home = rehome(queries)
    terms = lax.dot_general(
        attended_home, weight_full, (((1,), (1,)), ((), ())), preferred_element_type=jnp.float32
    )
    mixed_rows = lax.psum_scatter(
        terms.astype(jnp.bfloat16), GRP, scatter_dimension=1, tiled=True
    ).astype(jnp.float32)
    patch_rows = (queries_home + mixed_rows).astype(jnp.bfloat16)
    gradient = jnp.dot(
        lax.all_gather(cotangent, GRP, axis=1, tiled=True),
        weight_full,
        preferred_element_type=jnp.float32,
    )
    return (patch_rows, gradient)


def solution(mesh):
    fine = Mesh(mesh.devices.reshape(8, 4, 4, 2), DP + GRP)
    return jax.shard_map(
        per_device,
        mesh=fine,
        in_specs=(
            P(DP, None),
            P(),
            P(DP, None),
            P(DP, GRP),
            P(DP, GRP),
            P(DP, GRP),
            P(GRP, DP),
            P(DP, GRP),
        ),
        out_specs=(P(DP, GRP), P(DP, GRP)),
        check_vma=False,
    )
```

```python
import jax
import jax.numpy as jnp
from jax import lax
from jax.experimental import pallas as pl
from jax.experimental.pallas import tpu as pltpu
from jax.sharding import Mesh, PartitionSpec as P

HDIM = 128
MOST = 16
PAT_DEV = 256
PCAP = 640
OFFSETS = (-2, -1, 0, 1, 2)
EPSILON = 1e-05
DP = ("z", "x")
GRP = ("y", "c")
VMEM_BYTES = 52 * 1024 * 1024


def ring(value, axis, steps):
    count = lax.axis_size(axis)
    return lax.ppermute(value, axis, [(i, (i + steps) % count) for i in range(count)])


def from_behind(value, steps):
    count = lax.axis_size(DP)
    leading, last = (max(0, -steps), min(count, count - steps))
    return lax.ppermute(value, DP, [(source, source + steps) for source in range(leading, last)])


def vmem_call(kernel, out_shape, **more):
    params = pltpu.CompilerParams(vmem_limit_bytes=VMEM_BYTES)
    return pl.pallas_call(kernel, out_shape=out_shape, compiler_params=params, **more)


def one_hot(rows, columns):
    return jnp.where(rows == columns, 1.0, 0.0).astype(jnp.bfloat16)


def f32_dot(a, b, contract=((1,), (0,))):
    return lax.dot_general(a, b, (contract, ((), ())), preferred_element_type=jnp.float32)


def prepare_kernel(before, states, gain, segment, key_order, value_order, key_out, value_out, pool_out):
    width = states.shape[1]
    for source, start in ((before, 0), (states, MOST)):
        rows = source[...].astype(jnp.float32)
        mean_square = jnp.mean(rows * rows, axis=1, keepdims=True)
        normed = rows * lax.rsqrt(mean_square + EPSILON) * gain[...]
        pool_rows = normed.astype(jnp.bfloat16)
        value_out[pl.ds(start, rows.shape[0]), :] = pool_rows
    normed = value_out[...]
    column = lax.broadcasted_iota(jnp.int32, (width, width), 0)
    key_out[...] = f32_dot(normed, one_hot(column, key_order[...])).astype(jnp.bfloat16)
    slot = lax.broadcasted_iota(jnp.int32, (PCAP, normed.shape[0]), 0)
    member = slot == segment[...]
    sizes = jnp.sum(jnp.where(member, 1.0, 0.0), axis=1, keepdims=True)
    sums = f32_dot(jnp.where(member, 1.0, 0.0).astype(jnp.bfloat16), key_out[...])
    pool_out[...] = (sums / jnp.where(sizes > 0, sizes, 1.0)).astype(jnp.bfloat16)
    value_out[...] = f32_dot(normed, one_hot(column, value_order[...])).astype(jnp.bfloat16)


def attend_kernel(key_in, value_in, pooled, segment_row, segment_col, base, *rest):
    key_blocks, value_blocks = rest[:9], rest[9:13]
    places = rest[13:23]
    key_weight, value_weight, product, value_ext, sems = rest[23:]
    span = key_in.shape[0]
    padded = product.shape[0]
    columns = value_weight.shape[1]
    depth = key_blocks[0].shape[0]
    copies = []
    row = 0
    for number in range(8):
        if number == 4:
            spots = ((4, 0, columns), (5, columns, columns))
        else:
            spots = ((number if number < 4 else number + 1, 0, 2 * columns),)
        for source, lane, lanes in spots:
            copies.append((key_blocks[source], key_weight.at[pl.ds(row, depth), pl.ds(lane, lanes)]))
        row += depth
    tall = value_blocks[0].shape[0]
    for number, block in enumerate(value_blocks):
        copies.append((block, value_weight.at[pl.ds(number * tall, tall), :]))
    copies = [
        pltpu.make_async_copy(source, target, sems.at[i]) for i, (source, target) in enumerate(copies)
    ]
    for copy in copies:
        copy.start()
    slot_col = lax.broadcasted_iota(jnp.int32, (span, PCAP), 1)
    reader = one_hot(slot_col, segment_col[...])
    value_ext[...] = jnp.where(
        lax.broadcasted_iota(jnp.int32, value_ext.shape, 2) < HDIM, 0.0, 1.0
    ).astype(jnp.bfloat16)
    product[pl.ds(span, padded - span), :] = jnp.zeros((padded - span, columns), jnp.float32)
    for copy in copies:
        copy.wait()
    queries = f32_dot(pooled[...], key_weight[:, :columns]).astype(jnp.bfloat16)
    wide = 2 * HDIM
    for start in range(0, columns, wide):
        lanes = slice(start, start + wide)
        keys = f32_dot(key_in[...], key_weight[:, columns + start : columns + start + wide])
        read = f32_dot(reader, queries[:, lanes])
        product[:span, lanes] = read * keys.astype(jnp.bfloat16).astype(jnp.float32)
        values = f32_dot(value_in[...], value_weight[:, lanes]).astype(jnp.bfloat16)
        value_ext[start // HDIM, :span, :HDIM] = values[:, :HDIM]
        value_ext[start // HDIM + 1, :span, :HDIM] = values[:, HDIM:]
    heads = columns // HDIM
    lane = lax.broadcasted_iota(jnp.int32, (8, columns), 1)
    head = lax.broadcasted_iota(jnp.int32, (8, columns), 0)
    low_lane = head * HDIM
    picker = jnp.where((lane >= low_lane) & (lane < low_lane + HDIM), 1.0, 0.0).astype(jnp.bfloat16)
    left = product[...]
    scores = jnp.zeros((8, padded), jnp.float32)
    for _ in range(3):
        part = left.astype(jnp.bfloat16)
        scores = scores + f32_dot(picker, part, ((1,), (1,)))
        left = left - part.astype(jnp.float32)
    scores = scores * HDIM ** (-0.5)
    segment = jnp.broadcast_to(segment_row[...], (8, padded))
    forward = backward = scores
    step = 1
    while step < span:
        same = pltpu.roll(segment, step, 1) == segment
        forward = jnp.maximum(forward, jnp.where(same, pltpu.roll(forward, step, 1), -1e30))
        same = pltpu.roll(segment, padded - step, 1) == segment
        backward = jnp.maximum(
            backward, jnp.where(same, pltpu.roll(backward, padded - step, 1), -1e30)
        )
        step *= 2
    weights = jnp.exp(scores - jnp.maximum(forward, backward))
    member = lax.broadcasted_iota(jnp.int32, (PCAP, padded), 0) == segment_row[...]
    gathered = []
    for number in range(heads):
        spread = jnp.where(member, weights[number : number + 1, :], 0.0).astype(jnp.bfloat16)
        total = f32_dot(spread, value_ext[number])
        divisor = total[:, HDIM:]
        gathered.append((total[:, :HDIM] / jnp.where(divisor > 0, divisor, 1.0)).astype(jnp.bfloat16))
    attended = jnp.concatenate(gathered, axis=1)
    for number in range(5):
        landing = lax.broadcasted_iota(jnp.int32, (PAT_DEV, PCAP), 0) + (
            base[0] + number * PAT_DEV
        )
        chosen = one_hot(landing, lax.broadcasted_iota(jnp.int32, (PAT_DEV, PCAP), 1))
        places[number][...] = f32_dot(chosen, attended).astype(jnp.bfloat16)
        places[5 + number][...] = f32_dot(chosen, queries).astype(jnp.bfloat16)


def term_kernel(which, *refs):
    pieces, weight, out, landed = refs[:5], refs[5], refs[6], refs[7]

    @pl.when(pl.program_id(0) == 0)
    def _():
        total = pieces[0][...].astype(jnp.float32)
        for piece in pieces[1:]:
            total = total + piece[...].astype(jnp.float32)
        landed[...] = total.astype(jnp.bfloat16)

    out[0] = f32_dot(landed[...], weight[...], ((1,), (1,))).astype(out.dtype)


def gradient_kernel(which, mine, other, weight, out):
    step = pl.program_id(0)

    @pl.when(step == 0)
    def _():
        out[...] = jnp.zeros_like(out)

    @pl.when(step < 4)
    def _():
        out[...] += f32_dot(mine[0], weight[...])

    @pl.when(step >= 4)
    def _():
        out[...] += f32_dot(other[0], weight[...])


def per_device(byte_states, norm_gain, patch_window, w_query, w_key, w_value, w_out, cotangent):
    byte_count, width = byte_states.shape
    columns = w_query.shape[1]
    rows = w_query.shape[0]
    span = byte_count + MOST
    padded = -(-span // HDIM) * HDIM
    my_z, my_x, my_y, my_c = (lax.axis_index(name) for name in DP + GRP)
    half = jax.ShapeDtypeStruct

    weight_full = lax.all_gather(w_out.T, DP, axis=0, tiled=True)
    packed = jnp.concatenate([w_query, w_key], axis=1)
    key_x = [packed] + [ring(packed, "x", steps) for steps in (1, 2, 3)]
    value_up, value_down = ring(w_value, "z", 1), ring(w_value, "z", -1)
    before = from_behind(byte_states[byte_count - MOST :], 1)
    key_own = jnp.concatenate(key_x, axis=0)
    value_z = {0: w_value, 1: value_up, 7: value_down}
    key_own, value_up, value_down, before = lax.optimization_barrier(
        (key_own, value_up, value_down, before)
    )

    key_z = {0: key_own, 1: ring(key_own, "z", 1), 7: ring(key_own, "z", -1)}
    value_z[2], value_z[6] = ring(value_up, "z", 1), ring(value_down, "z", -1)
    value_z[2], value_z[6] = lax.optimization_barrier((value_z[2], value_z[6]))
    value_z[3], value_z[5] = ring(value_z[2], "z", 1), ring(value_z[6], "z", -1)

    patch_ids = patch_window[:, :span]
    first_patch = patch_window[0, MOST]
    patch_total = patch_window[0, span] - first_patch
    relative = patch_ids - first_patch
    owned = (relative >= 0) & (relative < patch_total)
    segment = jnp.where(owned, relative, PCAP)
    segment_wide = jnp.pad(segment, ((0, 0), (0, padded - span)), constant_values=PCAP)
    segment_col = segment.reshape(span, 1)
    base = ((lax.axis_index(DP) - 2) * PAT_DEV - first_patch).reshape(1)
    spot = jnp.arange(width, dtype=jnp.int32)
    wide = width // 8
    key_from = ((my_z - spot // wide) % 8) * wide + ((my_x - spot % wide // rows) % 4) * rows
    key_from = (key_from + spot % rows)[None, :]
    tall = width // 4
    value_from = ((my_z - spot % tall // rows) % 8) * wide + ((my_x - spot // tall) % 4) * rows
    value_from = (value_from + spot % rows)[None, :]
    key_in, value_in, pooled = vmem_call(
        prepare_kernel,
        (
            half((span, width), jnp.bfloat16),
            half((span, width), jnp.bfloat16),
            half((PCAP, width), jnp.bfloat16),
        ),
    )(before, byte_states, norm_gain[None, :], segment, key_from, value_from)

    key_z[1], key_z[7], value_z[3], value_z[5], pooled = lax.optimization_barrier(
        (key_z[1], key_z[7], value_z[3], value_z[5], pooled)
    )
    key_z[2], key_z[6] = ring(key_z[1], "z", 1), ring(key_z[7], "z", -1)
    mid = columns // 2
    value_4a = ring(value_z[3][:, :mid], "z", 1)
    value_4b = ring(value_z[5][:, mid:], "z", -1)
    value_own = jnp.concatenate(
        [value_z[s] for s in range(4)]
        + [jnp.concatenate([value_4a, value_4b], axis=1)]
        + [value_z[s] for s in range(5, 8)],
        axis=0,
    )
    key_z[2], key_z[6], value_own = lax.optimization_barrier((key_z[2], key_z[6], value_own))
    value_x = [value_own] + [ring(value_own, "x", steps) for steps in (1, 2, 3)]
    key_z[3], key_z[5] = ring(key_z[2], "z", 1), ring(key_z[6], "z", -1)
    key_z[3], key_z[5] = lax.optimization_barrier((key_z[3], key_z[5]))
    key_4a = ring(key_z[3][:, :columns], "z", 1)
    key_4b = ring(key_z[5][:, columns:], "z", -1)
    key_blocks = [key_z[0], key_z[1], key_z[2], key_z[3], key_4a, key_4b]
    key_blocks += [key_z[5], key_z[6], key_z[7]]

    cot_y = [cotangent] + [ring(cotangent, "y", steps) for steps in (1, 2, 3)]
    cot_mine = jnp.stack(cot_y)
    cot_other = ring(cot_mine, "c", 1)

    vmem = pl.BlockSpec(memory_space=pltpu.VMEM)
    anywhere = pl.BlockSpec(memory_space=pl.ANY)
    place = half((PAT_DEV, columns), jnp.bfloat16)
    places = vmem_call(
        attend_kernel,
        (place,) * 10,
        in_specs=[vmem] * 5 + [pl.BlockSpec(memory_space=pltpu.SMEM)] + [anywhere] * 13,
        out_specs=(vmem,) * 10,
        scratch_shapes=[
            pltpu.VMEM((width, 2 * columns), jnp.bfloat16),
            pltpu.VMEM((width, columns), jnp.bfloat16),
            pltpu.VMEM((padded, columns), jnp.float32),
            pltpu.VMEM((columns // HDIM, padded, 2 * HDIM), jnp.bfloat16),
            pltpu.SemaphoreType.DMA((13,)),
        ],
    )(key_in, value_in, pooled, segment_wide, segment_col, base, *key_blocks, *value_x)

    pieces = [places[2]] + [
        from_behind(places[offset + 2], offset) for offset in (-2, 2, -1, 1)
    ]
    pieces = lax.optimization_barrier(pieces)

    def terms(core):
        which = 2 * ((my_y + jnp.arange(4, dtype=jnp.int32)) % 4) + core
        piece = pl.BlockSpec((PAT_DEV, columns), lambda i, which: (0, 0))
        return vmem_call(
            term_kernel,
            half((4, PAT_DEV, columns), jnp.bfloat16),
            grid_spec=pltpu.PrefetchScalarGridSpec(
                num_scalar_prefetch=1,
                grid=(4,),
                in_specs=[piece] * 5
                + [pl.BlockSpec((columns, columns), lambda i, which: (which[i], 0))],
                out_specs=pl.BlockSpec((1, PAT_DEV, columns), lambda i, which: (i, 0, 0)),
                scratch_shapes=[pltpu.VMEM((PAT_DEV, columns), jnp.bfloat16)],
            ),
        )(which.astype(jnp.int32), *pieces, weight_full)

    theirs = terms(1 - my_c)
    arrived = ring(theirs, "c", 1)
    mine = terms(my_c)
    paired = [
        (mine[d].astype(jnp.float32) + arrived[d].astype(jnp.float32)).astype(jnp.bfloat16)
        for d in range(4)
    ]
    paired = lax.optimization_barrier(paired)
    mixed = paired[0].astype(jnp.float32)
    for steps in (2, 1, 3):
        mixed = mixed + ring(paired[steps], "y", steps).astype(jnp.float32)

    later = lax.optimization_barrier((theirs,) + tuple(places[5:]))[1:]
    queries = later[2].astype(jnp.float32)
    for offset in (-2, 2, -1, 1):
        queries = queries + from_behind(later[offset + 2], offset).astype(jnp.float32)
    patch_rows = (queries + mixed).astype(jnp.bfloat16)

    turn = (my_y - jnp.arange(4, dtype=jnp.int32)) % 4
    which = jnp.concatenate([2 * turn + my_c, 2 * turn + 1 - my_c]).astype(jnp.int32)
    gradient = vmem_call(
        gradient_kernel,
        half((PAT_DEV, columns), jnp.float32),
        grid_spec=pltpu.PrefetchScalarGridSpec(
            num_scalar_prefetch=1,
            grid=(8,),
            in_specs=[
                pl.BlockSpec((1, PAT_DEV, columns), lambda i, which: (jnp.minimum(i, 3), 0, 0)),
                pl.BlockSpec((1, PAT_DEV, columns), lambda i, which: (jnp.maximum(i - 4, 0), 0, 0)),
                pl.BlockSpec((columns, columns), lambda i, which: (which[i], 0)),
            ],
            out_specs=pl.BlockSpec((PAT_DEV, columns), lambda i, which: (0, 0)),
        ),
    )(which, cot_mine, cot_other, weight_full)
    return (patch_rows, gradient)


def solution(mesh):
    fine = Mesh(mesh.devices.reshape(8, 4, 4, 2), DP + GRP)
    return jax.shard_map(
        per_device,
        mesh=fine,
        in_specs=(
            P(DP, None),
            P(),
            P(DP, None),
            P(DP, GRP),
            P(DP, GRP),
            P(DP, GRP),
            P(GRP, DP),
            P(DP, GRP),
        ),
        out_specs=(P(DP, GRP), P(DP, GRP)),
        check_vma=False,
    )
```

```python
import functools

import jax
import jax.numpy as jnp
from jax import lax
from jax.experimental import pallas as pl
from jax.experimental.pallas import tpu as pltpu
from jax.sharding import Mesh, PartitionSpec as P

HDIM = 128
MOST = 16
PAT_DEV = 256
PCAP = 640
OFFSETS = (-2, -1, 0, 1, 2)
EPSILON = 1e-05
DP = ("z", "x")
GRP = ("y", "c")
VMEM_BYTES = 52 * 1024 * 1024


def ring(value, axis, steps):
    count = lax.axis_size(axis)
    return lax.ppermute(value, axis, [(i, (i + steps) % count) for i in range(count)])


def from_behind(value, steps):
    count = lax.axis_size(DP)
    leading, last = (max(0, -steps), min(count, count - steps))
    return lax.ppermute(value, DP, [(source, source + steps) for source in range(leading, last)])


def vmem_call(kernel, out_shape, **more):
    params = pltpu.CompilerParams(vmem_limit_bytes=VMEM_BYTES)
    return pl.pallas_call(kernel, out_shape=out_shape, compiler_params=params, **more)


def one_hot(rows, columns):
    return jnp.where(rows == columns, 1.0, 0.0).astype(jnp.bfloat16)


def f32_dot(a, b, contract=((1,), (0,))):
    return lax.dot_general(a, b, (contract, ((), ())), preferred_element_type=jnp.float32)


def prepare_kernel(before, states, gain, segment, query_order, normed_out, pool_out):
    width = states.shape[1]
    for source, start in ((before, 0), (states, MOST)):
        rows = source[...].astype(jnp.float32)
        mean_square = jnp.mean(rows * rows, axis=1, keepdims=True)
        normed = rows * lax.rsqrt(mean_square + EPSILON) * gain[...]
        normed_out[pl.ds(start, rows.shape[0]), :] = normed.astype(jnp.bfloat16)
    normed = normed_out[...]
    slot = lax.broadcasted_iota(jnp.int32, (PCAP, normed.shape[0]), 0)
    member = jnp.where(slot == segment[...], 1.0, 0.0)
    sizes = jnp.sum(member, axis=1, keepdims=True)
    sums = f32_dot(member.astype(jnp.bfloat16), normed)
    pooled = (sums / jnp.where(sizes > 0, sizes, 1.0)).astype(jnp.bfloat16)
    column = lax.broadcasted_iota(jnp.int32, (width, width), 0)
    pool_out[...] = f32_dot(pooled, one_hot(column, query_order[...])).astype(jnp.bfloat16)


def project_kernel(place, normed, *rest):
    blocks, keys, values, weight, sems = rest[:9], rest[9], rest[10], rest[11], rest[12]
    depth = blocks[0].shape[0]
    columns = keys.shape[1]
    copies = []
    for steps in range(8):
        row = pl.multiple_of(((place[0] + 8 - steps) & 7) * depth, 16)
        if steps == 4:
            spots = ((4, 0, columns), (5, columns, columns))
        else:
            spots = ((steps if steps < 4 else steps + 1, 0, 2 * columns),)
        for source, lane, lanes in spots:
            target = weight.at[pl.ds(row, depth), pl.ds(lane, lanes)]
            copies.append(pltpu.make_async_copy(blocks[source], target, sems.at[source]))
    for copy in copies:
        copy.start()
    for copy in copies:
        copy.wait()
    for out, start in ((keys, 0), (values, columns)):
        out[...] = f32_dot(normed[...], weight[:, start : start + columns]).astype(jnp.bfloat16)


def attend_kernel(keys, values, pooled, segment_row, segment_col, place, *rest):
    blocks, places = rest[:4], rest[4:14]
    weight, product, value_ext, sems = rest[14:]
    span, columns = keys.shape
    padded = product.shape[0]
    tall = blocks[0].shape[0]
    copies = [
        pltpu.make_async_copy(block, weight.at[pl.ds(number * tall, tall), :], sems.at[number])
        for number, block in enumerate(blocks)
    ]
    for copy in copies:
        copy.start()
    slot_col = lax.broadcasted_iota(jnp.int32, (span, PCAP), 1)
    reader = one_hot(slot_col, segment_col[...])
    heads = columns // HDIM
    for number in range(heads):
        value_ext[number, :span, :HDIM] = values[:, number * HDIM : (number + 1) * HDIM]
    value_ext[:, span:, :HDIM] = jnp.zeros((heads, padded - span, HDIM), jnp.bfloat16)
    value_ext[:, :, HDIM:] = jnp.ones((heads, padded, HDIM), jnp.bfloat16)
    product[pl.ds(span, padded - span), :] = jnp.zeros((padded - span, columns), jnp.float32)
    for copy in copies:
        copy.wait()
    queries = f32_dot(pooled[...], weight[...]).astype(jnp.bfloat16)
    product[:span, :] = f32_dot(reader, queries) * keys[...].astype(jnp.float32)
    lane = lax.broadcasted_iota(jnp.int32, (8, columns), 1)
    low_lane = lax.broadcasted_iota(jnp.int32, (8, columns), 0) * HDIM
    picker = jnp.where((lane >= low_lane) & (lane < low_lane + HDIM), 1.0, 0.0).astype(jnp.bfloat16)
    left = product[...]
    scores = jnp.zeros((8, padded), jnp.float32)
    for _ in range(3):
        part = left.astype(jnp.bfloat16)
        scores = scores + f32_dot(picker, part, ((1,), (1,)))
        left = left - part.astype(jnp.float32)
    scores = scores * HDIM ** (-0.5)
    segment = jnp.broadcast_to(segment_row[...], (8, padded))
    forward = backward = scores
    step = 1
    while step < span:
        same = pltpu.roll(segment, step, 1) == segment
        forward = jnp.maximum(forward, jnp.where(same, pltpu.roll(forward, step, 1), -1e30))
        same = pltpu.roll(segment, padded - step, 1) == segment
        backward = jnp.maximum(
            backward, jnp.where(same, pltpu.roll(backward, padded - step, 1), -1e30)
        )
        step *= 2
    weights = jnp.exp(scores - jnp.maximum(forward, backward))
    member = lax.broadcasted_iota(jnp.int32, (PCAP, padded), 0) == segment_row[...]
    gathered = []
    for number in range(heads):
        spread = jnp.where(member, weights[number : number + 1, :], 0.0).astype(jnp.bfloat16)
        total = f32_dot(spread, value_ext[number])
        divisor = total[:, HDIM:]
        gathered.append((total[:, :HDIM] / jnp.where(divisor > 0, divisor, 1.0)).astype(jnp.bfloat16))
    attended = jnp.concatenate(gathered, axis=1)
    for number in range(5):
        landing = lax.broadcasted_iota(jnp.int32, (PAT_DEV, PCAP), 0) + (
            place[4] + number * PAT_DEV
        )
        chosen = one_hot(landing, lax.broadcasted_iota(jnp.int32, (PAT_DEV, PCAP), 1))
        places[number][...] = f32_dot(chosen, attended).astype(jnp.bfloat16)
        places[5 + number][...] = f32_dot(chosen, queries).astype(jnp.bfloat16)


def term_kernel(partner, place, *refs):
    pieces, blocks, out, buffer, sems = refs[:5], refs[5:13], refs[13], refs[14], refs[15]
    z, y, c = place[0], place[2], place[3]
    parity = (z + (1 - c if partner else c)) & 1
    for pair in range(4):
        for odd in range(2):

            @pl.when(parity == odd)
            def _(pair=pair, odd=odd):
                pltpu.make_async_copy(blocks[2 * pair + odd], buffer.at[pair], sems.at[pair]).start()

    total = pieces[0][...].astype(jnp.float32)
    for piece in pieces[1:]:
        total = total + piece[...].astype(jnp.float32)
    landed = total.astype(jnp.bfloat16)
    for pair in range(4):
        pltpu.make_async_copy(blocks[2 * pair], buffer.at[pair], sems.at[pair]).wait()
        group = (z + 8 - (2 * pair + parity)) & 7
        slot = ((group >> 1) + 4 - y) & 3
        out[slot] = f32_dot(landed, buffer[pair], ((1,), (1,))).astype(out.dtype)


def gradient_kernel(steps, place, mine, other, *refs):
    blocks, out, sums = refs[: len(steps)], refs[-1], refs[len(steps) : -1]
    z, y, c = place[0], place[2], place[3]
    total = sums[0][...] if sums else jnp.zeros(out.shape, jnp.float32)
    for step, block in zip(steps, blocks):
        group = (z + 8 - step) & 7
        slot = (y + 4 - (group >> 1)) & 3
        picked = jnp.where((group & 1) == c, mine[slot], other[slot])
        total = total + f32_dot(picked, block[...])
    out[...] = total


def per_device(byte_states, norm_gain, patch_window, w_query, w_key, w_value, w_out, cotangent):
    byte_count, width = byte_states.shape
    rows, columns = w_query.shape
    span = byte_count + MOST
    padded = -(-span // HDIM) * HDIM
    my_z, my_x, my_y, my_c = (lax.axis_index(name) for name in DP + GRP)
    shape = jax.ShapeDtypeStruct
    barrier = lax.optimization_barrier

    def along_x(block):
        turns = [block] + [ring(block, "x", steps) for steps in (1, 2, 3)]

        def assemble(turns):
            ordered = []
            for number in range(4):
                behind = (my_x + 4 - number) & 3
                picked = turns[3]
                for steps in (2, 1, 0):
                    picked = jnp.where(behind == steps, turns[steps], picked)
                ordered.append(picked)
            return jnp.concatenate(ordered, axis=0)

        return turns, assemble

    packed = jnp.concatenate([w_key, w_value], axis=1)
    turns, assemble = along_x(packed)
    query_z = {0: w_query, 1: ring(w_query, "z", 1), 7: ring(w_query, "z", -1)}
    before = from_behind(byte_states[byte_count - MOST :], 1)
    turns, query_z[1], query_z[7], before = barrier((turns, query_z[1], query_z[7], before))
    key_own = assemble(turns)

    key_z = {0: key_own, 1: ring(key_own, "z", 1), 7: ring(key_own, "z", -1)}
    query_z[2], query_z[6] = ring(query_z[1], "z", 1), ring(query_z[7], "z", -1)
    query_z[2], query_z[6], before, window = barrier(
        (query_z[2], query_z[6], before, patch_window)
    )
    query_z[3], query_z[5] = ring(query_z[2], "z", 1), ring(query_z[6], "z", -1)

    patch_ids = window[:, :span]
    first_patch = window[0, MOST]
    patch_total = window[0, span] - first_patch
    relative = patch_ids - first_patch
    owned = (relative >= 0) & (relative < patch_total)
    segment = jnp.where(owned, relative, PCAP)
    segment_wide = jnp.pad(segment, ((0, 0), (0, padded - span)), constant_values=PCAP)
    segment_col = segment.reshape(span, 1)
    base = (lax.axis_index(DP) - 2) * PAT_DEV - first_patch
    place = jnp.stack([my_z, my_x, my_y, my_c, base]).astype(jnp.int32)
    spot = jnp.arange(width, dtype=jnp.int32)
    wide, tall = width // 8, width // 4
    query_from = ((my_z - spot % tall // rows) % 8) * wide + ((my_x - spot // tall) % 4) * rows
    query_from = (query_from + spot % rows)[None, :]
    normed, pooled = vmem_call(
        prepare_kernel,
        (shape((span, width), jnp.bfloat16), shape((PCAP, width), jnp.bfloat16)),
    )(before, byte_states, norm_gain[None, :], segment, query_from)
    out_turns, out_assemble = along_x(w_out.T)

    key_z[1], key_z[7], query_z[3], query_z[5], normed, pooled, out_turns, cotangent = barrier(
        (key_z[1], key_z[7], query_z[3], query_z[5], normed, pooled, out_turns, cotangent)
    )
    key_z[2], key_z[6] = ring(key_z[1], "z", 1), ring(key_z[7], "z", -1)
    query_z[4] = ring(query_z[3], "z", 1)
    out_own = out_assemble(out_turns)
    cot_mine = jnp.stack([cotangent] + [ring(cotangent, "y", steps) for steps in (1, 2, 3)])

    key_z[2], key_z[6], query_z[4], out_own = barrier((key_z[2], key_z[6], query_z[4], out_own))
    query_own = jnp.concatenate([query_z[steps] for steps in range(8)], axis=0)
    query_x = [query_own] + [ring(query_own, "x", steps) for steps in (1, 2, 3)]
    key_z[3], key_z[5] = ring(key_z[2], "z", 1), ring(key_z[6], "z", -1)
    key_z[3], key_z[5], out_own, cot_mine = barrier((key_z[3], key_z[5], out_own, cot_mine))
    key_4a = ring(key_z[3][:, :columns], "z", 1)
    key_4b = ring(key_z[5][:, columns:], "z", -1)
    out_z = {0: out_own, 1: ring(out_own, "z", 1), 7: ring(out_own, "z", -1)}
    cot_other = ring(cot_mine, "c", 1)
    key_blocks = [key_z[0], key_z[1], key_z[2], key_z[3], key_4a, key_4b]
    key_blocks += [key_z[5], key_z[6], key_z[7]]

    vmem = pl.BlockSpec(memory_space=pltpu.VMEM)
    smem = pl.BlockSpec(memory_space=pltpu.SMEM)
    anywhere = pl.BlockSpec(memory_space=pl.ANY)
    flat = shape((span, columns), jnp.bfloat16)
    keys, values = vmem_call(
        project_kernel,
        (flat, flat),
        in_specs=[smem, vmem] + [anywhere] * 9,
        out_specs=(vmem, vmem),
        scratch_shapes=[
            pltpu.VMEM((width, 2 * columns), jnp.bfloat16),
            pltpu.SemaphoreType.DMA((9,)),
        ],
    )(place, normed, *key_blocks)
    out_z[1], out_z[7], keys, values = barrier((out_z[1], out_z[7], keys, values))
    out_z[2], out_z[6] = ring(out_z[1], "z", 1), ring(out_z[7], "z", -1)
    spot_shape = shape((PAT_DEV, columns), jnp.bfloat16)
    places = vmem_call(
        attend_kernel,
        (spot_shape,) * 10,
        in_specs=[vmem] * 5 + [smem] + [anywhere] * 4,
        out_specs=(vmem,) * 10,
        scratch_shapes=[
            pltpu.VMEM((width, columns), jnp.bfloat16),
            pltpu.VMEM((padded, columns), jnp.float32),
            pltpu.VMEM((columns // HDIM, padded, 2 * HDIM), jnp.bfloat16),
            pltpu.SemaphoreType.DMA((4,)),
        ],
    )(keys, values, pooled, segment_wide, segment_col, place, *query_x)
    places, out_z[2], out_z[6] = barrier((places, out_z[2], out_z[6]))
    pieces = [places[2]] + [from_behind(places[offset + 2], offset) for offset in (-2, 2, -1, 1)]
    out_z[3], out_z[5] = ring(out_z[2], "z", 1), ring(out_z[6], "z", -1)

    def gradient_part(steps, *sums):
        return vmem_call(
            functools.partial(gradient_kernel, steps),
            shape((PAT_DEV, columns), jnp.float32),
            in_specs=[smem] + [vmem] * (2 + len(steps) + len(sums)),
            out_specs=vmem,
        )(place, cot_mine, cot_other, *[out_z[step] for step in steps], *sums)

    gradient = gradient_part((0, 1, 7, 2, 6))
    out_z[3], out_z[5], gradient = barrier((out_z[3], out_z[5], gradient))
    mid = columns // 2
    out_4a = ring(out_z[3][:, :mid], "z", 1)
    out_4b = ring(out_z[5][:, mid:], "z", -1)
    out_z[4] = jnp.concatenate([out_4a, out_4b], axis=1)

    out_blocks = [out_z[steps] for steps in range(8)]

    def terms(partner):
        return vmem_call(
            functools.partial(term_kernel, partner),
            shape((4, PAT_DEV, columns), jnp.bfloat16),
            in_specs=[smem] + [vmem] * 5 + [anywhere] * 8,
            out_specs=vmem,
            scratch_shapes=[
                pltpu.VMEM((4, columns, columns), jnp.bfloat16),
                pltpu.SemaphoreType.DMA((4,)),
            ],
        )(place, *pieces, *out_blocks)

    theirs = terms(True)
    arrived = ring(theirs, "c", 1)
    mine = terms(False)
    arrived, mine, gradient, last = barrier((arrived, mine, gradient, out_blocks[3:6]))
    out_z[3], out_z[4], out_z[5] = last
    paired = [
        (mine[d].astype(jnp.float32) + arrived[d].astype(jnp.float32)).astype(jnp.bfloat16)
        for d in range(4)
    ]
    paired, later, gradient = barrier((paired, places[5:], gradient))
    mixed = paired[0].astype(jnp.float32)
    for steps in (2, 1, 3):
        mixed = mixed + ring(paired[steps], "y", steps).astype(jnp.float32)
    queries = later[2].astype(jnp.float32)
    for offset in (-2, 2, -1, 1):
        queries = queries + from_behind(later[offset + 2], offset).astype(jnp.float32)
    gradient = gradient_part((3, 4, 5), gradient)
    patch_rows = (queries + mixed).astype(jnp.bfloat16)
    return (patch_rows, gradient)


def solution(mesh):
    fine = Mesh(mesh.devices.reshape(8, 4, 4, 2), DP + GRP)
    return jax.shard_map(
        per_device,
        mesh=fine,
        in_specs=(
            P(DP, None),
            P(),
            P(DP, None),
            P(DP, GRP),
            P(DP, GRP),
            P(DP, GRP),
            P(GRP, DP),
            P(DP, GRP),
        ),
        out_specs=(P(DP, GRP), P(DP, GRP)),
        check_vma=False,
    )
```

```python
import functools

import jax
import jax.numpy as jnp
from jax import lax
from jax.experimental import pallas as pl
from jax.experimental.pallas import tpu as pltpu
from jax.sharding import Mesh, PartitionSpec as P

HDIM = 128
MOST = 16
PAT_DEV = 256
PCAP = 640
OFFSETS = (-2, -1, 0, 1, 2)
EPSILON = 1e-05
DP = ("z", "x")
GRP = ("y", "c")
VMEM_BYTES = 52 * 1024 * 1024


def ring(value, axis, steps):
    count = lax.axis_size(axis)
    return lax.ppermute(value, axis, [(i, (i + steps) % count) for i in range(count)])


def from_behind(value, steps):
    count = lax.axis_size(DP)
    leading, last = (max(0, -steps), min(count, count - steps))
    return lax.ppermute(value, DP, [(source, source + steps) for source in range(leading, last)])


def vmem_call(kernel, out_shape, **more):
    params = pltpu.CompilerParams(vmem_limit_bytes=VMEM_BYTES)
    return pl.pallas_call(kernel, out_shape=out_shape, compiler_params=params, **more)


def one_hot(rows, columns):
    return jnp.where(rows == columns, 1.0, 0.0).astype(jnp.bfloat16)


def f32_dot(a, b, contract=((1,), (0,))):
    return lax.dot_general(a, b, (contract, ((), ())), preferred_element_type=jnp.float32)


def prepare_kernel(before, states, gain, segment, query_order, normed_out, pool_out):
    width = states.shape[1]
    for source, start in ((before, 0), (states, MOST)):
        rows = source[...].astype(jnp.float32)
        mean_square = jnp.mean(rows * rows, axis=1, keepdims=True)
        normed = rows * lax.rsqrt(mean_square + EPSILON) * gain[...]
        normed_out[pl.ds(start, rows.shape[0]), :] = normed.astype(jnp.bfloat16)
    normed = normed_out[...]
    slot = lax.broadcasted_iota(jnp.int32, (PCAP, normed.shape[0]), 0)
    member = jnp.where(slot == segment[...], 1.0, 0.0)
    sizes = jnp.sum(member, axis=1, keepdims=True)
    sums = f32_dot(member.astype(jnp.bfloat16), normed)
    pooled = (sums / jnp.where(sizes > 0, sizes, 1.0)).astype(jnp.bfloat16)
    column = lax.broadcasted_iota(jnp.int32, (width, width), 0)
    pool_out[...] = f32_dot(pooled, one_hot(column, query_order[...])).astype(jnp.bfloat16)


def project_kernel(place, normed, *rest):
    blocks, keys, values, weight, sems = rest[:9], rest[9], rest[10], rest[11], rest[12]
    depth = blocks[0].shape[0]
    columns = keys.shape[1]
    copies = []
    for steps in range(8):
        row = pl.multiple_of(((place[0] + 8 - steps) & 7) * depth, 16)
        if steps == 4:
            spots = ((4, 0, columns), (5, columns, columns))
        else:
            spots = ((steps if steps < 4 else steps + 1, 0, 2 * columns),)
        for source, lane, lanes in spots:
            target = weight.at[pl.ds(row, depth), pl.ds(lane, lanes)]
            copies.append(pltpu.make_async_copy(blocks[source], target, sems.at[source]))
    for copy in copies:
        copy.start()
    for copy in copies:
        copy.wait()
    for out, start in ((keys, 0), (values, columns)):
        out[...] = f32_dot(normed[...], weight[:, start : start + columns]).astype(jnp.bfloat16)


def attend_kernel(keys, values, pooled, segment_row, segment_col, place, *rest):
    blocks, places = rest[:4], rest[4:14]
    weight, product, value_ext, sems = rest[14:]
    span, columns = keys.shape
    padded = product.shape[0]
    tall = blocks[0].shape[0]
    copies = [
        pltpu.make_async_copy(block, weight.at[pl.ds(number * tall, tall), :], sems.at[number])
        for number, block in enumerate(blocks)
    ]
    for copy in copies:
        copy.start()
    slot_col = lax.broadcasted_iota(jnp.int32, (span, PCAP), 1)
    reader = one_hot(slot_col, segment_col[...])
    heads = columns // HDIM
    for number in range(heads):
        value_ext[number, :span, :HDIM] = values[:, number * HDIM : (number + 1) * HDIM]
    value_ext[:, span:, :HDIM] = jnp.zeros((heads, padded - span, HDIM), jnp.bfloat16)
    value_ext[:, :, HDIM:] = jnp.ones((heads, padded, HDIM), jnp.bfloat16)
    product[pl.ds(span, padded - span), :] = jnp.zeros((padded - span, columns), jnp.float32)
    for copy in copies:
        copy.wait()
    queries = f32_dot(pooled[...], weight[...]).astype(jnp.bfloat16)
    product[:span, :] = f32_dot(reader, queries) * keys[...].astype(jnp.float32)
    lane = lax.broadcasted_iota(jnp.int32, (8, columns), 1)
    low_lane = lax.broadcasted_iota(jnp.int32, (8, columns), 0) * HDIM
    picker = jnp.where((lane >= low_lane) & (lane < low_lane + HDIM), 1.0, 0.0).astype(jnp.bfloat16)
    left = product[...]
    scores = jnp.zeros((8, padded), jnp.float32)
    for _ in range(3):
        part = left.astype(jnp.bfloat16)
        scores = scores + f32_dot(picker, part, ((1,), (1,)))
        left = left - part.astype(jnp.float32)
    scores = scores * HDIM ** (-0.5)
    segment = jnp.broadcast_to(segment_row[...], (8, padded))
    forward = backward = scores
    step = 1
    while step < span:
        same = pltpu.roll(segment, step, 1) == segment
        forward = jnp.maximum(forward, jnp.where(same, pltpu.roll(forward, step, 1), -1e30))
        same = pltpu.roll(segment, padded - step, 1) == segment
        backward = jnp.maximum(
            backward, jnp.where(same, pltpu.roll(backward, padded - step, 1), -1e30)
        )
        step *= 2
    weights = jnp.exp(scores - jnp.maximum(forward, backward))
    member = lax.broadcasted_iota(jnp.int32, (PCAP, padded), 0) == segment_row[...]
    gathered = []
    for number in range(heads):
        spread = jnp.where(member, weights[number : number + 1, :], 0.0).astype(jnp.bfloat16)
        total = f32_dot(spread, value_ext[number])
        divisor = total[:, HDIM:]
        gathered.append((total[:, :HDIM] / jnp.where(divisor > 0, divisor, 1.0)).astype(jnp.bfloat16))
    attended = jnp.concatenate(gathered, axis=1)
    for number in range(5):
        landing = lax.broadcasted_iota(jnp.int32, (PAT_DEV, PCAP), 0) + (
            place[4] + number * PAT_DEV
        )
        chosen = one_hot(landing, lax.broadcasted_iota(jnp.int32, (PAT_DEV, PCAP), 1))
        places[number][...] = f32_dot(chosen, attended).astype(jnp.bfloat16)
        places[5 + number][...] = f32_dot(chosen, queries).astype(jnp.bfloat16)


def pack_kernel(key, value, out_rows, packed):
    columns = key.shape[1]
    tall = packed.shape[0] - key.shape[0]
    for number in range(packed.shape[1] // HDIM):
        piece = out_rows[number * tall : (number + 1) * tall, :]
        packed[:tall, number * HDIM : (number + 1) * HDIM] = piece
    packed[tall:, :columns] = key[...]
    packed[tall:, columns:] = value[...]


def order_kernel(place, *refs):
    turns, keys, out_rows, wide = refs[:4], refs[4], refs[5], refs[6]
    rows = keys.shape[0] // 4
    tall = turns[0].shape[0] - rows
    for number, turn in enumerate(turns):
        at = (place[0] + 4 - number) & 3
        wide[pl.ds(pl.multiple_of(at * rows, 8), rows), :] = turn[tall:, :].astype(jnp.float32)
        lane = pl.multiple_of(at * HDIM, HDIM)
        for start in range(0, turn.shape[1], HDIM):
            height = start // HDIM * tall
            out_rows[height : height + tall, pl.ds(lane, HDIM)] = turn[:tall, start : start + HDIM]
    keys[...] = wide[...].astype(jnp.bfloat16)


def join_kernel(*refs):
    blocks, out, wide = refs[:-2], refs[-2], refs[-1]
    rows = blocks[0].shape[0]
    for number, block in enumerate(blocks):
        wide[number * rows : (number + 1) * rows, :] = block[...].astype(jnp.float32)
    out[...] = wide[...].astype(jnp.bfloat16)


def block_copies(blocks, steps, target, sem):
    if steps != 4:
        return [pltpu.make_async_copy(blocks[steps + (steps > 4)], target, sem)]
    half = target.shape[1] // 2
    return [
        pltpu.make_async_copy(blocks[4 + i], target.at[:, pl.ds(i * half, half)], sem) for i in (0, 1)
    ]


def term_kernel(partner, place, *refs):
    pieces, blocks, out, buffer, sems = refs[:3], refs[3:12], *refs[12:]
    z, y, c = place[0], place[2], place[3]
    parity = (z + (1 - c if partner else c)) & 1
    for pair in range(4):
        for odd in range(2):

            @pl.when(parity == odd)
            def _(pair=pair, odd=odd):
                for copy in block_copies(blocks, 2 * pair + odd, buffer.at[pair], sems.at[pair]):
                    copy.start()

    total = pieces[0][...].astype(jnp.float32)
    for piece in pieces[1:]:
        total = total + piece[...].astype(jnp.float32)
    landed = total.astype(jnp.bfloat16)
    for pair in range(4):
        pltpu.make_async_copy(buffer.at[pair], buffer.at[pair], sems.at[pair]).wait()
        group = (z + 8 - (2 * pair + parity)) & 7
        slot = ((group >> 1) + 4 - y) & 3
        out[slot] = f32_dot(landed, buffer[pair]).astype(out.dtype)


def pick_block(place, mine, other, steps):
    group = (place[0] + 8 - steps) & 7
    slot = (place[2] + 4 - (group >> 1)) & 3
    return jnp.where((group & 1) == place[3], mine[slot], other[slot])


def gradient_kernel(place, mine, other, *refs):
    blocks, out, buffer, sems = refs[:9], *refs[9:]
    for steps in range(8):
        for copy in block_copies(blocks, steps, buffer.at[steps], sems.at[steps]):
            copy.start()
    total = jnp.zeros(out.shape, jnp.float32)
    for steps in range(8):
        pltpu.make_async_copy(buffer.at[steps], buffer.at[steps], sems.at[steps]).wait()
        picked = pick_block(place, mine, other, steps)
        total = total + f32_dot(picked, buffer[steps], ((1,), (1,)))
    out[...] = total


def per_device(byte_states, norm_gain, patch_window, w_query, w_key, w_value, w_out, cotangent):
    byte_count, width = byte_states.shape
    rows, columns = w_query.shape
    span = byte_count + MOST
    padded = -(-span // HDIM) * HDIM
    my_z, my_x, my_y, my_c = (lax.axis_index(name) for name in DP + GRP)
    shape, half, full = jax.ShapeDtypeStruct, jnp.bfloat16, jnp.float32
    barrier = lax.optimization_barrier
    vmem = pl.BlockSpec(memory_space=pltpu.VMEM)
    smem = pl.BlockSpec(memory_space=pltpu.SMEM)
    anywhere = pl.BlockSpec(memory_space=pl.ANY)

    folded = w_out.shape[0] * HDIM // (2 * columns)
    packed = vmem_call(pack_kernel, shape((rows + folded, 2 * columns), half))(
        w_key, w_value, w_out
    )
    turns = [packed] + [ring(packed, "x", steps) for steps in (1, 2, 3)]
    query_z = {0: w_query, 1: ring(w_query, "z", 1), 7: ring(w_query, "z", -1)}
    turns, query_z[1], query_z[7] = barrier((turns, query_z[1], query_z[7]))
    key_own, out_own = vmem_call(
        order_kernel,
        (shape((4 * rows, 2 * columns), half), shape((columns, columns), half)),
        in_specs=[smem] + [vmem] * 4,
        out_specs=(vmem, vmem),
        scratch_shapes=[pltpu.VMEM((4 * rows, 2 * columns), full)],
    )(my_x.astype(jnp.int32).reshape(1), *turns)
    key_own, query_z[1], query_z[7], last_rows = barrier(
        (key_own, query_z[1], query_z[7], byte_states[byte_count - MOST :])
    )

    key_z = {0: key_own, 1: ring(key_own, "z", 1), 7: ring(key_own, "z", -1)}
    query_z[2], query_z[6] = ring(query_z[1], "z", 1), ring(query_z[7], "z", -1)
    before = from_behind(last_rows, 1)
    query_z[2], query_z[6], before = barrier((query_z[2], query_z[6], before))
    query_z[3], query_z[5] = ring(query_z[2], "z", 1), ring(query_z[6], "z", -1)

    key_z[1], key_z[7], before, query_z[3], query_z[5] = barrier(
        (key_z[1], key_z[7], before, query_z[3], query_z[5])
    )
    key_z[2], key_z[6] = ring(key_z[1], "z", 1), ring(key_z[7], "z", -1)
    query_z[4] = ring(query_z[3], "z", 1)
    query_own = vmem_call(
        join_kernel,
        shape((8 * rows, columns), half),
        scratch_shapes=[pltpu.VMEM((8 * rows, columns), full)],
    )(*[query_z[steps] for steps in range(8)])

    key_z[2], key_z[6], before, states, window, query_own = barrier(
        (key_z[2], key_z[6], before, byte_states, patch_window, query_own)
    )
    query_x = [query_own, ring(query_own, "x", 1), None, ring(query_own, "x", -1)]
    key_z[3], key_z[5] = ring(key_z[2], "z", 1), ring(key_z[6], "z", -1)
    patch_ids = window[:, :span]
    first_patch = window[0, MOST]
    patch_total = window[0, span] - first_patch
    relative = patch_ids - first_patch
    owned = (relative >= 0) & (relative < patch_total)
    segment = jnp.where(owned, relative, PCAP)
    segment_wide = jnp.pad(segment, ((0, 0), (0, padded - span)), constant_values=PCAP)
    segment_col = segment.reshape(span, 1)
    base = (lax.axis_index(DP) - 2) * PAT_DEV - first_patch
    place = jnp.stack([my_z, my_x, my_y, my_c, base]).astype(jnp.int32)
    spot = jnp.arange(width, dtype=jnp.int32)
    wide, part = width // 8, width // 4
    query_from = ((my_z - spot % part // rows) % 8) * wide + ((my_x - spot // part) % 4) * rows
    query_from = (query_from + spot % rows)[None, :]
    normed, pooled = vmem_call(
        prepare_kernel, (shape((span, width), half), shape((PCAP, width), half))
    )(before, states, norm_gain[None, :], segment, query_from)

    key_z[3], key_z[5], out_own, normed, pooled, segment_col, segment_wide, query_x[1::2] = barrier(
        (key_z[3], key_z[5], out_own, normed, pooled, segment_col, segment_wide, query_x[1::2])
    )
    query_x[2] = ring(query_x[1], "x", 1)
    key_4a = ring(key_z[3][:, :columns], "z", 1)
    key_4b = ring(key_z[5][:, columns:], "z", -1)
    out_z = {0: out_own, 1: ring(out_own, "z", 1), 7: ring(out_own, "z", -1)}
    key_4a, key_4b, query_x = barrier((key_4a, key_4b, query_x))
    key_blocks = [key_z[0], key_z[1], key_z[2], key_z[3], key_4a, key_4b]
    key_blocks += [key_z[5], key_z[6], key_z[7]]
    flat = shape((span, columns), half)
    keys, values = vmem_call(
        project_kernel,
        (flat, flat),
        in_specs=[smem, vmem] + [anywhere] * 9,
        out_specs=(vmem, vmem),
        scratch_shapes=[
            pltpu.VMEM((width, 2 * columns), half),
            pltpu.SemaphoreType.DMA((9,)),
        ],
    )(place, normed, *key_blocks)

    out_z[1], out_z[7], keys, values, cotangent = barrier(
        (out_z[1], out_z[7], keys, values, cotangent)
    )
    out_z[2], out_z[6] = ring(out_z[1], "z", 1), ring(out_z[7], "z", -1)
    cot_mine = jnp.stack([cotangent] + [ring(cotangent, "y", steps) for steps in (1, 2, 3)])
    spot_shape = shape((PAT_DEV, columns), half)
    places = vmem_call(
        attend_kernel,
        (spot_shape,) * 10,
        in_specs=[vmem] * 5 + [smem] + [anywhere] * 4,
        out_specs=(vmem,) * 10,
        scratch_shapes=[
            pltpu.VMEM((width, columns), half),
            pltpu.VMEM((padded, columns), full),
            pltpu.VMEM((columns // HDIM, padded, 2 * HDIM), half),
            pltpu.SemaphoreType.DMA((4,)),
        ],
    )(keys, values, pooled, segment_wide, segment_col, place, *query_x)

    def first_step(spread):
        return from_behind(spread[4], 1), from_behind(spread[0], -1)

    def second_step(spread, up, down):
        return [
            spread[2],
            from_behind(spread[3] + up, 1),
            from_behind(spread[1] + down, -1),
        ]

    places, out_z[2], out_z[6], cot_mine = barrier((places, out_z[2], out_z[6], cot_mine))
    up, down = first_step(places[:5])
    out_z[3], out_z[5] = ring(out_z[2], "z", 1), ring(out_z[6], "z", -1)
    cot_other = ring(cot_mine, "c", 1)
    pieces = second_step(places[:5], up, down)
    mid = columns // 2
    out_4a = ring(out_z[3][:, :mid], "z", 1)
    out_4b = ring(out_z[5][:, mid:], "z", -1)
    pieces, out_4a, out_4b, cot_other, asked = barrier(
        (pieces, out_4a, out_4b, cot_other, places[5:])
    )

    out_blocks = [out_z[0], out_z[1], out_z[2], out_z[3], out_4a, out_4b]
    out_blocks += [out_z[5], out_z[6], out_z[7]]

    def terms(partner):
        return vmem_call(
            functools.partial(term_kernel, partner),
            shape((4, PAT_DEV, columns), half),
            in_specs=[smem] + [vmem] * 3 + [anywhere] * 9,
            out_specs=vmem,
            scratch_shapes=[
                pltpu.VMEM((4, columns, columns), half),
                pltpu.SemaphoreType.DMA((4,)),
            ],
        )(place, *pieces, *out_blocks)

    theirs = terms(True)
    theirs, asked = barrier((theirs, asked))
    arrived = ring(theirs, "c", 1)
    up, down = first_step(asked)
    mine = terms(False)
    arrived, mine, up, down = barrier((arrived, mine, up, down))
    paired = [(mine[d].astype(full) + arrived[d].astype(full)).astype(half) for d in range(4)]
    paired, asked = barrier((paired, asked))
    mixed = paired[0].astype(full)
    for steps in (2, 1, 3):
        mixed = mixed + ring(paired[steps], "y", steps).astype(full)
    asked = second_step(asked, up, down)
    queries = asked[0].astype(full) + asked[1].astype(full) + asked[2].astype(full)
    gradient = vmem_call(
        gradient_kernel,
        shape((PAT_DEV, columns), full),
        in_specs=[smem, vmem, vmem] + [anywhere] * 9,
        out_specs=vmem,
        scratch_shapes=[
            pltpu.VMEM((8, columns, columns), half),
            pltpu.SemaphoreType.DMA((8,)),
        ],
    )(place, cot_mine, cot_other, *out_blocks)
    patch_rows = (queries + mixed).astype(half)
    return (patch_rows, gradient)


def solution(mesh):
    fine = Mesh(mesh.devices.reshape(8, 4, 4, 2), DP + GRP)
    return jax.shard_map(
        per_device,
        mesh=fine,
        in_specs=(
            P(DP, None),
            P(),
            P(DP, None),
            P(DP, GRP),
            P(DP, GRP),
            P(DP, GRP),
            P(GRP, DP),
            P(DP, GRP),
        ),
        out_specs=(P(DP, GRP), P(DP, GRP)),
        check_vma=False,
    )
```

```python
import functools

import jax
import jax.numpy as jnp
from jax import lax
from jax.experimental import pallas as pl
from jax.experimental.pallas import tpu as pltpu
from jax.sharding import Mesh, PartitionSpec as P

HDIM = 128
MOST = 16
PAT_DEV = 256
PCAP = 640
OFFSETS = (-2, -1, 0, 1, 2)
EPSILON = 1e-05
DP = ("z", "x")
GRP = ("y", "c")
VMEM_BYTES = 52 * 1024 * 1024


def ring(value, axis, steps):
    count = lax.axis_size(axis)
    return lax.ppermute(value, axis, [(i, (i + steps) % count) for i in range(count)])


def from_behind(value, steps):
    count = lax.axis_size(DP)
    leading, last = (max(0, -steps), min(count, count - steps))
    return lax.ppermute(value, DP, [(source, source + steps) for source in range(leading, last)])


def vmem_call(kernel, out_shape, **more):
    params = pltpu.CompilerParams(vmem_limit_bytes=VMEM_BYTES)
    return pl.pallas_call(kernel, out_shape=out_shape, compiler_params=params, **more)


def one_hot(rows, columns):
    return jnp.where(rows == columns, 1.0, 0.0).astype(jnp.bfloat16)


def f32_dot(a, b, contract=((1,), (0,))):
    return lax.dot_general(a, b, (contract, ((), ())), preferred_element_type=jnp.float32)


def prepare_kernel(
    place, before, states, gain, segment_row, segment_col, normed_out, pool_out, member_out, read_out, land_out
):
    for source, start in ((before, 0), (states, MOST)):
        rows = source[...].astype(jnp.float32)
        mean_square = jnp.mean(rows * rows, axis=1, keepdims=True)
        normed = rows * lax.rsqrt(mean_square + EPSILON) * gain[...]
        normed_out[pl.ds(start, rows.shape[0]), :] = normed.astype(jnp.bfloat16)
    span = normed_out.shape[0]
    member = jnp.where(
        lax.broadcasted_iota(jnp.int32, member_out.shape, 0) == segment_row[...], 1.0, 0.0
    )
    member_out[...] = member.astype(jnp.bfloat16)
    sizes = jnp.sum(member, axis=1, keepdims=True)
    sums = f32_dot(member_out[:, :span], normed_out[...])
    pool_out[...] = (sums / jnp.where(sizes > 0, sizes, 1.0)).astype(jnp.bfloat16)
    read_out[...] = one_hot(lax.broadcasted_iota(jnp.int32, read_out.shape, 1), segment_col[...])
    landing = lax.broadcasted_iota(jnp.int32, land_out.shape, 0) + place[4]
    land_out[...] = one_hot(landing, lax.broadcasted_iota(jnp.int32, land_out.shape, 1))


def attend_kernel(place, normed, pooled, member, reader, chosen, segment_row, *rest):
    blocks, places = rest[:9], rest[9:19]
    weight, product, value_ext, sems = rest[19:]
    span = normed.shape[0]
    padded, columns = product.shape
    heads = columns // HDIM
    depth = weight.shape[0] // 8
    copies = []
    for steps in range(8):
        row = pl.multiple_of(((place[0] + 8 - steps) & 7) * depth, 16)
        for part in range(3):
            lanes = pl.ds(part * columns, columns)
            for block, first, start, count in block_parts(blocks, steps, part * depth, depth):
                source = block.at[pl.ds(first, count), :]
                target = weight.at[pl.ds(row + start, count), lanes]
                copies.append(pltpu.make_async_copy(source, target, sems.at[part]))
    for copy in copies:
        copy.start()
    value_ext[:, span:, :HDIM] = jnp.zeros((heads, padded - span, HDIM), jnp.bfloat16)
    value_ext[:, :, HDIM:] = jnp.ones((heads, padded, HDIM), jnp.bfloat16)
    product[pl.ds(span, padded - span), :] = jnp.zeros((padded - span, columns), jnp.float32)
    for part in range(3):
        whole = weight.at[:, pl.ds(part * columns, columns)]
        pltpu.make_async_copy(whole, whole, sems.at[part]).wait()
    queries = f32_dot(pooled[...], weight[:, :columns]).astype(jnp.bfloat16)
    wide = 2 * HDIM
    for start in range(0, columns, wide):
        lanes = slice(start, start + wide)
        keys = f32_dot(normed[...], weight[:, columns + start : columns + start + wide])
        read = f32_dot(reader[...], queries[:, lanes])
        product[:span, lanes] = read * keys.astype(jnp.bfloat16).astype(jnp.float32)
        values = f32_dot(normed[...], weight[:, 2 * columns + start : 2 * columns + start + wide])
        values = values.astype(jnp.bfloat16)
        value_ext[start // HDIM, :span, :HDIM] = values[:, :HDIM]
        value_ext[start // HDIM + 1, :span, :HDIM] = values[:, HDIM:]
    lane = lax.broadcasted_iota(jnp.int32, (8, columns), 1)
    low_lane = lax.broadcasted_iota(jnp.int32, (8, columns), 0) * HDIM
    picker = jnp.where((lane >= low_lane) & (lane < low_lane + HDIM), 1.0, 0.0).astype(jnp.bfloat16)
    left = product[...]
    scores = jnp.zeros((8, padded), jnp.float32)
    for _ in range(3):
        part = left.astype(jnp.bfloat16)
        scores = scores + f32_dot(picker, part, ((1,), (1,)))
        left = left - part.astype(jnp.float32)
    scores = scores * HDIM ** (-0.5)
    segment = jnp.broadcast_to(segment_row[...], (8, padded))
    forward = backward = scores
    step = 1
    while step < span:
        same = pltpu.roll(segment, step, 1) == segment
        forward = jnp.maximum(forward, jnp.where(same, pltpu.roll(forward, step, 1), -1e30))
        same = pltpu.roll(segment, padded - step, 1) == segment
        backward = jnp.maximum(
            backward, jnp.where(same, pltpu.roll(backward, padded - step, 1), -1e30)
        )
        step *= 2
    weights = jnp.exp(scores - jnp.maximum(forward, backward)).astype(jnp.bfloat16)
    gathered = []
    for number in range(heads):
        spread = member[...] * weights[number : number + 1, :]
        total = f32_dot(spread, value_ext[number])
        divisor = total[:, HDIM:]
        gathered.append((total[:, :HDIM] / jnp.where(divisor > 0, divisor, 1.0)).astype(jnp.bfloat16))
    attended = jnp.concatenate(gathered, axis=1)
    for number in range(5):
        rows = slice(number * PAT_DEV, (number + 1) * PAT_DEV)
        places[number][...] = f32_dot(chosen[rows, :], attended).astype(jnp.bfloat16)
        places[5 + number][...] = f32_dot(chosen[rows, :], queries).astype(jnp.bfloat16)


def block_parts(blocks, steps, first, count):
    if steps != 4:
        return [(blocks[steps + (steps > 4)], first, 0, count)]
    half = blocks[4].shape[0]
    parts = []
    if first < half:
        parts.append((blocks[4], first, 0, min(count, half - first)))
    if first + count > half:
        start = max(first, half)
        parts.append((blocks[5], start - half, start - first, first + count - start))
    return parts


def pack_kernel(query, key, value, out_rows, packed, folded, wide):
    rows = query.shape[0]
    for number, source in enumerate((query, key, value)):
        wide[number * rows : (number + 1) * rows, :] = source[...].astype(jnp.float32)
    packed[...] = wide[...].astype(jnp.bfloat16)
    tall = folded.shape[0]
    for number in range(folded.shape[1] // HDIM):
        piece = out_rows[number * tall : (number + 1) * tall, :]
        folded[:, number * HDIM : (number + 1) * HDIM] = piece


def order_kernel(place, *refs):
    turns, folded, block, wide = refs[:4], refs[4], refs[5], refs[6]
    rows = turns[0].shape[0] // 3
    for number, turn in enumerate(turns):
        at = (place[0] + 4 - number) & 3
        values = turn[...].astype(jnp.float32)
        for part in range(3):
            row = pl.multiple_of(part * 4 * rows + at * rows, 8)
            wide[pl.ds(row, rows), :] = values[part * rows : (part + 1) * rows, :]
    block[: 12 * rows, :] = wide[...].astype(jnp.bfloat16)
    block[12 * rows :, :] = folded[...]


def join_kernel(first, *refs):
    out = refs[-1]
    tall = out.shape[0] // (len(refs) - 1)
    for number, block in enumerate(refs[:-1]):
        start = min(first, block.shape[0] - tall)
        out[number * tall : (number + 1) * tall, :] = block[start : start + tall, :]


def unfold_kernel(place, *refs):
    sources, out, sems = refs[:16], refs[16], refs[17]
    tall = sources[0].shape[0]
    for number, sets in enumerate(((0,), (1, 7), (2, 6), (3, 5, 4))):
        for turn in range(4):
            source = sources[4 * number + turn]
            lane = pl.multiple_of(((place[1] + 4 - turn) & 3) * HDIM, HDIM)
            for order, steps in enumerate(sets):
                group = (place[0] + 8 - steps) & 7
                for piece in range(4):
                    pltpu.make_async_copy(
                        source.at[pl.ds(order * tall, tall), pl.ds(piece * HDIM, HDIM)],
                        out.at[group, pl.ds(piece * tall, tall), pl.ds(lane, HDIM)],
                        sems.at[0],
                    ).start()
    pltpu.make_async_copy(out, out, sems.at[0]).wait()


def term_kernel(partner, place, *refs):
    pieces, weight, out, buffer, sems = refs[:3], *refs[3:]
    core = 1 - place[3] if partner else place[3]
    copies = [
        pltpu.make_async_copy(weight.at[2 * ((place[2] + i) & 3) + core], buffer.at[i], sems.at[i])
        for i in range(4)
    ]
    for copy in copies:
        copy.start()
    total = pieces[0][...].astype(jnp.float32)
    for piece in pieces[1:]:
        total = total + piece[...].astype(jnp.float32)
    landed = total.astype(jnp.bfloat16)
    for i in range(4):
        copies[i].wait()
        out[i] = f32_dot(landed, buffer[i]).astype(out.dtype)


def gradient_kernel(place, mine, other, weight, out, buffer, sems):
    copies = []
    for i in range(8):
        core = place[3] if i < 4 else 1 - place[3]
        group = 2 * ((place[2] + 4 - i % 4) & 3) + core
        copies.append(pltpu.make_async_copy(weight.at[group], buffer.at[i], sems.at[i]))
    for copy in copies:
        copy.start()
    total = jnp.zeros(out.shape, jnp.float32)
    for i in range(8):
        copies[i].wait()
        picked = mine[i] if i < 4 else other[i - 4]
        total = total + f32_dot(picked, buffer[i], ((1,), (1,)))
    out[...] = total


def per_device(byte_states, norm_gain, patch_window, w_query, w_key, w_value, w_out, cotangent):
    byte_count, width = byte_states.shape
    rows, columns = w_query.shape
    span = byte_count + MOST
    padded = -(-span // HDIM) * HDIM
    my_z, my_x, my_y, my_c = (lax.axis_index(name) for name in DP + GRP)
    shape, half, full = jax.ShapeDtypeStruct, jnp.bfloat16, jnp.float32
    barrier = lax.optimization_barrier
    vmem = pl.BlockSpec(memory_space=pltpu.VMEM)
    smem = pl.BlockSpec(memory_space=pltpu.SMEM)
    anywhere = pl.BlockSpec(memory_space=pl.ANY)

    tall = w_out.shape[0] * HDIM // columns
    packed, folded = vmem_call(
        pack_kernel,
        (shape((3 * rows, columns), half), shape((tall, columns), half)),
        scratch_shapes=[pltpu.VMEM((3 * rows, columns), full)],
    )(w_query, w_key, w_value, w_out)
    turns = [packed] + [ring(packed, "x", steps) for steps in (1, 2, 3)]
    before = from_behind(byte_states[byte_count - MOST :], 1)
    turns, before = barrier((turns, before))
    deep = 12 * rows
    block = vmem_call(
        order_kernel,
        shape((deep + tall, columns), half),
        in_specs=[smem] + [vmem] * 5,
        out_specs=vmem,
        scratch_shapes=[pltpu.VMEM((deep, columns), full)],
    )(my_x.astype(jnp.int32).reshape(1), *turns, folded)
    block, folded, before, window, states = barrier(
        (block, folded, before, patch_window, byte_states)
    )

    def along_x(piece):
        return [piece] + [ring(piece, "x", steps) for steps in (1, 2, 3)]

    def join(*blocks):
        return vmem_call(functools.partial(join_kernel, deep), shape((len(blocks) * tall, columns), half))(
            *blocks
        )

    ring_z = {0: block, 1: ring(block, "z", 1), 7: ring(block, "z", -1)}
    out_x = [along_x(folded)]
    patch_ids = window[:, :span]
    first_patch = window[0, MOST]
    patch_total = window[0, span] - first_patch
    relative = patch_ids - first_patch
    owned = (relative >= 0) & (relative < patch_total)
    segment = jnp.where(owned, relative, PCAP)
    segment_row = jnp.pad(segment, ((0, 0), (0, padded - span)), constant_values=PCAP)
    segment_col = segment.reshape(span, 1)
    base = (lax.axis_index(DP) - 2) * PAT_DEV - first_patch
    place = jnp.stack([my_z, my_x, my_y, my_c, base]).astype(jnp.int32)
    ring_z[1], ring_z[7], out_x, place, segment_row, segment_col = barrier(
        (ring_z[1], ring_z[7], out_x, place, segment_row, segment_col)
    )
    ring_z[2], ring_z[6] = ring(ring_z[1], "z", 1), ring(ring_z[7], "z", -1)
    out_x.append(along_x(join(ring_z[1], ring_z[7])))
    normed, pooled, member, reader, chosen = vmem_call(
        prepare_kernel,
        (
            shape((span, width), half),
            shape((PCAP, width), half),
            shape((PCAP, padded), half),
            shape((span, PCAP), half),
            shape((5 * PAT_DEV, PCAP), half),
        ),
        in_specs=[smem] + [vmem] * 5,
        out_specs=(vmem,) * 5,
    )(place, before, states, norm_gain[None, :], segment_row, segment_col)
    ring_z[2], ring_z[6], out_x, normed, pooled, member, reader, chosen = barrier(
        (ring_z[2], ring_z[6], out_x, normed, pooled, member, reader, chosen)
    )
    ring_z[3], ring_z[5] = ring(ring_z[2], "z", 1), ring(ring_z[6], "z", -1)
    out_x.append(along_x(join(ring_z[2], ring_z[6])))
    ring_z[3], ring_z[5], out_x = barrier((ring_z[3], ring_z[5], out_x))
    mid = (deep + tall) // 2
    last_a, last_b = ring(ring_z[3][:mid], "z", 1), ring(ring_z[5][mid:], "z", -1)
    cot_y = [cotangent, ring(cotangent, "y", 1), None, ring(cotangent, "y", -1)]
    last_a, last_b, cot_y[1::2], ring_z[3], ring_z[5] = barrier(
        (last_a, last_b, cot_y[1::2], ring_z[3], ring_z[5])
    )
    blocks = [ring_z[0], ring_z[1], ring_z[2], ring_z[3], last_a, last_b]
    blocks += [ring_z[5], ring_z[6], ring_z[7]]
    rest = join(ring_z[3], ring_z[5], last_b)
    rest_x = [rest, ring(rest, "x", 1), None, ring(rest, "x", -1)]
    cot_y[2] = ring(cot_y[1], "y", 1)

    spot_shape = shape((PAT_DEV, columns), half)
    places = vmem_call(
        attend_kernel,
        (spot_shape,) * 10,
        in_specs=[smem] + [vmem] * 6 + [anywhere] * 9,
        out_specs=(vmem,) * 10,
        scratch_shapes=[
            pltpu.VMEM((width, 3 * columns), half),
            pltpu.VMEM((padded, columns), full),
            pltpu.VMEM((columns // HDIM, padded, 2 * HDIM), half),
            pltpu.SemaphoreType.DMA((3,)),
        ],
    )(place, normed, pooled, member, reader, chosen, segment_row, *blocks)
    places, cot_y, rest_x[1::2] = barrier((places, cot_y, rest_x[1::2]))

    def first_step(spread):
        return from_behind(spread[4], 1), from_behind(spread[0], -1)

    def second_step(spread, up, down):
        return [
            spread[2],
            from_behind(spread[3] + up, 1),
            from_behind(spread[1] + down, -1),
        ]

    up, down = first_step(places[:5])
    rest_x[2] = ring(rest_x[1], "x", 1)
    out_x.append(rest_x)
    cot_mine = jnp.stack(cot_y)
    cot_other = ring(cot_mine, "c", 1)
    weight = vmem_call(
        unfold_kernel,
        shape((8, columns, columns), half),
        in_specs=[smem] + [anywhere] * 16,
        out_specs=anywhere,
        scratch_shapes=[pltpu.SemaphoreType.DMA((1,))],
    )(place, *[piece for pieces in out_x for piece in pieces])
    pieces = second_step(places[:5], up, down)
    gradient = vmem_call(
        gradient_kernel,
        shape((PAT_DEV, columns), full),
        in_specs=[smem, vmem, vmem, anywhere],
        out_specs=vmem,
        scratch_shapes=[
            pltpu.VMEM((8, columns, columns), half),
            pltpu.SemaphoreType.DMA((8,)),
        ],
    )(place, cot_mine, cot_other, weight)
    pieces, weight, asked, gradient = barrier((pieces, weight, places[5:], gradient))

    def terms(partner):
        return vmem_call(
            functools.partial(term_kernel, partner),
            shape((4, PAT_DEV, columns), half),
            in_specs=[smem] + [vmem] * 3 + [anywhere],
            out_specs=vmem,
            scratch_shapes=[
                pltpu.VMEM((4, columns, columns), half),
                pltpu.SemaphoreType.DMA((4,)),
            ],
        )(place, *pieces, weight)

    theirs = terms(True)
    theirs, asked = barrier((theirs, asked))
    arrived = ring(theirs, "c", 1)
    up, down = first_step(asked)
    mine = terms(False)
    arrived, mine = barrier((arrived, mine))
    paired = [(mine[d].astype(full) + arrived[d].astype(full)).astype(half) for d in range(4)]
    paired, asked = barrier((paired, asked))
    mixed = paired[0].astype(full)
    for steps in (2, 1, 3):
        mixed = mixed + ring(paired[steps], "y", steps).astype(full)
    asked = second_step(asked, up, down)
    queries = asked[0].astype(full) + asked[1].astype(full) + asked[2].astype(full)
    patch_rows = (queries + mixed).astype(half)
    return (patch_rows, gradient)


def solution(mesh):
    fine = Mesh(mesh.devices.reshape(8, 4, 4, 2), DP + GRP)
    return jax.shard_map(
        per_device,
        mesh=fine,
        in_specs=(
            P(DP, None),
            P(),
            P(DP, None),
            P(DP, GRP),
            P(DP, GRP),
            P(DP, GRP),
            P(GRP, DP),
            P(DP, GRP),
        ),
        out_specs=(P(DP, GRP), P(DP, GRP)),
        check_vma=False,
    )
```

```python
import functools

import jax
import jax.numpy as jnp
from jax import lax
from jax.experimental import pallas as pl
from jax.experimental.pallas import tpu as pltpu
from jax.sharding import Mesh, PartitionSpec as P

HDIM = 128
MOST = 16
PAT_DEV = 256
PCAP = 640
OFFSETS = (-2, -1, 0, 1, 2)
EPSILON = 1e-05
DP = ("z", "x")
GRP = ("y", "c")
VMEM_BYTES = 52 * 1024 * 1024


def ring(value, axis, steps):
    count = lax.axis_size(axis)
    return lax.ppermute(value, axis, [(i, (i + steps) % count) for i in range(count)])


def from_behind(value, steps):
    count = lax.axis_size(DP)
    leading, last = (max(0, -steps), min(count, count - steps))
    return lax.ppermute(value, DP, [(source, source + steps) for source in range(leading, last)])


def vmem_call(kernel, out_shape, **more):
    params = pltpu.CompilerParams(vmem_limit_bytes=VMEM_BYTES)
    return pl.pallas_call(kernel, out_shape=out_shape, compiler_params=params, **more)


def one_hot(rows, columns):
    return jnp.where(rows == columns, 1.0, 0.0).astype(jnp.bfloat16)


def f32_dot(a, b, contract=((1,), (0,))):
    return lax.dot_general(a, b, (contract, ((), ())), preferred_element_type=jnp.float32)


def prepare_kernel(
    place, before, states, gain, segment_row, segment_col, normed_out, pool_out, member_out, read_out, land_out
):
    for source, start in ((before, 0), (states, MOST)):
        rows = source[...].astype(jnp.float32)
        mean_square = jnp.mean(rows * rows, axis=1, keepdims=True)
        normed = rows * lax.rsqrt(mean_square + EPSILON) * gain[...]
        normed_out[pl.ds(start, rows.shape[0]), :] = normed.astype(jnp.bfloat16)
    span = normed_out.shape[0]
    member = jnp.where(
        lax.broadcasted_iota(jnp.int32, member_out.shape, 0) == segment_row[...], 1.0, 0.0
    )
    member_out[...] = member.astype(jnp.bfloat16)
    sizes = jnp.sum(member, axis=1, keepdims=True)
    sums = f32_dot(member_out[:, :span], normed_out[...])
    pool_out[...] = (sums / jnp.where(sizes > 0, sizes, 1.0)).astype(jnp.bfloat16)
    read_out[...] = one_hot(lax.broadcasted_iota(jnp.int32, read_out.shape, 1), segment_col[...])
    landing = lax.broadcasted_iota(jnp.int32, land_out.shape, 0) + place[4]
    land_out[...] = one_hot(landing, lax.broadcasted_iota(jnp.int32, land_out.shape, 1))


def attend_kernel(place, normed, pooled, member, reader, chosen, segment_row, *rest):
    blocks, places = rest[:9], rest[9:19]
    weight, product, value_ext, sems = rest[19:]
    span = normed.shape[0]
    padded, columns = product.shape
    heads = columns // HDIM
    depth = weight.shape[0] // 8
    copies = []
    for steps in range(8):
        row = pl.multiple_of(((place[0] + 8 - steps) & 7) * depth, 16)
        for part in range(3):
            lanes = pl.ds(part * columns, columns)
            for block, first, start, count in block_parts(blocks, steps, part * depth, depth):
                source = block.at[pl.ds(first, count), :]
                target = weight.at[pl.ds(row + start, count), lanes]
                copies.append(pltpu.make_async_copy(source, target, sems.at[part]))
    for copy in copies:
        copy.start()
    value_ext[:, span:, :HDIM] = jnp.zeros((heads, padded - span, HDIM), jnp.bfloat16)
    value_ext[:, :, HDIM:] = jnp.ones((heads, padded, HDIM), jnp.bfloat16)
    product[pl.ds(span, padded - span), :] = jnp.zeros((padded - span, columns), jnp.float32)
    for part in range(3):
        whole = weight.at[:, pl.ds(part * columns, columns)]
        pltpu.make_async_copy(whole, whole, sems.at[part]).wait()
    queries = f32_dot(pooled[...], weight[:, :columns]).astype(jnp.bfloat16)
    wide = 2 * HDIM
    for start in range(0, columns, wide):
        lanes = slice(start, start + wide)
        keys = f32_dot(normed[...], weight[:, columns + start : columns + start + wide])
        read = f32_dot(reader[...], queries[:, lanes])
        product[:span, lanes] = read * keys.astype(jnp.bfloat16).astype(jnp.float32)
        values = f32_dot(normed[...], weight[:, 2 * columns + start : 2 * columns + start + wide])
        values = values.astype(jnp.bfloat16)
        value_ext[start // HDIM, :span, :HDIM] = values[:, :HDIM]
        value_ext[start // HDIM + 1, :span, :HDIM] = values[:, HDIM:]
    lane = lax.broadcasted_iota(jnp.int32, (8, columns), 1)
    low_lane = lax.broadcasted_iota(jnp.int32, (8, columns), 0) * HDIM
    picker = jnp.where((lane >= low_lane) & (lane < low_lane + HDIM), 1.0, 0.0).astype(jnp.bfloat16)
    left = product[...]
    scores = jnp.zeros((8, padded), jnp.float32)
    for _ in range(3):
        part = left.astype(jnp.bfloat16)
        scores = scores + f32_dot(picker, part, ((1,), (1,)))
        left = left - part.astype(jnp.float32)
    scores = scores * HDIM ** (-0.5)
    segment = jnp.broadcast_to(segment_row[...], (8, padded))
    forward = backward = scores
    step = 1
    while step < span:
        same = pltpu.roll(segment, step, 1) == segment
        forward = jnp.maximum(forward, jnp.where(same, pltpu.roll(forward, step, 1), -1e30))
        same = pltpu.roll(segment, padded - step, 1) == segment
        backward = jnp.maximum(
            backward, jnp.where(same, pltpu.roll(backward, padded - step, 1), -1e30)
        )
        step *= 2
    weights = jnp.exp(scores - jnp.maximum(forward, backward)).astype(jnp.bfloat16)
    gathered = []
    for number in range(heads):
        spread = member[...] * weights[number : number + 1, :]
        total = f32_dot(spread, value_ext[number])
        divisor = total[:, HDIM:]
        gathered.append((total[:, :HDIM] / jnp.where(divisor > 0, divisor, 1.0)).astype(jnp.bfloat16))
    attended = jnp.concatenate(gathered, axis=1)
    for number in range(5):
        rows = slice(number * PAT_DEV, (number + 1) * PAT_DEV)
        places[number][...] = f32_dot(chosen[rows, :], attended).astype(jnp.bfloat16)
        places[5 + number][...] = f32_dot(chosen[rows, :], queries).astype(jnp.bfloat16)


def block_parts(blocks, steps, first, count):
    if steps != 4:
        return [(blocks[steps + (steps > 4)], first, 0, count)]
    half = blocks[4].shape[0]
    parts = []
    if first < half:
        parts.append((blocks[4], first, 0, min(count, half - first)))
    if first + count > half:
        start = max(first, half)
        parts.append((blocks[5], start - half, start - first, first + count - start))
    return parts


def pack_kernel(query, key, value, out_rows, packed, folded, wide):
    rows = query.shape[0]
    for number, source in enumerate((query, key, value)):
        wide[number * rows : (number + 1) * rows, :] = source[...].astype(jnp.float32)
    packed[...] = wide[...].astype(jnp.bfloat16)
    tall = folded.shape[0]
    for number in range(folded.shape[1] // HDIM):
        piece = out_rows[number * tall : (number + 1) * tall, :]
        folded[:, number * HDIM : (number + 1) * HDIM] = piece


def order_kernel(place, *refs):
    turns, folded, block, wide = refs[:4], refs[4], refs[5], refs[6]
    rows = turns[0].shape[0] // 3
    for number, turn in enumerate(turns):
        at = (place[0] + 4 - number) & 3
        values = turn[...].astype(jnp.float32)
        for part in range(3):
            row = pl.multiple_of(part * 4 * rows + at * rows, 8)
            wide[pl.ds(row, rows), :] = values[part * rows : (part + 1) * rows, :]
    block[: 12 * rows, :] = wide[...].astype(jnp.bfloat16)
    block[12 * rows :, :] = folded[...]


def join_kernel(first, *refs):
    out = refs[-1]
    tall = out.shape[0] // (len(refs) - 1)
    for number, block in enumerate(refs[:-1]):
        start = min(first, block.shape[0] - tall)
        out[number * tall : (number + 1) * tall, :] = block[start : start + tall, :]


def unfold_kernel(place, *refs):
    sources, out = refs[:12], refs[12]
    tall = sources[0].shape[0] // 3
    for number, sets in enumerate(((0, 1, 7), (2, 6), (3, 5, 4))):
        for turn in range(4):
            source = sources[4 * number + turn]
            lanes = pl.ds(pl.multiple_of(((place[1] + 4 - turn) & 3) * HDIM, HDIM), HDIM)
            for order, steps in enumerate(sets):
                group = (place[0] + 8 - steps) & 7
                for piece in range(4):
                    out[group, piece * tall : (piece + 1) * tall, lanes] = source[
                        order * tall : (order + 1) * tall, piece * HDIM : (piece + 1) * HDIM
                    ]


def term_kernel(partner, place, *refs):
    pieces, weight, out, buffer, sems = refs[:3], *refs[3:]
    core = 1 - place[3] if partner else place[3]
    copies = [
        pltpu.make_async_copy(weight.at[2 * ((place[2] + i) & 3) + core], buffer.at[i], sems.at[i])
        for i in range(4)
    ]
    for copy in copies:
        copy.start()
    total = pieces[0][...].astype(jnp.float32)
    for piece in pieces[1:]:
        total = total + piece[...].astype(jnp.float32)
    landed = total.astype(jnp.bfloat16)
    for i in range(4):
        copies[i].wait()
        out[i] = f32_dot(landed, buffer[i]).astype(out.dtype)


def gradient_kernel(place, mine, other, weight, out, buffer, sems):
    copies = []
    for i in range(8):
        core = place[3] if i < 4 else 1 - place[3]
        group = 2 * ((place[2] + 4 - i % 4) & 3) + core
        copies.append(pltpu.make_async_copy(weight.at[group], buffer.at[i], sems.at[i]))
    for copy in copies:
        copy.start()
    total = jnp.zeros(out.shape, jnp.float32)
    for i in range(8):
        copies[i].wait()
        picked = mine[i] if i < 4 else other[i - 4]
        total = total + f32_dot(picked, buffer[i], ((1,), (1,)))
    out[...] = total


def per_device(byte_states, norm_gain, patch_window, w_query, w_key, w_value, w_out, cotangent):
    byte_count, width = byte_states.shape
    rows, columns = w_query.shape
    span = byte_count + MOST
    padded = -(-span // HDIM) * HDIM
    my_z, my_x, my_y, my_c = (lax.axis_index(name) for name in DP + GRP)
    shape, half, full = jax.ShapeDtypeStruct, jnp.bfloat16, jnp.float32
    barrier = lax.optimization_barrier
    vmem = pl.BlockSpec(memory_space=pltpu.VMEM)
    smem = pl.BlockSpec(memory_space=pltpu.SMEM)
    anywhere = pl.BlockSpec(memory_space=pl.ANY)

    tall = w_out.shape[0] * HDIM // columns
    packed, folded = vmem_call(
        pack_kernel,
        (shape((3 * rows, columns), half), shape((tall, columns), half)),
        scratch_shapes=[pltpu.VMEM((3 * rows, columns), full)],
    )(w_query, w_key, w_value, w_out)
    turns = [packed] + [ring(packed, "x", steps) for steps in (1, 2, 3)]
    turns, folded = barrier((turns, folded))
    deep = 12 * rows
    block = vmem_call(
        order_kernel,
        shape((deep + tall, columns), half),
        in_specs=[smem] + [vmem] * 5,
        out_specs=vmem,
        scratch_shapes=[pltpu.VMEM((deep, columns), full)],
    )(my_x.astype(jnp.int32).reshape(1), *turns, folded)
    block, last_rows, window = barrier((block, byte_states[byte_count - MOST :], patch_window))

    def join(*blocks):
        return vmem_call(functools.partial(join_kernel, deep), shape((len(blocks) * tall, columns), half))(
            *blocks
        )

    def along_x(piece):
        return [piece, ring(piece, "x", 1), None, ring(piece, "x", -1)]

    ring_z = {0: block, 1: ring(block, "z", 1), 7: ring(block, "z", -1)}
    before = from_behind(last_rows, 1)
    patch_ids = window[:, :span]
    first_patch = window[0, MOST]
    patch_total = window[0, span] - first_patch
    relative = patch_ids - first_patch
    owned = (relative >= 0) & (relative < patch_total)
    segment = jnp.where(owned, relative, PCAP)
    segment_row = jnp.pad(segment, ((0, 0), (0, padded - span)), constant_values=PCAP)
    segment_col = segment.reshape(span, 1)
    base = (lax.axis_index(DP) - 2) * PAT_DEV - first_patch
    place = jnp.stack([my_z, my_x, my_y, my_c, base]).astype(jnp.int32)
    gain = norm_gain[None, :]
    ring_z[1], ring_z[7], before, place, segment_row = barrier(
        (ring_z[1], ring_z[7], before, place, segment_row)
    )
    ring_z[2], ring_z[6] = ring(ring_z[1], "z", 1), ring(ring_z[7], "z", -1)
    out_x = [along_x(join(block, ring_z[1], ring_z[7]))]
    ring_z[2], ring_z[6], out_x[0][1::2], segment_col, gain, before, states = barrier(
        (ring_z[2], ring_z[6], out_x[0][1::2], segment_col, gain, before, byte_states)
    )
    ring_z[3], ring_z[5] = ring(ring_z[2], "z", 1), ring(ring_z[6], "z", -1)
    out_x[0][2] = ring(out_x[0][1], "x", 1)
    out_x.append(along_x(join(ring_z[2], ring_z[6])))
    normed, pooled, member, reader, chosen = vmem_call(
        prepare_kernel,
        (
            shape((span, width), half),
            shape((PCAP, width), half),
            shape((PCAP, padded), half),
            shape((span, PCAP), half),
            shape((5 * PAT_DEV, PCAP), half),
        ),
        in_specs=[smem] + [vmem] * 5,
        out_specs=(vmem,) * 5,
    )(place, before, states, gain, segment_row, segment_col)
    ring_z[3], ring_z[5], out_x[0][2], out_x[1][1::2], normed, pooled, member, reader, chosen = barrier(
        (ring_z[3], ring_z[5], out_x[0][2], out_x[1][1::2], normed, pooled, member, reader, chosen)
    )
    mid = (deep + tall) // 2
    last_a, last_b = ring(ring_z[3][:mid], "z", 1), ring(ring_z[5][mid:], "z", -1)
    out_x[1][2] = ring(out_x[1][1], "x", 1)
    cot_y = [cotangent, ring(cotangent, "y", 1), None, ring(cotangent, "y", -1)]
    last_a, last_b, cot_y[1::2], ring_z[3], ring_z[5], out_x[1][2] = barrier(
        (last_a, last_b, cot_y[1::2], ring_z[3], ring_z[5], out_x[1][2])
    )
    blocks = [ring_z[0], ring_z[1], ring_z[2], ring_z[3], last_a, last_b]
    blocks += [ring_z[5], ring_z[6], ring_z[7]]
    out_x.append(along_x(join(ring_z[3], ring_z[5], last_b)))
    cot_y[2] = ring(cot_y[1], "y", 1)

    spot_shape = shape((PAT_DEV, columns), half)
    places = vmem_call(
        attend_kernel,
        (spot_shape,) * 10,
        in_specs=[smem] + [vmem] * 6 + [anywhere] * 9,
        out_specs=(vmem,) * 10,
        scratch_shapes=[
            pltpu.VMEM((width, 3 * columns), half),
            pltpu.VMEM((padded, columns), full),
            pltpu.VMEM((columns // HDIM, padded, 2 * HDIM), half),
            pltpu.SemaphoreType.DMA((3,)),
        ],
    )(place, normed, pooled, member, reader, chosen, segment_row, *blocks)
    places, cot_y, out_x[2][1::2] = barrier((places, cot_y, out_x[2][1::2]))

    def first_step(spread):
        return from_behind(spread[4], 1), from_behind(spread[0], -1)

    def second_step(spread, up, down):
        return [
            spread[2],
            from_behind(spread[3] + up, 1),
            from_behind(spread[1] + down, -1),
        ]

    up, down = first_step(places[:5])
    asked_up, asked_down = first_step(places[5:])
    out_x[2][2] = ring(out_x[2][1], "x", 1)
    weight = vmem_call(
        unfold_kernel,
        shape((8, columns, columns), half),
        in_specs=[smem] + [vmem] * 12,
        out_specs=vmem,
    )(place, *[piece for pieces in out_x for piece in pieces])
    pieces = second_step(places[:5], up, down)
    asked = second_step(places[5:], asked_up, asked_down)
    cot_mine = jnp.stack(cot_y)
    pieces, weight, cot_mine, asked = barrier((pieces, weight, cot_mine, asked))

    def terms(partner):
        return vmem_call(
            functools.partial(term_kernel, partner),
            shape((4, PAT_DEV, columns), half),
            in_specs=[smem] + [vmem] * 3 + [anywhere],
            out_specs=vmem,
            scratch_shapes=[
                pltpu.VMEM((4, columns, columns), half),
                pltpu.SemaphoreType.DMA((4,)),
            ],
        )(place, *pieces, weight)

    theirs = terms(True)
    arrived = ring(theirs, "c", 1)
    mine = terms(False)
    arrived, mine = barrier((arrived, mine))
    paired = [(mine[d].astype(full) + arrived[d].astype(full)).astype(half) for d in range(4)]
    paired, cot_mine = barrier((paired, cot_mine))
    mixed = [paired[0]] + [ring(paired[steps], "y", steps) for steps in (2, 1, 3)]
    gradient = vmem_call(
        gradient_kernel,
        shape((PAT_DEV, columns), full),
        in_specs=[smem, vmem, vmem, anywhere],
        out_specs=vmem,
        scratch_shapes=[
            pltpu.VMEM((8, columns, columns), half),
            pltpu.SemaphoreType.DMA((8,)),
        ],
    )(place, cot_mine, ring(cot_mine, "c", 1), weight)
    mixed, gradient = barrier((mixed, gradient))
    queries = asked[0].astype(full) + asked[1].astype(full) + asked[2].astype(full)
    mixed = (mixed[0].astype(full) + mixed[1].astype(full)) + (
        mixed[2].astype(full) + mixed[3].astype(full)
    )
    patch_rows = (queries + mixed).astype(half)
    return (patch_rows, gradient)


def solution(mesh):
    fine = Mesh(mesh.devices.reshape(8, 4, 4, 2), DP + GRP)
    return jax.shard_map(
        per_device,
        mesh=fine,
        in_specs=(
            P(DP, None),
            P(),
            P(DP, None),
            P(DP, GRP),
            P(DP, GRP),
            P(DP, GRP),
            P(GRP, DP),
            P(DP, GRP),
        ),
        out_specs=(P(DP, GRP), P(DP, GRP)),
        check_vma=False,
    )
```

```python
import functools

import jax
import jax.numpy as jnp
from jax import lax
from jax.experimental import pallas as pl
from jax.experimental.pallas import tpu as pltpu
from jax.sharding import Mesh, PartitionSpec as P

HDIM = 128
MOST = 16
PAT_DEV = 256
PCAP = 640
OFFSETS = (-2, -1, 0, 1, 2)
EPSILON = 1e-05
DP = ("z", "x")
GRP = ("y", "c")
VMEM_BYTES = 52 * 1024 * 1024


def ring(value, axis, steps):
    count = lax.axis_size(axis)
    return lax.ppermute(value, axis, [(i, (i + steps) % count) for i in range(count)])


def from_behind(value, steps):
    count = lax.axis_size(DP)
    leading, last = (max(0, -steps), min(count, count - steps))
    return lax.ppermute(value, DP, [(source, source + steps) for source in range(leading, last)])


def vmem_call(kernel, out_shape, **more):
    params = pltpu.CompilerParams(vmem_limit_bytes=VMEM_BYTES)
    return pl.pallas_call(kernel, out_shape=out_shape, compiler_params=params, **more)


def one_hot(rows, columns):
    return jnp.where(rows == columns, 1.0, 0.0).astype(jnp.bfloat16)


def f32_dot(a, b, contract=((1,), (0,))):
    return lax.dot_general(a, b, (contract, ((), ())), preferred_element_type=jnp.float32)


def mask_kernel(place, segment_row, segment_col, member_out, read_out, land_out, size_out):
    member = jnp.where(
        lax.broadcasted_iota(jnp.int32, member_out.shape, 0) == segment_row[...], 1.0, 0.0
    )
    member_out[...] = member.astype(jnp.bfloat16)
    sizes = jnp.sum(member, axis=1, keepdims=True)
    size_out[...] = jnp.where(sizes > 0, sizes, 1.0)
    read_out[...] = one_hot(lax.broadcasted_iota(jnp.int32, read_out.shape, 1), segment_col[...])
    landing = lax.broadcasted_iota(jnp.int32, land_out.shape, 0) + place[4]
    land_out[...] = one_hot(landing, lax.broadcasted_iota(jnp.int32, land_out.shape, 1))


def prepare_kernel(before, states, gain, member, sizes, normed_out, pool_out):
    for source, start in ((before, 0), (states, MOST)):
        rows = source[...].astype(jnp.float32)
        mean_square = jnp.mean(rows * rows, axis=1, keepdims=True)
        normed = rows * lax.rsqrt(mean_square + EPSILON) * gain[...]
        normed_out[pl.ds(start, rows.shape[0]), :] = normed.astype(jnp.bfloat16)
    sums = f32_dot(member[:, : normed_out.shape[0]], normed_out[...])
    pool_out[...] = (sums / sizes[...]).astype(jnp.bfloat16)


def place_kernel(chosen, source, *places):
    for number, place in enumerate(places):
        rows = slice(number * PAT_DEV, (number + 1) * PAT_DEV)
        place[...] = f32_dot(chosen[rows, :], source[...]).astype(jnp.bfloat16)


def attend_kernel(place, normed, pooled, member, reader, chosen, segment_row, *rest):
    blocks, places, asked = rest[:9], rest[9:14], rest[14]
    weight, product, value_ext, sems = rest[15:]
    span = normed.shape[0]
    padded, columns = product.shape
    heads = columns // HDIM
    depth = weight.shape[0] // 8
    copies = []
    for steps in range(8):
        row = pl.multiple_of(((place[0] + 8 - steps) & 7) * depth, 16)
        for part in range(3):
            lanes = pl.ds(part * columns, columns)
            for block, first, start, count in block_parts(blocks, steps, part * depth, depth):
                source = block.at[pl.ds(first, count), :]
                target = weight.at[pl.ds(row + start, count), lanes]
                copies.append(pltpu.make_async_copy(source, target, sems.at[part]))
    for copy in copies:
        copy.start()
    value_ext[:, span:, :HDIM] = jnp.zeros((heads, padded - span, HDIM), jnp.bfloat16)
    value_ext[:, :, HDIM:] = jnp.ones((heads, padded, HDIM), jnp.bfloat16)
    product[pl.ds(span, padded - span), :] = jnp.zeros((padded - span, columns), jnp.float32)

    def arrive(part):
        whole = weight.at[:, pl.ds(part * columns, columns)]
        pltpu.make_async_copy(whole, whole, sems.at[part]).wait()

    arrive(0)
    queries = f32_dot(pooled[...], weight[:, :columns]).astype(jnp.bfloat16)
    asked[...] = queries
    arrive(1)
    wide = 2 * HDIM
    for start in range(0, columns, wide):
        lanes = slice(start, start + wide)
        keys = f32_dot(normed[...], weight[:, columns + start : columns + start + wide])
        read = f32_dot(reader[...], queries[:, lanes])
        product[:span, lanes] = read * keys.astype(jnp.bfloat16).astype(jnp.float32)
    arrive(2)
    for start in range(0, columns, wide):
        values = f32_dot(normed[...], weight[:, 2 * columns + start : 2 * columns + start + wide])
        values = values.astype(jnp.bfloat16)
        value_ext[start // HDIM, :span, :HDIM] = values[:, :HDIM]
        value_ext[start // HDIM + 1, :span, :HDIM] = values[:, HDIM:]
    lane = lax.broadcasted_iota(jnp.int32, (padded, HDIM), 1)
    scores = jnp.zeros((padded, HDIM), jnp.float32)
    for number in range(heads):
        total = jnp.sum(product[:, number * HDIM : (number + 1) * HDIM], axis=1, keepdims=True)
        scores = jnp.where(lane == number, total, scores)
    scores = scores.T[:8]
    scores = scores * HDIM ** (-0.5)
    segment = jnp.broadcast_to(segment_row[...], (8, padded))
    forward = backward = scores
    step = 1
    while step < span:
        same = pltpu.roll(segment, step, 1) == segment
        forward = jnp.maximum(forward, jnp.where(same, pltpu.roll(forward, step, 1), -1e30))
        same = pltpu.roll(segment, padded - step, 1) == segment
        backward = jnp.maximum(
            backward, jnp.where(same, pltpu.roll(backward, padded - step, 1), -1e30)
        )
        step *= 2
    weights = jnp.exp(scores - jnp.maximum(forward, backward)).astype(jnp.bfloat16)
    gathered = []
    for number in range(heads):
        spread = member[...] * weights[number : number + 1, :]
        total = f32_dot(spread, value_ext[number])
        divisor = total[:, HDIM:]
        gathered.append((total[:, :HDIM] / jnp.where(divisor > 0, divisor, 1.0)).astype(jnp.bfloat16))
    attended = jnp.concatenate(gathered, axis=1)
    for number in range(5):
        rows = slice(number * PAT_DEV, (number + 1) * PAT_DEV)
        places[number][...] = f32_dot(chosen[rows, :], attended).astype(jnp.bfloat16)


def block_parts(blocks, steps, first, count):
    if steps != 4:
        return [(blocks[steps + (steps > 4)], first, 0, count)]
    half = blocks[4].shape[0]
    parts = []
    if first < half:
        parts.append((blocks[4], first, 0, min(count, half - first)))
    if first + count > half:
        start = max(first, half)
        parts.append((blocks[5], start - half, start - first, first + count - start))
    return parts


def pack_kernel(query, key, value, out_rows, packed, folded, wide, *rest):
    landed, sems = rest[:4], rest[4]
    copies = [
        pltpu.make_async_copy(source, target, sems.at[i])
        for i, (source, target) in enumerate(zip((query, key, value, out_rows), landed))
    ]
    for copy in copies:
        copy.start()
    rows = query.shape[0]
    for number in range(3):
        copies[number].wait()
        wide[number * rows : (number + 1) * rows, :] = landed[number][...].astype(jnp.float32)
    packed[...] = wide[...].astype(jnp.bfloat16)
    copies[3].wait()
    tall = folded.shape[0]
    for number in range(folded.shape[1] // HDIM):
        piece = landed[3][number * tall : (number + 1) * tall, :]
        folded[:, number * HDIM : (number + 1) * HDIM] = piece


def order_kernel(place, *refs):
    turns, folded, block, wide = refs[:4], refs[4], refs[5], refs[6]
    rows = turns[0].shape[0] // 3
    for number, turn in enumerate(turns):
        at = (place[0] + 4 - number) & 3
        values = turn[...].astype(jnp.float32)
        for part in range(3):
            row = pl.multiple_of(part * 4 * rows + at * rows, 8)
            wide[pl.ds(row, rows), :] = values[part * rows : (part + 1) * rows, :]
    block[: 12 * rows, :] = wide[...].astype(jnp.bfloat16)
    block[12 * rows :, :] = folded[...]


def join_kernel(first, *refs):
    out = refs[-1]
    tall = out.shape[0] // (len(refs) - 1)
    for number, block in enumerate(refs[:-1]):
        start = min(first, block.shape[0] - tall)
        out[number * tall : (number + 1) * tall, :] = block[start : start + tall, :]


def unfold_kernel(place, *refs):
    sources, out = refs[:12], refs[12]
    tall = sources[0].shape[0] // 3
    for number, sets in enumerate(((0, 1, 7), (2, 6), (3, 5, 4))):
        for turn in range(4):
            source = sources[4 * number + turn]
            lanes = pl.ds(pl.multiple_of(((place[1] + 4 - turn) & 3) * HDIM, HDIM), HDIM)
            for order, steps in enumerate(sets):
                group = (place[0] + 8 - steps) & 7
                for piece in range(4):
                    out[group, piece * tall : (piece + 1) * tall, lanes] = source[
                        order * tall : (order + 1) * tall, piece * HDIM : (piece + 1) * HDIM
                    ]


def term_kernel(partner, place, *refs):
    pieces, weight, out, buffer, sems = refs[:3], *refs[3:]
    core = 1 - place[3] if partner else place[3]
    copies = [
        pltpu.make_async_copy(weight.at[2 * ((place[2] + i) & 3) + core], buffer.at[i], sems.at[i])
        for i in range(4)
    ]
    for copy in copies:
        copy.start()
    total = pieces[0][...].astype(jnp.float32)
    for piece in pieces[1:]:
        total = total + piece[...].astype(jnp.float32)
    landed = total.astype(jnp.bfloat16)
    for i in range(4):
        copies[i].wait()
        out[i] = f32_dot(landed, buffer[i]).astype(out.dtype)


def gradient_kernel(place, mine, other, weight, out, buffer, sems):
    copies = []
    for i in range(8):
        core = place[3] if i < 4 else 1 - place[3]
        group = 2 * ((place[2] + 4 - i % 4) & 3) + core
        copies.append(pltpu.make_async_copy(weight.at[group], buffer.at[i], sems.at[i]))
    for copy in copies:
        copy.start()
    total = jnp.zeros(out.shape, jnp.float32)
    for i in range(8):
        copies[i].wait()
        picked = mine[i] if i < 4 else other[i - 4]
        total = total + f32_dot(picked, buffer[i], ((1,), (1,)))
    out[...] = total


def per_device(byte_states, norm_gain, patch_window, w_query, w_key, w_value, w_out, cotangent):
    byte_count, width = byte_states.shape
    rows, columns = w_query.shape
    span = byte_count + MOST
    padded = -(-span // HDIM) * HDIM
    my_z, my_x, my_y, my_c = (lax.axis_index(name) for name in DP + GRP)
    shape, half, full = jax.ShapeDtypeStruct, jnp.bfloat16, jnp.float32
    barrier = lax.optimization_barrier
    vmem = pl.BlockSpec(memory_space=pltpu.VMEM)
    smem = pl.BlockSpec(memory_space=pltpu.SMEM)
    anywhere = pl.BlockSpec(memory_space=pl.ANY)

    tall = w_out.shape[0] * HDIM // columns
    packed, folded = vmem_call(
        pack_kernel,
        (shape((3 * rows, columns), half), shape((tall, columns), half)),
        in_specs=[anywhere] * 4,
        out_specs=(vmem, vmem),
        scratch_shapes=[pltpu.VMEM((3 * rows, columns), full)]
        + [pltpu.VMEM((rows, columns), half)] * 3
        + [pltpu.VMEM(w_out.shape, half), pltpu.SemaphoreType.DMA((4,))],
    )(w_query, w_key, w_value, w_out)
    turns = [packed] + [ring(packed, "x", steps) for steps in (1, 2, 3)]
    turns, folded = barrier((turns, folded))
    deep = 12 * rows
    block = vmem_call(
        order_kernel,
        shape((deep + tall, columns), half),
        in_specs=[smem] + [vmem] * 5,
        out_specs=vmem,
        scratch_shapes=[pltpu.VMEM((deep, columns), full)],
    )(my_x.astype(jnp.int32).reshape(1), *turns, folded)
    block, last_rows, window = barrier((block, byte_states[byte_count - MOST :], patch_window))

    def join(*blocks):
        return vmem_call(functools.partial(join_kernel, deep), shape((len(blocks) * tall, columns), half))(
            *blocks
        )

    def along_x(piece):
        return [piece, ring(piece, "x", 1), None, ring(piece, "x", -1)]

    ring_z = {0: block, 1: ring(block, "z", 1), 7: ring(block, "z", -1)}
    before = from_behind(last_rows, 1)
    cot_y = [cotangent, ring(cotangent, "y", 1), None, ring(cotangent, "y", -1)]
    patch_ids = window[:, :span]
    first_patch = window[0, MOST]
    patch_total = window[0, span] - first_patch
    relative = patch_ids - first_patch
    owned = (relative >= 0) & (relative < patch_total)
    segment = jnp.where(owned, relative, PCAP)
    segment_row = jnp.pad(segment, ((0, 0), (0, padded - span)), constant_values=PCAP)
    segment_col = segment.reshape(span, 1)
    base = (lax.axis_index(DP) - 2) * PAT_DEV - first_patch
    place = jnp.stack([my_z, my_x, my_y, my_c, base]).astype(jnp.int32)
    gain = norm_gain[None, :]
    masks = vmem_call(
        mask_kernel,
        (
            shape((PCAP, padded), half),
            shape((span, PCAP), half),
            shape((5 * PAT_DEV, PCAP), half),
            shape((PCAP, 1), full),
        ),
        in_specs=[smem, vmem, vmem],
        out_specs=(vmem,) * 4,
    )(place, segment_row, segment_col)
    ring_z[1], ring_z[7], before, cot_y[1::2], place, segment_row, gain, masks, states = barrier(
        (ring_z[1], ring_z[7], before, cot_y[1::2], place, segment_row, gain, masks, byte_states)
    )
    member, reader, chosen, sizes = masks
    ring_z[2], ring_z[6] = ring(ring_z[1], "z", 1), ring(ring_z[7], "z", -1)
    out_x = [along_x(join(block, ring_z[1], ring_z[7]))]
    cot_y[2] = ring(cot_y[1], "y", 1)
    normed, pooled = vmem_call(
        prepare_kernel,
        (shape((span, width), half), shape((PCAP, width), half)),
        in_specs=[vmem] * 5,
        out_specs=(vmem,) * 2,
    )(before, states, gain, member, sizes)
    ring_z[2], ring_z[6], out_x[0][1::2], cot_y[2], normed, pooled = barrier(
        (ring_z[2], ring_z[6], out_x[0][1::2], cot_y[2], normed, pooled)
    )
    ring_z[3], ring_z[5] = ring(ring_z[2], "z", 1), ring(ring_z[6], "z", -1)
    out_x[0][2] = ring(out_x[0][1], "x", 1)
    out_x.append(along_x(join(ring_z[2], ring_z[6])))
    cot_mine = jnp.stack(cot_y)
    ring_z[3], ring_z[5], out_x[0][2], out_x[1][1::2], cot_mine = barrier(
        (ring_z[3], ring_z[5], out_x[0][2], out_x[1][1::2], cot_mine)
    )
    mid = (deep + tall) // 2
    last_a, last_b = ring(ring_z[3][:mid], "z", 1), ring(ring_z[5][mid:], "z", -1)
    out_x[1][2] = ring(out_x[1][1], "x", 1)
    cot_other = ring(cot_mine, "c", 1)
    last_a, last_b, cot_other, ring_z[3], ring_z[5], out_x[1][2] = barrier(
        (last_a, last_b, cot_other, ring_z[3], ring_z[5], out_x[1][2])
    )
    blocks = [ring_z[0], ring_z[1], ring_z[2], ring_z[3], last_a, last_b]
    blocks += [ring_z[5], ring_z[6], ring_z[7]]
    out_x.append(along_x(join(ring_z[3], ring_z[5], last_b)))

    spot_shape = shape((PAT_DEV, columns), half)
    *places, queries = vmem_call(
        attend_kernel,
        (spot_shape,) * 5 + (shape((PCAP, columns), half),),
        in_specs=[smem] + [vmem] * 6 + [anywhere] * 9,
        out_specs=(vmem,) * 6,
        scratch_shapes=[
            pltpu.VMEM((width, 3 * columns), half),
            pltpu.VMEM((padded, columns), full),
            pltpu.VMEM((columns // HDIM, padded, 2 * HDIM), half),
            pltpu.SemaphoreType.DMA((3,)),
        ],
    )(place, normed, pooled, member, reader, chosen, segment_row, *blocks)
    places, queries, out_x[2][1::2] = barrier((places, queries, out_x[2][1::2]))

    def first_step(spread):
        return from_behind(spread[4], 1), from_behind(spread[0], -1)

    def second_step(spread, up, down):
        return [
            spread[2],
            from_behind(spread[3] + up, 1),
            from_behind(spread[1] + down, -1),
        ]

    up, down = first_step(places)
    out_x[2][2] = ring(out_x[2][1], "x", 1)
    asked = vmem_call(place_kernel, (spot_shape,) * 5)(chosen, queries)
    up, down, asked = barrier((up, down, asked))
    pieces = second_step(places, up, down)
    asked_up, asked_down = first_step(asked)
    weight = vmem_call(
        unfold_kernel,
        shape((8, columns, columns), half),
        in_specs=[smem] + [vmem] * 12,
        out_specs=vmem,
    )(place, *[piece for pieces in out_x for piece in pieces])
    pieces, weight, asked, asked_up, asked_down = barrier(
        (pieces, weight, asked, asked_up, asked_down)
    )

    def terms(partner):
        return vmem_call(
            functools.partial(term_kernel, partner),
            shape((4, PAT_DEV, columns), half),
            in_specs=[smem] + [vmem] * 3 + [anywhere],
            out_specs=vmem,
            scratch_shapes=[
                pltpu.VMEM((4, columns, columns), half),
                pltpu.SemaphoreType.DMA((4,)),
            ],
        )(place, *pieces, weight)

    theirs = terms(True)
    arrived = ring(theirs, "c", 1)
    mine = terms(False)
    arrived, mine = barrier((arrived, mine))
    paired = [(mine[d].astype(full) + arrived[d].astype(full)).astype(half) for d in range(4)]
    paired, asked = barrier((paired, asked))
    mixed = [paired[0]] + [ring(paired[steps], "y", steps) for steps in (2, 1, 3)]
    gradient = vmem_call(
        gradient_kernel,
        shape((PAT_DEV, columns), full),
        in_specs=[smem, vmem, vmem, anywhere],
        out_specs=vmem,
        scratch_shapes=[
            pltpu.VMEM((8, columns, columns), half),
            pltpu.SemaphoreType.DMA((8,)),
        ],
    )(place, cot_mine, cot_other, weight)
    asked = second_step(asked, asked_up, asked_down)
    mixed, gradient = barrier((mixed, gradient))
    queries = asked[0].astype(full) + asked[1].astype(full) + asked[2].astype(full)
    mixed = (mixed[0].astype(full) + mixed[1].astype(full)) + (
        mixed[2].astype(full) + mixed[3].astype(full)
    )
    patch_rows = (queries + mixed).astype(half)
    return (patch_rows, gradient)


def solution(mesh):
    fine = Mesh(mesh.devices.reshape(8, 4, 4, 2), DP + GRP)
    return jax.shard_map(
        per_device,
        mesh=fine,
        in_specs=(
            P(DP, None),
            P(),
            P(DP, None),
            P(DP, GRP),
            P(DP, GRP),
            P(DP, GRP),
            P(GRP, DP),
            P(DP, GRP),
        ),
        out_specs=(P(DP, GRP), P(DP, GRP)),
        check_vma=False,
    )
```

```python
import functools

import jax
import jax.numpy as jnp
from jax import lax
from jax.experimental import pallas as pl
from jax.experimental.pallas import tpu as pltpu
from jax.sharding import Mesh, PartitionSpec as P

HDIM = 128
MOST = 16
PAT_DEV = 256
PCAP = 640
OFFSETS = (-2, -1, 0, 1, 2)
EPSILON = 1e-05
DP = ("z", "x")
GRP = ("y", "c")
VMEM_BYTES = 52 * 1024 * 1024


def ring(value, axis, steps):
    count = lax.axis_size(axis)
    return lax.ppermute(value, axis, [(i, (i + steps) % count) for i in range(count)])


def from_behind(value, steps):
    count = lax.axis_size(DP)
    leading, last = (max(0, -steps), min(count, count - steps))
    return lax.ppermute(value, DP, [(source, source + steps) for source in range(leading, last)])


def vmem_call(kernel, out_shape, **more):
    params = pltpu.CompilerParams(vmem_limit_bytes=VMEM_BYTES)
    return pl.pallas_call(kernel, out_shape=out_shape, compiler_params=params, **more)


def one_hot(rows, columns):
    return jnp.where(rows == columns, 1.0, 0.0).astype(jnp.bfloat16)


def f32_dot(a, b, contract=((1,), (0,))):
    return lax.dot_general(a, b, (contract, ((), ())), preferred_element_type=jnp.float32)


def mask_kernel(place, segment_row, segment_col, member_out, read_out, land_out, size_out):
    member = jnp.where(
        lax.broadcasted_iota(jnp.int32, member_out.shape, 0) == segment_row[...], 1.0, 0.0
    )
    member_out[...] = member.astype(jnp.bfloat16)
    sizes = jnp.sum(member, axis=1, keepdims=True)
    size_out[...] = jnp.where(sizes > 0, sizes, 1.0)
    read_out[...] = one_hot(lax.broadcasted_iota(jnp.int32, read_out.shape, 1), segment_col[...])
    landing = lax.broadcasted_iota(jnp.int32, land_out.shape, 0) + place[4]
    land_out[...] = one_hot(landing, lax.broadcasted_iota(jnp.int32, land_out.shape, 1))


def prepare_kernel(before, states, gain, member, sizes, normed_out, pool_out):
    for source, start in ((before, 0), (states, MOST)):
        rows = source[...].astype(jnp.float32)
        mean_square = jnp.mean(rows * rows, axis=1, keepdims=True)
        normed = rows * lax.rsqrt(mean_square + EPSILON) * gain[...]
        normed_out[pl.ds(start, rows.shape[0]), :] = normed.astype(jnp.bfloat16)
    sums = f32_dot(member[:, : normed_out.shape[0]], normed_out[...])
    pool_out[...] = (sums / sizes[...]).astype(jnp.bfloat16)


def place_kernel(chosen, source, *places):
    for number, place in enumerate(places):
        rows = slice(number * PAT_DEV, (number + 1) * PAT_DEV)
        place[...] = f32_dot(chosen[rows, :], source[...]).astype(jnp.bfloat16)


def attend_kernel(place, normed, pooled, member, reader, chosen, segment_row, *rest):
    blocks, places, asked = rest[:9], rest[9:14], rest[14]
    weight, product, value_ext, sems = rest[15:]
    span = normed.shape[0]
    padded, columns = product.shape
    heads = columns // HDIM
    depth = weight.shape[0] // 8
    copies = []
    for steps in range(8):
        row = pl.multiple_of(((place[0] + 8 - steps) & 7) * depth, 16)
        for part in range(3):
            lanes = pl.ds(part * columns, columns)
            for block, first, start, count in block_parts(blocks, steps, part * depth, depth):
                source = block.at[pl.ds(first, count), :]
                target = weight.at[pl.ds(row + start, count), lanes]
                copies.append(pltpu.make_async_copy(source, target, sems.at[part]))
    for copy in copies:
        copy.start()
    value_ext[:, span:, :HDIM] = jnp.zeros((heads, padded - span, HDIM), jnp.bfloat16)
    value_ext[:, :, HDIM:] = jnp.ones((heads, padded, HDIM), jnp.bfloat16)
    product[pl.ds(span, padded - span), :] = jnp.zeros((padded - span, columns), jnp.float32)

    def arrive(part):
        whole = weight.at[:, pl.ds(part * columns, columns)]
        pltpu.make_async_copy(whole, whole, sems.at[part]).wait()

    arrive(0)
    queries = f32_dot(pooled[...], weight[:, :columns]).astype(jnp.bfloat16)
    asked[...] = queries
    arrive(1)
    wide = 2 * HDIM
    for start in range(0, columns, wide):
        lanes = slice(start, start + wide)
        keys = f32_dot(normed[...], weight[:, columns + start : columns + start + wide])
        read = f32_dot(reader[...], queries[:, lanes])
        product[:span, lanes] = read * keys.astype(jnp.bfloat16).astype(jnp.float32)
    arrive(2)
    for start in range(0, columns, wide):
        values = f32_dot(normed[...], weight[:, 2 * columns + start : 2 * columns + start + wide])
        values = values.astype(jnp.bfloat16)
        value_ext[start // HDIM, :span, :HDIM] = values[:, :HDIM]
        value_ext[start // HDIM + 1, :span, :HDIM] = values[:, HDIM:]
    lane = lax.broadcasted_iota(jnp.int32, (padded, HDIM), 1)
    scores = jnp.zeros((padded, HDIM), jnp.float32)
    for number in range(heads):
        total = jnp.sum(product[:, number * HDIM : (number + 1) * HDIM], axis=1, keepdims=True)
        scores = jnp.where(lane == number, total, scores)
    scores = scores.T[:8]
    scores = scores * HDIM ** (-0.5)
    segment = jnp.broadcast_to(segment_row[...], (8, padded))
    forward = backward = scores
    step = 1
    while step < span:
        same = pltpu.roll(segment, step, 1) == segment
        forward = jnp.maximum(forward, jnp.where(same, pltpu.roll(forward, step, 1), -1e30))
        same = pltpu.roll(segment, padded - step, 1) == segment
        backward = jnp.maximum(
            backward, jnp.where(same, pltpu.roll(backward, padded - step, 1), -1e30)
        )
        step *= 2
    weights = jnp.exp(scores - jnp.maximum(forward, backward)).astype(jnp.bfloat16)
    gathered = []
    for number in range(heads):
        spread = member[...] * weights[number : number + 1, :]
        total = f32_dot(spread, value_ext[number])
        divisor = total[:, HDIM:]
        gathered.append((total[:, :HDIM] / jnp.where(divisor > 0, divisor, 1.0)).astype(jnp.bfloat16))
    attended = jnp.concatenate(gathered, axis=1)
    for number in range(5):
        rows = slice(number * PAT_DEV, (number + 1) * PAT_DEV)
        places[number][...] = f32_dot(chosen[rows, :], attended).astype(jnp.bfloat16)


def block_parts(blocks, steps, first, count):
    if steps != 4:
        return [(blocks[steps + (steps > 4)], first, 0, count)]
    half = blocks[4].shape[0]
    parts = []
    if first < half:
        parts.append((blocks[4], first, 0, min(count, half - first)))
    if first + count > half:
        start = max(first, half)
        parts.append((blocks[5], start - half, start - first, first + count - start))
    return parts


def pack_kernel(query, key, value, out_rows, packed, folded, wide, *rest):
    landed, sems = rest[:4], rest[4]
    copies = [
        pltpu.make_async_copy(source, target, sems.at[i])
        for i, (source, target) in enumerate(zip((query, key, value, out_rows), landed))
    ]
    for copy in copies:
        copy.start()
    rows = query.shape[0]
    for number in range(3):
        copies[number].wait()
        wide[number * rows : (number + 1) * rows, :] = landed[number][...].astype(jnp.float32)
    packed[...] = wide[...].astype(jnp.bfloat16)
    copies[3].wait()
    tall = folded.shape[0]
    for number in range(folded.shape[1] // HDIM):
        piece = landed[3][number * tall : (number + 1) * tall, :]
        folded[:, number * HDIM : (number + 1) * HDIM] = piece


def order_kernel(place, *refs):
    turns, folded, block, wide = refs[:4], refs[4], refs[5], refs[6]
    rows = turns[0].shape[0] // 3
    for number, turn in enumerate(turns):
        at = (place[0] + 4 - number) & 3
        values = turn[...].astype(jnp.float32)
        for part in range(3):
            row = pl.multiple_of(part * 4 * rows + at * rows, 8)
            wide[pl.ds(row, rows), :] = values[part * rows : (part + 1) * rows, :]
    block[: 12 * rows, :] = wide[...].astype(jnp.bfloat16)
    block[12 * rows :, :] = folded[...]


def join_kernel(first, *refs):
    out = refs[-1]
    tall = out.shape[0] // (len(refs) - 1)
    for number, block in enumerate(refs[:-1]):
        start = min(first, block.shape[0] - tall)
        out[number * tall : (number + 1) * tall, :] = block[start : start + tall, :]


def unfold_kernel(counts, place, *refs):
    sources, out = refs[:-1], refs[-1]
    first = 0
    for number, count in enumerate(counts):
        tall = sources[4 * number].shape[0] // count
        for turn in range(4):
            source = sources[4 * number + turn]
            lanes = pl.ds(pl.multiple_of(((place[1] + 4 - turn) & 3) * HDIM, HDIM), HDIM)
            for order in range(count):
                for piece in range(4):
                    out[first + order, piece * tall : (piece + 1) * tall, lanes] = source[
                        order * tall : (order + 1) * tall, piece * HDIM : (piece + 1) * HDIM
                    ]
        first += count


def start_block(place, group, near, far, target, sem):
    steps = (place[0] + 8 - group) & 7
    is_near = (steps < 2) | (steps == 7)
    where_far = jnp.where(steps == 2, 0, jnp.where(steps == 6, 1, jnp.where(steps == 3, 2, 8 - steps)))

    @pl.when(is_near)
    def _():
        pltpu.make_async_copy(near.at[jnp.minimum(steps, 2)], target, sem).start()

    @pl.when(jnp.logical_not(is_near))
    def _():
        pltpu.make_async_copy(far.at[where_far], target, sem).start()


def term_kernel(partner, place, *refs):
    pieces, near, far, out, buffer, sems = refs[:5], *refs[5:]
    core = 1 - place[3] if partner else place[3]
    for i in range(4):
        group = 2 * ((place[2] + i) & 3) + core
        start_block(place, group, near, far, buffer.at[i], sems.at[i])
    total = pieces[0][...].astype(jnp.float32)
    for piece in pieces[1:]:
        total = total + piece[...].astype(jnp.float32)
    landed = total.astype(jnp.bfloat16)
    for i in range(4):
        pltpu.make_async_copy(buffer.at[i], buffer.at[i], sems.at[i]).wait()
        out[i] = f32_dot(landed, buffer[i]).astype(out.dtype)


def gradient_kernel(place, mine, other, near, far, out, buffer, sems):
    for i in range(8):
        core = place[3] if i < 4 else 1 - place[3]
        group = 2 * ((place[2] + 4 - i % 4) & 3) + core
        start_block(place, group, near, far, buffer.at[i], sems.at[i])
    total = jnp.zeros(out.shape, jnp.float32)
    for i in range(8):
        pltpu.make_async_copy(buffer.at[i], buffer.at[i], sems.at[i]).wait()
        picked = mine[i] if i < 4 else other[i - 4]
        total = total + f32_dot(picked, buffer[i], ((1,), (1,)))
    out[...] = total


def per_device(byte_states, norm_gain, patch_window, w_query, w_key, w_value, w_out, cotangent):
    byte_count, width = byte_states.shape
    rows, columns = w_query.shape
    span = byte_count + MOST
    padded = -(-span // HDIM) * HDIM
    my_z, my_x, my_y, my_c = (lax.axis_index(name) for name in DP + GRP)
    shape, half, full = jax.ShapeDtypeStruct, jnp.bfloat16, jnp.float32
    barrier = lax.optimization_barrier
    vmem = pl.BlockSpec(memory_space=pltpu.VMEM)
    smem = pl.BlockSpec(memory_space=pltpu.SMEM)
    anywhere = pl.BlockSpec(memory_space=pl.ANY)

    tall = w_out.shape[0] * HDIM // columns
    packed, folded = vmem_call(
        pack_kernel,
        (shape((3 * rows, columns), half), shape((tall, columns), half)),
        in_specs=[anywhere] * 4,
        out_specs=(vmem, vmem),
        scratch_shapes=[pltpu.VMEM((3 * rows, columns), full)]
        + [pltpu.VMEM((rows, columns), half)] * 3
        + [pltpu.VMEM(w_out.shape, half), pltpu.SemaphoreType.DMA((4,))],
    )(w_query, w_key, w_value, w_out)
    turns = [packed] + [ring(packed, "x", steps) for steps in (1, 2, 3)]
    turns, folded = barrier((turns, folded))
    deep = 12 * rows
    block = vmem_call(
        order_kernel,
        shape((deep + tall, columns), half),
        in_specs=[smem] + [vmem] * 5,
        out_specs=vmem,
        scratch_shapes=[pltpu.VMEM((deep, columns), full)],
    )(my_x.astype(jnp.int32).reshape(1), *turns, folded)
    block, last_rows, window = barrier((block, byte_states[byte_count - MOST :], patch_window))

    def join(*blocks):
        return vmem_call(functools.partial(join_kernel, deep), shape((len(blocks) * tall, columns), half))(
            *blocks
        )

    def along_x(piece):
        return [piece, ring(piece, "x", 1), None, ring(piece, "x", -1)]

    ring_z = {0: block, 1: ring(block, "z", 1), 7: ring(block, "z", -1)}
    before = from_behind(last_rows, 1)
    cot_y = [cotangent, ring(cotangent, "y", 1), None, ring(cotangent, "y", -1)]
    patch_ids = window[:, :span]
    first_patch = window[0, MOST]
    patch_total = window[0, span] - first_patch
    relative = patch_ids - first_patch
    owned = (relative >= 0) & (relative < patch_total)
    segment = jnp.where(owned, relative, PCAP)
    segment_row = jnp.pad(segment, ((0, 0), (0, padded - span)), constant_values=PCAP)
    segment_col = segment.reshape(span, 1)
    base = (lax.axis_index(DP) - 2) * PAT_DEV - first_patch
    place = jnp.stack([my_z, my_x, my_y, my_c, base]).astype(jnp.int32)
    gain = norm_gain[None, :]
    masks = vmem_call(
        mask_kernel,
        (
            shape((PCAP, padded), half),
            shape((span, PCAP), half),
            shape((5 * PAT_DEV, PCAP), half),
            shape((PCAP, 1), full),
        ),
        in_specs=[smem, vmem, vmem],
        out_specs=(vmem,) * 4,
    )(place, segment_row, segment_col)
    ring_z[1], ring_z[7], before, cot_y[1::2], place, segment_row, gain, masks, states = barrier(
        (ring_z[1], ring_z[7], before, cot_y[1::2], place, segment_row, gain, masks, byte_states)
    )
    member, reader, chosen, sizes = masks
    ring_z[2], ring_z[6] = ring(ring_z[1], "z", 1), ring(ring_z[7], "z", -1)
    out_x = [along_x(join(block, ring_z[1], ring_z[7]))]
    cot_y[2] = ring(cot_y[1], "y", 1)
    normed, pooled = vmem_call(
        prepare_kernel,
        (shape((span, width), half), shape((PCAP, width), half)),
        in_specs=[vmem] * 5,
        out_specs=(vmem,) * 2,
    )(before, states, gain, member, sizes)
    ring_z[2], ring_z[6], out_x[0][1::2], cot_y[2], normed, pooled = barrier(
        (ring_z[2], ring_z[6], out_x[0][1::2], cot_y[2], normed, pooled)
    )
    ring_z[3], ring_z[5] = ring(ring_z[2], "z", 1), ring(ring_z[6], "z", -1)
    out_x[0][2] = ring(out_x[0][1], "x", 1)
    out_x.append(along_x(join(ring_z[2], ring_z[6])))
    cot_mine = jnp.stack(cot_y)
    ring_z[3], ring_z[5], out_x[0][2], out_x[1][1::2], cot_mine = barrier(
        (ring_z[3], ring_z[5], out_x[0][2], out_x[1][1::2], cot_mine)
    )
    mid = (deep + tall) // 2
    last_a, last_b = ring(ring_z[3][:mid], "z", 1), ring(ring_z[5][mid:], "z", -1)
    out_x[1][2] = ring(out_x[1][1], "x", 1)
    out_x.append(along_x(join(ring_z[3], ring_z[5])))

    def unfold(place, *sources):
        counts = tuple(source[0].shape[0] // tall for source in sources)
        return vmem_call(
            functools.partial(unfold_kernel, counts),
            shape((sum(counts), columns, columns), half),
            in_specs=[smem] + [vmem] * (4 * len(counts)),
            out_specs=vmem,
        )(place, *[piece for source in sources for piece in source])

    near = unfold(place, out_x[0])
    last_a, last_b, out_x[1][2], out_x[2][1::2], near = barrier(
        (last_a, last_b, out_x[1][2], out_x[2][1::2], near)
    )
    blocks = [ring_z[0], ring_z[1], ring_z[2], ring_z[3], last_a, last_b]
    blocks += [ring_z[5], ring_z[6], ring_z[7]]
    out_x[2][2] = ring(out_x[2][1], "x", 1)
    out_x.append(along_x(last_b[deep - mid :]))

    spot_shape = shape((PAT_DEV, columns), half)
    *places, queries = vmem_call(
        attend_kernel,
        (spot_shape,) * 5 + (shape((PCAP, columns), half),),
        in_specs=[smem] + [vmem] * 6 + [anywhere] * 9,
        out_specs=(vmem,) * 6,
        scratch_shapes=[
            pltpu.VMEM((width, 3 * columns), half),
            pltpu.VMEM((padded, columns), full),
            pltpu.VMEM((columns // HDIM, padded, 2 * HDIM), half),
            pltpu.SemaphoreType.DMA((3,)),
        ],
    )(place, normed, pooled, member, reader, chosen, segment_row, *blocks)
    places, queries, out_x[2][2], out_x[3][1::2] = barrier(
        (places, queries, out_x[2][2], out_x[3][1::2])
    )

    def first_step(spread):
        return from_behind(spread[4], 1), from_behind(spread[0], -1)

    def second_step(spread, up, down):
        return [
            spread[2],
            from_behind(spread[3] + up, 1),
            from_behind(spread[1] + down, -1),
        ]

    pieces = [places[2]] + [from_behind(places[offset + 2], offset) for offset in (-2, -1, 1, 2)]
    out_x[3][2] = ring(out_x[3][1], "x", 1)
    asked = vmem_call(place_kernel, (spot_shape,) * 5)(chosen, queries)
    far = unfold(place, *out_x[1:])
    pieces, far, asked, cot_mine = barrier((pieces, far, asked, cot_mine))

    def terms(partner):
        return vmem_call(
            functools.partial(term_kernel, partner),
            shape((4, PAT_DEV, columns), half),
            in_specs=[smem] + [vmem] * 5 + [anywhere] * 2,
            out_specs=vmem,
            scratch_shapes=[
                pltpu.VMEM((4, columns, columns), half),
                pltpu.SemaphoreType.DMA((4,)),
            ],
        )(place, *pieces, near, far)

    theirs = terms(True)
    theirs, asked, cot_mine = barrier((theirs, asked, cot_mine))
    arrived = ring(theirs, "c", 1)
    asked_up, asked_down = first_step(asked)
    cot_other = ring(cot_mine, "c", 1)
    mine = terms(False)
    arrived, mine = barrier((arrived, mine))
    paired = [(mine[d].astype(full) + arrived[d].astype(full)).astype(half) for d in range(4)]
    paired, asked = barrier((paired, asked))
    mixed = [paired[0]] + [ring(paired[steps], "y", steps) for steps in (2, 1, 3)]
    gradient = vmem_call(
        gradient_kernel,
        shape((PAT_DEV, columns), full),
        in_specs=[smem, vmem, vmem, anywhere, anywhere],
        out_specs=vmem,
        scratch_shapes=[
            pltpu.VMEM((8, columns, columns), half),
            pltpu.SemaphoreType.DMA((8,)),
        ],
    )(place, cot_mine, cot_other, near, far)
    asked = second_step(asked, asked_up, asked_down)
    mixed, gradient = barrier((mixed, gradient))
    queries = asked[0].astype(full) + asked[1].astype(full) + asked[2].astype(full)
    mixed = (mixed[0].astype(full) + mixed[1].astype(full)) + (
        mixed[2].astype(full) + mixed[3].astype(full)
    )
    patch_rows = (queries + mixed).astype(half)
    return (patch_rows, gradient)


def solution(mesh):
    fine = Mesh(mesh.devices.reshape(8, 4, 4, 2), DP + GRP)
    return jax.shard_map(
        per_device,
        mesh=fine,
        in_specs=(
            P(DP, None),
            P(),
            P(DP, None),
            P(DP, GRP),
            P(DP, GRP),
            P(DP, GRP),
            P(GRP, DP),
            P(DP, GRP),
        ),
        out_specs=(P(DP, GRP), P(DP, GRP)),
        check_vma=False,
    )
```

```python
import functools

import jax
import jax.numpy as jnp
from jax import lax
from jax.experimental import pallas as pl
from jax.experimental.pallas import tpu as pltpu
from jax.sharding import Mesh, PartitionSpec as P

HDIM = 128
MOST = 16
PAT_DEV = 256
PCAP = 640
OFFSETS = (-2, -1, 0, 1, 2)
EPSILON = 1e-05
DP = ("z", "x")
GRP = ("y", "c")
VMEM_BYTES = 52 * 1024 * 1024


def ring(value, axis, steps):
    count = lax.axis_size(axis)
    return lax.ppermute(value, axis, [(i, (i + steps) % count) for i in range(count)])


def from_behind(value, steps):
    count = lax.axis_size(DP)
    leading, last = (max(0, -steps), min(count, count - steps))
    return lax.ppermute(value, DP, [(source, source + steps) for source in range(leading, last)])


def vmem_call(kernel, out_shape, **more):
    params = pltpu.CompilerParams(vmem_limit_bytes=VMEM_BYTES)
    return pl.pallas_call(kernel, out_shape=out_shape, compiler_params=params, **more)


def one_hot(rows, columns):
    return jnp.where(rows == columns, 1.0, 0.0).astype(jnp.bfloat16)


def f32_dot(a, b, contract=((1,), (0,))):
    return lax.dot_general(a, b, (contract, ((), ())), preferred_element_type=jnp.float32)


def mask_kernel(place, segment_row, segment_col, member_out, read_out, land_out, size_out):
    member = jnp.where(
        lax.broadcasted_iota(jnp.int32, member_out.shape, 0) == segment_row[...], 1.0, 0.0
    )
    member_out[...] = member.astype(jnp.bfloat16)
    sizes = jnp.sum(member, axis=1, keepdims=True)
    size_out[...] = jnp.where(sizes > 0, sizes, 1.0)
    read_out[...] = one_hot(lax.broadcasted_iota(jnp.int32, read_out.shape, 1), segment_col[...])
    landing = lax.broadcasted_iota(jnp.int32, land_out.shape, 0) + place[4]
    land_out[...] = one_hot(landing, lax.broadcasted_iota(jnp.int32, land_out.shape, 1))


def prepare_kernel(before, states, gain, member, sizes, normed_out, pool_out):
    for source, start in ((before, 0), (states, MOST)):
        rows = source[...].astype(jnp.float32)
        mean_square = jnp.mean(rows * rows, axis=1, keepdims=True)
        normed = rows * lax.rsqrt(mean_square + EPSILON) * gain[...]
        normed_out[pl.ds(start, rows.shape[0]), :] = normed.astype(jnp.bfloat16)
    sums = f32_dot(member[:, : normed_out.shape[0]], normed_out[...])
    pool_out[...] = (sums / sizes[...]).astype(jnp.bfloat16)


def place_kernel(chosen, source, *places):
    for number, place in enumerate(places):
        rows = slice(number * PAT_DEV, (number + 1) * PAT_DEV)
        place[...] = f32_dot(chosen[rows, :], source[...]).astype(jnp.bfloat16)


def attend_kernel(place, normed, pooled, member, reader, chosen, segment_row, *rest):
    blocks, places, asked = rest[:9], rest[9:14], rest[14]
    weight, product, value_ext, sems = rest[15:]
    span = normed.shape[0]
    padded, columns = product.shape
    heads = columns // HDIM
    depth = weight.shape[0] // 8
    copies = []
    for steps in range(8):
        row = pl.multiple_of(((place[0] + 8 - steps) & 7) * depth, 16)
        for part in range(3):
            lanes = pl.ds(part * columns, columns)
            for block, first, start, count in block_parts(blocks, steps, part * depth, depth):
                source = block.at[pl.ds(first, count), :]
                target = weight.at[pl.ds(row + start, count), lanes]
                copies.append(pltpu.make_async_copy(source, target, sems.at[part]))
    for copy in copies:
        copy.start()
    value_ext[:, span:, :HDIM] = jnp.zeros((heads, padded - span, HDIM), jnp.bfloat16)
    value_ext[:, :, HDIM:] = jnp.ones((heads, padded, HDIM), jnp.bfloat16)
    product[pl.ds(span, padded - span), :] = jnp.zeros((padded - span, columns), jnp.float32)

    def arrive(part):
        whole = weight.at[:, pl.ds(part * columns, columns)]
        pltpu.make_async_copy(whole, whole, sems.at[part]).wait()

    arrive(0)
    queries = f32_dot(pooled[...], weight[:, :columns]).astype(jnp.bfloat16)
    asked[...] = queries
    arrive(1)
    wide = 2 * HDIM
    for start in range(0, columns, wide):
        lanes = slice(start, start + wide)
        keys = f32_dot(normed[...], weight[:, columns + start : columns + start + wide])
        read = f32_dot(reader[...], queries[:, lanes])
        product[:span, lanes] = read * keys.astype(jnp.bfloat16).astype(jnp.float32)
    arrive(2)
    for start in range(0, columns, wide):
        values = f32_dot(normed[...], weight[:, 2 * columns + start : 2 * columns + start + wide])
        values = values.astype(jnp.bfloat16)
        value_ext[start // HDIM, :span, :HDIM] = values[:, :HDIM]
        value_ext[start // HDIM + 1, :span, :HDIM] = values[:, HDIM:]
    lane = lax.broadcasted_iota(jnp.int32, (padded, HDIM), 1)
    scores = jnp.zeros((padded, HDIM), jnp.float32)
    for number in range(heads):
        total = jnp.sum(product[:, number * HDIM : (number + 1) * HDIM], axis=1, keepdims=True)
        scores = jnp.where(lane == number, total, scores)
    scores = scores.T[:8]
    scores = scores * HDIM ** (-0.5)
    segment = jnp.broadcast_to(segment_row[...], (8, padded))
    forward = backward = scores
    step = 1
    while step < span:
        same = pltpu.roll(segment, step, 1) == segment
        forward = jnp.maximum(forward, jnp.where(same, pltpu.roll(forward, step, 1), -1e30))
        same = pltpu.roll(segment, padded - step, 1) == segment
        backward = jnp.maximum(
            backward, jnp.where(same, pltpu.roll(backward, padded - step, 1), -1e30)
        )
        step *= 2
    weights = jnp.exp(scores - jnp.maximum(forward, backward)).astype(jnp.bfloat16)
    gathered = []
    for number in range(heads):
        spread = member[...] * weights[number : number + 1, :]
        total = f32_dot(spread, value_ext[number])
        divisor = total[:, HDIM:]
        gathered.append((total[:, :HDIM] / jnp.where(divisor > 0, divisor, 1.0)).astype(jnp.bfloat16))
    attended = jnp.concatenate(gathered, axis=1)
    for number in range(5):
        rows = slice(number * PAT_DEV, (number + 1) * PAT_DEV)
        places[number][...] = f32_dot(chosen[rows, :], attended).astype(jnp.bfloat16)


def block_parts(blocks, steps, first, count):
    if steps != 4:
        return [(blocks[steps + (steps > 4)], first, 0, count)]
    half = blocks[4].shape[0]
    parts = []
    if first < half:
        parts.append((blocks[4], first, 0, min(count, half - first)))
    if first + count > half:
        start = max(first, half)
        parts.append((blocks[5], start - half, start - first, first + count - start))
    return parts


def pack_kernel(query, key, value, out_rows, packed, folded, wide, *rest):
    landed, sems = rest[:4], rest[4]
    copies = [
        pltpu.make_async_copy(source, target, sems.at[i])
        for i, (source, target) in enumerate(zip((query, key, value, out_rows), landed))
    ]
    for copy in copies:
        copy.start()
    rows = query.shape[0]
    for number in range(3):
        copies[number].wait()
        wide[number * rows : (number + 1) * rows, :] = landed[number][...].astype(jnp.float32)
    packed[...] = wide[...].astype(jnp.bfloat16)
    copies[3].wait()
    tall = folded.shape[0]
    for number in range(folded.shape[1] // HDIM):
        piece = landed[3][number * tall : (number + 1) * tall, :]
        folded[:, number * HDIM : (number + 1) * HDIM] = piece


def order_kernel(place, *refs):
    turns, folded, block, wide = refs[:4], refs[4], refs[5], refs[6]
    rows = turns[0].shape[0] // 3
    for number, turn in enumerate(turns):
        at = (place[0] + 4 - number) & 3
        values = turn[...].astype(jnp.float32)
        for part in range(3):
            row = pl.multiple_of(part * 4 * rows + at * rows, 8)
            wide[pl.ds(row, rows), :] = values[part * rows : (part + 1) * rows, :]
    block[: 12 * rows, :] = wide[...].astype(jnp.bfloat16)
    block[12 * rows :, :] = folded[...]


def join_kernel(first, *refs):
    out = refs[-1]
    tall = out.shape[0] // (len(refs) - 1)
    for number, block in enumerate(refs[:-1]):
        start = min(first, block.shape[0] - tall)
        out[number * tall : (number + 1) * tall, :] = block[start : start + tall, :]


def unfold_kernel(place, *refs):
    sources, out = refs[:4], refs[4]
    count = out.shape[0]
    tall = sources[0].shape[0] // count
    for turn, source in enumerate(sources):
        lanes = pl.ds(pl.multiple_of(((place[1] + 4 - turn) & 3) * HDIM, HDIM), HDIM)
        for order in range(count):
            for piece in range(4):
                out[order, piece * tall : (piece + 1) * tall, lanes] = source[
                    order * tall : (order + 1) * tall, piece * HDIM : (piece + 1) * HDIM
                ]


ARRIVALS = ((0, 1, 7), (2, 6), (3, 5, 4))


def start_block(place, group, weights, target, sem):
    steps = (place[0] + 8 - group) & 7
    for part, weight in zip(ARRIVALS, weights):
        held = steps == part[0]
        index = 0
        for order, number in enumerate(part[1:], 1):
            held = held | (steps == number)
            index = jnp.where(steps == number, order, index)

        @pl.when(held)
        def _(weight=weight, index=index):
            pltpu.make_async_copy(weight.at[index], target, sem).start()


def term_kernel(partner, place, *refs):
    pieces, weights, out, buffer, sems = refs[:3], refs[3:6], *refs[6:]
    core = 1 - place[3] if partner else place[3]
    for i in range(4):
        group = 2 * ((place[2] + i) & 3) + core
        start_block(place, group, weights, buffer.at[i], sems.at[i])
    total = pieces[0][...].astype(jnp.float32)
    for piece in pieces[1:]:
        total = total + piece[...].astype(jnp.float32)
    landed = total.astype(jnp.bfloat16)
    for i in range(4):
        pltpu.make_async_copy(buffer.at[i], buffer.at[i], sems.at[i]).wait()
        out[i] = f32_dot(landed, buffer[i]).astype(out.dtype)


def gradient_kernel(place, mine, other, *refs):
    weights, out, buffer, sems = refs[:3], *refs[3:]
    for i in range(8):
        core = place[3] if i < 4 else 1 - place[3]
        group = 2 * ((place[2] + 4 - i % 4) & 3) + core
        start_block(place, group, weights, buffer.at[i], sems.at[i])
    total = jnp.zeros(out.shape, jnp.float32)
    for i in range(8):
        pltpu.make_async_copy(buffer.at[i], buffer.at[i], sems.at[i]).wait()
        picked = mine[i] if i < 4 else other[i - 4]
        total = total + f32_dot(picked, buffer[i], ((1,), (1,)))
    out[...] = total


def per_device(byte_states, norm_gain, patch_window, w_query, w_key, w_value, w_out, cotangent):
    byte_count, width = byte_states.shape
    rows, columns = w_query.shape
    span = byte_count + MOST
    padded = -(-span // HDIM) * HDIM
    my_z, my_x, my_y, my_c = (lax.axis_index(name) for name in DP + GRP)
    shape, half, full = jax.ShapeDtypeStruct, jnp.bfloat16, jnp.float32
    barrier = lax.optimization_barrier
    vmem = pl.BlockSpec(memory_space=pltpu.VMEM)
    smem = pl.BlockSpec(memory_space=pltpu.SMEM)
    anywhere = pl.BlockSpec(memory_space=pl.ANY)

    tall = w_out.shape[0] * HDIM // columns
    packed, folded = vmem_call(
        pack_kernel,
        (shape((3 * rows, columns), half), shape((tall, columns), half)),
        in_specs=[anywhere] * 4,
        out_specs=(vmem, vmem),
        scratch_shapes=[pltpu.VMEM((3 * rows, columns), full)]
        + [pltpu.VMEM((rows, columns), half)] * 3
        + [pltpu.VMEM(w_out.shape, half), pltpu.SemaphoreType.DMA((4,))],
    )(w_query, w_key, w_value, w_out)
    turns = [packed] + [ring(packed, "x", steps) for steps in (1, 2, 3)]
    turns, folded = barrier((turns, folded))
    deep = 12 * rows
    block = vmem_call(
        order_kernel,
        shape((deep + tall, columns), half),
        in_specs=[smem] + [vmem] * 5,
        out_specs=vmem,
        scratch_shapes=[pltpu.VMEM((deep, columns), full)],
    )(my_x.astype(jnp.int32).reshape(1), *turns, folded)
    block, last_rows, window = barrier((block, byte_states[byte_count - MOST :], patch_window))

    def join(*blocks):
        return vmem_call(functools.partial(join_kernel, deep), shape((len(blocks) * tall, columns), half))(
            *blocks
        )

    def along_x(piece):
        return [piece, ring(piece, "x", 1), None, ring(piece, "x", -1)]

    ring_z = {0: block, 1: ring(block, "z", 1), 7: ring(block, "z", -1)}
    before = from_behind(last_rows, 1)
    cot_y = [cotangent, ring(cotangent, "y", 1), None, ring(cotangent, "y", -1)]
    patch_ids = window[:, :span]
    first_patch = window[0, MOST]
    patch_total = window[0, span] - first_patch
    relative = patch_ids - first_patch
    owned = (relative >= 0) & (relative < patch_total)
    segment = jnp.where(owned, relative, PCAP)
    segment_row = jnp.pad(segment, ((0, 0), (0, padded - span)), constant_values=PCAP)
    segment_col = segment.reshape(span, 1)
    base = (lax.axis_index(DP) - 2) * PAT_DEV - first_patch
    place = jnp.stack([my_z, my_x, my_y, my_c, base]).astype(jnp.int32)
    gain = norm_gain[None, :]
    masks = vmem_call(
        mask_kernel,
        (
            shape((PCAP, padded), half),
            shape((span, PCAP), half),
            shape((5 * PAT_DEV, PCAP), half),
            shape((PCAP, 1), full),
        ),
        in_specs=[smem, vmem, vmem],
        out_specs=(vmem,) * 4,
    )(place, segment_row, segment_col)
    ring_z[1], ring_z[7], before, cot_y[1::2], place, segment_row, gain, masks, states = barrier(
        (ring_z[1], ring_z[7], before, cot_y[1::2], place, segment_row, gain, masks, byte_states)
    )
    member, reader, chosen, sizes = masks
    ring_z[2], ring_z[6] = ring(ring_z[1], "z", 1), ring(ring_z[7], "z", -1)
    out_x = [along_x(join(block, ring_z[1], ring_z[7]))]
    cot_y[2] = ring(cot_y[1], "y", 1)
    normed, pooled = vmem_call(
        prepare_kernel,
        (shape((span, width), half), shape((PCAP, width), half)),
        in_specs=[vmem] * 5,
        out_specs=(vmem,) * 2,
    )(before, states, gain, member, sizes)
    ring_z[2], ring_z[6], out_x[0][1::2], cot_y[2], normed, pooled = barrier(
        (ring_z[2], ring_z[6], out_x[0][1::2], cot_y[2], normed, pooled)
    )
    ring_z[3], ring_z[5] = ring(ring_z[2], "z", 1), ring(ring_z[6], "z", -1)
    out_x[0][2] = ring(out_x[0][1], "x", 1)
    out_x.append(along_x(join(ring_z[2], ring_z[6])))
    cot_mine = jnp.stack(cot_y)
    ring_z[3], ring_z[5], out_x[0][2], out_x[1][1::2], cot_mine = barrier(
        (ring_z[3], ring_z[5], out_x[0][2], out_x[1][1::2], cot_mine)
    )
    mid = (deep + tall) // 2
    last_a, last_b = ring(ring_z[3][:mid], "z", 1), ring(ring_z[5][mid:], "z", -1)
    out_x[1][2] = ring(out_x[1][1], "x", 1)
    cot_other = ring(cot_mine, "c", 1)

    def unfold(sources):
        return vmem_call(
            unfold_kernel,
            shape((sources[0].shape[0] // tall, columns, columns), half),
            in_specs=[smem] + [vmem] * 4,
            out_specs=vmem,
        )(place, *sources)

    weights = [unfold(out_x[0])]
    last_a, last_b, cot_other, ring_z[3], ring_z[5], weights = barrier(
        (last_a, last_b, cot_other, ring_z[3], ring_z[5], weights)
    )
    blocks = [ring_z[0], ring_z[1], ring_z[2], ring_z[3], last_a, last_b]
    blocks += [ring_z[5], ring_z[6], ring_z[7]]
    out_x.append(along_x(join(ring_z[3], ring_z[5], last_b)))

    spot_shape = shape((PAT_DEV, columns), half)
    *places, queries = vmem_call(
        attend_kernel,
        (spot_shape,) * 5 + (shape((PCAP, columns), half),),
        in_specs=[smem] + [vmem] * 6 + [anywhere] * 9,
        out_specs=(vmem,) * 6,
        scratch_shapes=[
            pltpu.VMEM((width, 3 * columns), half),
            pltpu.VMEM((padded, columns), full),
            pltpu.VMEM((columns // HDIM, padded, 2 * HDIM), half),
            pltpu.SemaphoreType.DMA((3,)),
        ],
    )(place, normed, pooled, member, reader, chosen, segment_row, *blocks)
    places, queries, out_x[2][1::2] = barrier((places, queries, out_x[2][1::2]))

    def first_step(spread):
        return from_behind(spread[4], 1), from_behind(spread[0], -1)

    def second_step(spread, up, down):
        return [
            spread[2],
            from_behind(spread[3] + up, 1),
            from_behind(spread[1] + down, -1),
        ]

    up, down = first_step(places)
    out_x[2][2] = ring(out_x[2][1], "x", 1)
    asked = vmem_call(place_kernel, (spot_shape,) * 5)(chosen, queries)
    weights.append(unfold(out_x[1]))
    up, down, asked, weights = barrier((up, down, asked, weights))
    pieces = second_step(places, up, down)
    asked_up, asked_down = first_step(asked)
    weights.append(unfold(out_x[2]))
    pieces, weights, asked, asked_up, asked_down = barrier(
        (pieces, weights, asked, asked_up, asked_down)
    )

    def terms(partner):
        return vmem_call(
            functools.partial(term_kernel, partner),
            shape((4, PAT_DEV, columns), half),
            in_specs=[smem] + [vmem] * 3 + [anywhere] * 3,
            out_specs=vmem,
            scratch_shapes=[
                pltpu.VMEM((4, columns, columns), half),
                pltpu.SemaphoreType.DMA((4,)),
            ],
        )(place, *pieces, *weights)

    theirs = terms(True)
    arrived = ring(theirs, "c", 1)
    mine = terms(False)
    asked = second_step(asked, asked_up, asked_down)
    arrived, mine = barrier((arrived, mine))
    paired = [(mine[d].astype(full) + arrived[d].astype(full)).astype(half) for d in range(4)]
    mixed = [paired[0]] + [ring(paired[steps], "y", steps) for steps in (2, 1, 3)]
    asked, cot_other = barrier((asked, cot_other))
    gradient = vmem_call(
        gradient_kernel,
        shape((PAT_DEV, columns), full),
        in_specs=[smem, vmem, vmem] + [anywhere] * 3,
        out_specs=vmem,
        scratch_shapes=[
            pltpu.VMEM((8, columns, columns), half),
            pltpu.SemaphoreType.DMA((8,)),
        ],
    )(place, cot_mine, cot_other, *weights)
    mixed, gradient = barrier((mixed, gradient))
    queries = asked[0].astype(full) + asked[1].astype(full) + asked[2].astype(full)
    mixed = (mixed[0].astype(full) + mixed[1].astype(full)) + (
        mixed[2].astype(full) + mixed[3].astype(full)
    )
    patch_rows = (queries + mixed).astype(half)
    return (patch_rows, gradient)


def solution(mesh):
    fine = Mesh(mesh.devices.reshape(8, 4, 4, 2), DP + GRP)
    return jax.shard_map(
        per_device,
        mesh=fine,
        in_specs=(
            P(DP, None),
            P(),
            P(DP, None),
            P(DP, GRP),
            P(DP, GRP),
            P(DP, GRP),
            P(GRP, DP),
            P(DP, GRP),
        ),
        out_specs=(P(DP, GRP), P(DP, GRP)),
        check_vma=False,
    )
```

```python
import functools

import jax
import jax.numpy as jnp
from jax import lax
from jax.experimental import pallas as pl
from jax.experimental.pallas import tpu as pltpu
from jax.sharding import Mesh, PartitionSpec as P

HDIM = 128
MOST = 16
PAT_DEV = 256
PCAP = 640
OFFSETS = (-2, -1, 0, 1, 2)
EPSILON = 1e-05
DP = ("z", "x")
GRP = ("y", "c")
VMEM_BYTES = 52 * 1024 * 1024


def ring(value, axis, steps):
    count = lax.axis_size(axis)
    return lax.ppermute(value, axis, [(i, (i + steps) % count) for i in range(count)])


def from_behind(value, steps):
    count = lax.axis_size(DP)
    leading, last = (max(0, -steps), min(count, count - steps))
    return lax.ppermute(value, DP, [(source, source + steps) for source in range(leading, last)])


def vmem_call(kernel, out_shape, limit=VMEM_BYTES, **more):
    params = pltpu.CompilerParams(vmem_limit_bytes=limit)
    return pl.pallas_call(kernel, out_shape=out_shape, compiler_params=params, **more)


def one_hot(rows, columns):
    return jnp.where(rows == columns, 1.0, 0.0).astype(jnp.bfloat16)


def f32_dot(a, b, contract=((1,), (0,))):
    return lax.dot_general(a, b, (contract, ((), ())), preferred_element_type=jnp.float32)


def mask_kernel(place, segment_row, segment_col, member_out, read_out, land_out, size_out):
    member = jnp.where(
        lax.broadcasted_iota(jnp.int32, member_out.shape, 0) == segment_row[...], 1.0, 0.0
    )
    member_out[...] = member.astype(jnp.bfloat16)
    sizes = jnp.sum(member, axis=1, keepdims=True)
    size_out[...] = jnp.where(sizes > 0, sizes, 1.0)
    read_out[...] = one_hot(lax.broadcasted_iota(jnp.int32, read_out.shape, 1), segment_col[...])
    landing = lax.broadcasted_iota(jnp.int32, land_out.shape, 0) + place[4]
    land_out[...] = one_hot(landing, lax.broadcasted_iota(jnp.int32, land_out.shape, 1))


def prepare_kernel(before, states, gain, member, sizes, normed_out, pool_out):
    for source, start in ((before, 0), (states, MOST)):
        rows = source[...].astype(jnp.float32)
        mean_square = jnp.mean(rows * rows, axis=1, keepdims=True)
        normed = rows * lax.rsqrt(mean_square + EPSILON) * gain[...]
        normed_out[pl.ds(start, rows.shape[0]), :] = normed.astype(jnp.bfloat16)
    sums = f32_dot(member[:, : normed_out.shape[0]], normed_out[...])
    pool_out[...] = (sums / sizes[...]).astype(jnp.bfloat16)


def place_kernel(chosen, source, *places):
    for number, place in enumerate(places):
        rows = slice(number * PAT_DEV, (number + 1) * PAT_DEV)
        place[...] = f32_dot(chosen[rows, :], source[...]).astype(jnp.bfloat16)


def attend_kernel(place, normed, pooled, member, reader, chosen, segment_row, *rest):
    blocks, places, asked = rest[:9], rest[9:14], rest[14]
    weight, product, value_ext, sems = rest[15:]
    span = normed.shape[0]
    padded, columns = product.shape
    heads = columns // HDIM
    depth = weight.shape[0] // 8
    copies = []
    for steps in range(8):
        row = pl.multiple_of(((place[0] + 8 - steps) & 7) * depth, 16)
        for part in range(3):
            lanes = pl.ds(part * columns, columns)
            for block, first, start, count in block_parts(blocks, steps, part * depth, depth):
                source = block.at[pl.ds(first, count), :]
                target = weight.at[pl.ds(row + start, count), lanes]
                copies.append(pltpu.make_async_copy(source, target, sems.at[part]))
    for copy in copies:
        copy.start()
    value_ext[:, span:, :HDIM] = jnp.zeros((heads, padded - span, HDIM), jnp.bfloat16)
    value_ext[:, :, HDIM:] = jnp.ones((heads, padded, HDIM), jnp.bfloat16)
    product[pl.ds(span, padded - span), :] = jnp.zeros((padded - span, columns), jnp.float32)

    def arrive(part):
        whole = weight.at[:, pl.ds(part * columns, columns)]
        pltpu.make_async_copy(whole, whole, sems.at[part]).wait()

    arrive(0)
    queries = f32_dot(pooled[...], weight[:, :columns]).astype(jnp.bfloat16)
    asked[...] = queries
    arrive(1)
    wide = 2 * HDIM
    for start in range(0, columns, wide):
        lanes = slice(start, start + wide)
        keys = f32_dot(normed[...], weight[:, columns + start : columns + start + wide])
        read = f32_dot(reader[...], queries[:, lanes])
        product[:span, lanes] = read * keys.astype(jnp.bfloat16).astype(jnp.float32)
    arrive(2)
    for start in range(0, columns, wide):
        values = f32_dot(normed[...], weight[:, 2 * columns + start : 2 * columns + start + wide])
        values = values.astype(jnp.bfloat16)
        value_ext[start // HDIM, :span, :HDIM] = values[:, :HDIM]
        value_ext[start // HDIM + 1, :span, :HDIM] = values[:, HDIM:]
    lane = lax.broadcasted_iota(jnp.int32, (padded, HDIM), 1)
    scores = jnp.zeros((padded, HDIM), jnp.float32)
    for number in range(heads):
        total = jnp.sum(product[:, number * HDIM : (number + 1) * HDIM], axis=1, keepdims=True)
        scores = jnp.where(lane == number, total, scores)
    scores = scores.T[:8]
    scores = scores * HDIM ** (-0.5)
    segment = jnp.broadcast_to(segment_row[...], (8, padded))
    forward = backward = scores
    step = 1
    while step < span:
        same = pltpu.roll(segment, step, 1) == segment
        forward = jnp.maximum(forward, jnp.where(same, pltpu.roll(forward, step, 1), -1e30))
        same = pltpu.roll(segment, padded - step, 1) == segment
        backward = jnp.maximum(
            backward, jnp.where(same, pltpu.roll(backward, padded - step, 1), -1e30)
        )
        step *= 2
    weights = jnp.exp(scores - jnp.maximum(forward, backward)).astype(jnp.bfloat16)
    gathered = []
    for number in range(heads):
        spread = member[...] * weights[number : number + 1, :]
        total = f32_dot(spread, value_ext[number])
        divisor = total[:, HDIM:]
        gathered.append((total[:, :HDIM] / jnp.where(divisor > 0, divisor, 1.0)).astype(jnp.bfloat16))
    attended = jnp.concatenate(gathered, axis=1)
    for number in range(5):
        rows = slice(number * PAT_DEV, (number + 1) * PAT_DEV)
        places[number][...] = f32_dot(chosen[rows, :], attended).astype(jnp.bfloat16)


def block_parts(blocks, steps, first, count):
    if steps != 4:
        return [(blocks[steps + (steps > 4)], first, 0, count)]
    half = blocks[4].shape[0]
    parts = []
    if first < half:
        parts.append((blocks[4], first, 0, min(count, half - first)))
    if first + count > half:
        start = max(first, half)
        parts.append((blocks[5], start - half, start - first, first + count - start))
    return parts


def pack_kernel(query, key, value, out_rows, packed, folded, wide, *rest):
    landed, sems = rest[:4], rest[4]
    copies = [
        pltpu.make_async_copy(source, target, sems.at[i])
        for i, (source, target) in enumerate(zip((query, key, value, out_rows), landed))
    ]
    for copy in copies:
        copy.start()
    rows = query.shape[0]
    for number in range(3):
        copies[number].wait()
        wide[number * rows : (number + 1) * rows, :] = landed[number][...].astype(jnp.float32)
    packed[...] = wide[...].astype(jnp.bfloat16)
    copies[3].wait()
    tall = folded.shape[0]
    for number in range(folded.shape[1] // HDIM):
        piece = landed[3][number * tall : (number + 1) * tall, :]
        folded[:, number * HDIM : (number + 1) * HDIM] = piece


def order_kernel(place, *refs):
    turns, folded, block, wide = refs[:4], refs[4], refs[5], refs[6]
    rows = turns[0].shape[0] // 3
    for number, turn in enumerate(turns):
        at = (place[0] + 4 - number) & 3
        values = turn[...].astype(jnp.float32)
        for part in range(3):
            row = pl.multiple_of(part * 4 * rows + at * rows, 8)
            wide[pl.ds(row, rows), :] = values[part * rows : (part + 1) * rows, :]
    block[: 12 * rows, :] = wide[...].astype(jnp.bfloat16)
    block[12 * rows :, :] = folded[...]


def join_kernel(first, *refs):
    out = refs[-1]
    tall = out.shape[0] // (len(refs) - 1)
    for number, block in enumerate(refs[:-1]):
        start = min(first, block.shape[0] - tall)
        out[number * tall : (number + 1) * tall, :] = block[start : start + tall, :]


def unfold_kernel(place, *refs):
    sources, out = refs[:4], refs[4]
    count = out.shape[0]
    tall = sources[0].shape[0] // count
    for turn, source in enumerate(sources):
        lanes = pl.ds(pl.multiple_of(((place[1] + 4 - turn) & 3) * HDIM, HDIM), HDIM)
        for order in range(count):
            for piece in range(4):
                out[order, piece * tall : (piece + 1) * tall, lanes] = source[
                    order * tall : (order + 1) * tall, piece * HDIM : (piece + 1) * HDIM
                ]


ARRIVALS = ((0, 1, 7), (2, 6), (3, 5, 4))


def start_block(place, group, weights, target, sem):
    steps = (place[0] + 8 - group) & 7
    for part, weight in zip(ARRIVALS, weights):
        held = steps == part[0]
        index = 0
        for order, number in enumerate(part[1:], 1):
            held = held | (steps == number)
            index = jnp.where(steps == number, order, index)

        @pl.when(held)
        def _(weight=weight, index=index):
            pltpu.make_async_copy(weight.at[index], target, sem).start()


def term_kernel(partner, place, *refs):
    pieces, weights, out, buffer, sems = refs[:3], refs[3:6], *refs[6:]
    core = 1 - place[3] if partner else place[3]
    for i in range(4):
        group = 2 * ((place[2] + i) & 3) + core
        start_block(place, group, weights, buffer.at[i], sems.at[i])
    total = pieces[0][...].astype(jnp.float32)
    for piece in pieces[1:]:
        total = total + piece[...].astype(jnp.float32)
    landed = total.astype(jnp.bfloat16)
    for i in range(4):
        pltpu.make_async_copy(buffer.at[i], buffer.at[i], sems.at[i]).wait()
        out[i] = f32_dot(landed, buffer[i]).astype(out.dtype)


def gradient_kernel(place, mine, other, *refs):
    weights, out, buffer, sems = refs[:3], *refs[3:]
    for i in range(8):
        core = place[3] if i < 4 else 1 - place[3]
        group = 2 * ((place[2] + 4 - i % 4) & 3) + core
        start_block(place, group, weights, buffer.at[i], sems.at[i])
    total = jnp.zeros(out.shape, jnp.float32)
    for i in range(8):
        pltpu.make_async_copy(buffer.at[i], buffer.at[i], sems.at[i]).wait()
        picked = mine[i] if i < 4 else other[i - 4]
        total = total + f32_dot(picked, buffer[i], ((1,), (1,)))
    out[...] = total


def per_device(byte_states, norm_gain, patch_window, w_query, w_key, w_value, w_out, cotangent):
    byte_count, width = byte_states.shape
    rows, columns = w_query.shape
    span = byte_count + MOST
    padded = -(-span // HDIM) * HDIM
    my_z, my_x, my_y, my_c = (lax.axis_index(name) for name in DP + GRP)
    shape, half, full = jax.ShapeDtypeStruct, jnp.bfloat16, jnp.float32
    barrier = lax.optimization_barrier
    vmem = pl.BlockSpec(memory_space=pltpu.VMEM)
    smem = pl.BlockSpec(memory_space=pltpu.SMEM)
    anywhere = pl.BlockSpec(memory_space=pl.ANY)

    tall = w_out.shape[0] * HDIM // columns
    packed, folded = vmem_call(
        pack_kernel,
        (shape((3 * rows, columns), half), shape((tall, columns), half)),
        in_specs=[anywhere] * 4,
        out_specs=(vmem, vmem),
        limit=64 * 1024 * 1024 - 64 * 1024,
        scratch_shapes=[pltpu.VMEM((3 * rows, columns), full)]
        + [pltpu.VMEM((rows, columns), half)] * 3
        + [pltpu.VMEM(w_out.shape, half), pltpu.SemaphoreType.DMA((4,))],
    )(w_query, w_key, w_value, w_out)
    turns = [packed] + [ring(packed, "x", steps) for steps in (1, 2, 3)]
    turns, folded = barrier((turns, folded))
    deep = 12 * rows
    block = vmem_call(
        order_kernel,
        shape((deep + tall, columns), half),
        in_specs=[smem] + [vmem] * 5,
        out_specs=vmem,
        scratch_shapes=[pltpu.VMEM((deep, columns), full)],
    )(my_x.astype(jnp.int32).reshape(1), *turns, folded)
    block, last_rows, window = barrier((block, byte_states[byte_count - MOST :], patch_window))

    def join(*blocks):
        return vmem_call(functools.partial(join_kernel, deep), shape((len(blocks) * tall, columns), half))(
            *blocks
        )

    def along_x(piece):
        return [piece, ring(piece, "x", 1), None, ring(piece, "x", -1)]

    ring_z = {0: block, 1: ring(block, "z", 1), 7: ring(block, "z", -1)}
    before = from_behind(last_rows, 1)
    cot_y = [cotangent, ring(cotangent, "y", 1), None, ring(cotangent, "y", -1)]
    patch_ids = window[:, :span]
    first_patch = window[0, MOST]
    patch_total = window[0, span] - first_patch
    relative = patch_ids - first_patch
    owned = (relative >= 0) & (relative < patch_total)
    segment = jnp.where(owned, relative, PCAP)
    segment_row = jnp.pad(segment, ((0, 0), (0, padded - span)), constant_values=PCAP)
    segment_col = segment.reshape(span, 1)
    base = (lax.axis_index(DP) - 2) * PAT_DEV - first_patch
    place = jnp.stack([my_z, my_x, my_y, my_c, base]).astype(jnp.int32)
    gain = norm_gain[None, :]
    masks = vmem_call(
        mask_kernel,
        (
            shape((PCAP, padded), half),
            shape((span, PCAP), half),
            shape((5 * PAT_DEV, PCAP), half),
            shape((PCAP, 1), full),
        ),
        in_specs=[smem, vmem, vmem],
        out_specs=(vmem,) * 4,
    )(place, segment_row, segment_col)
    ring_z[1], ring_z[7], before, cot_y[1::2], place, segment_row, gain, masks, states = barrier(
        (ring_z[1], ring_z[7], before, cot_y[1::2], place, segment_row, gain, masks, byte_states)
    )
    member, reader, chosen, sizes = masks
    ring_z[2], ring_z[6] = ring(ring_z[1], "z", 1), ring(ring_z[7], "z", -1)
    out_x = [along_x(join(block, ring_z[1], ring_z[7]))]
    cot_y[2] = ring(cot_y[1], "y", 1)
    normed, pooled = vmem_call(
        prepare_kernel,
        (shape((span, width), half), shape((PCAP, width), half)),
        in_specs=[vmem] * 5,
        out_specs=(vmem,) * 2,
    )(before, states, gain, member, sizes)
    ring_z[2], ring_z[6], out_x[0][1::2], cot_y[2], normed, pooled = barrier(
        (ring_z[2], ring_z[6], out_x[0][1::2], cot_y[2], normed, pooled)
    )
    ring_z[3], ring_z[5] = ring(ring_z[2], "z", 1), ring(ring_z[6], "z", -1)
    out_x[0][2] = ring(out_x[0][1], "x", 1)
    out_x.append(along_x(join(ring_z[2], ring_z[6])))
    cot_mine = jnp.stack(cot_y)
    ring_z[3], ring_z[5], out_x[0][2], out_x[1][1::2], cot_mine = barrier(
        (ring_z[3], ring_z[5], out_x[0][2], out_x[1][1::2], cot_mine)
    )
    mid = (deep + tall) // 2
    last_a, last_b = ring(ring_z[3][:mid], "z", 1), ring(ring_z[5][mid:], "z", -1)
    out_x[1][2] = ring(out_x[1][1], "x", 1)
    cot_other = ring(cot_mine, "c", 1)

    def unfold(sources):
        return vmem_call(
            unfold_kernel,
            shape((sources[0].shape[0] // tall, columns, columns), half),
            in_specs=[smem] + [vmem] * 4,
            out_specs=vmem,
        )(place, *sources)

    weights = [unfold(out_x[0])]
    last_a, last_b, cot_other, ring_z[3], ring_z[5], weights = barrier(
        (last_a, last_b, cot_other, ring_z[3], ring_z[5], weights)
    )
    blocks = [ring_z[0], ring_z[1], ring_z[2], ring_z[3], last_a, last_b]
    blocks += [ring_z[5], ring_z[6], ring_z[7]]
    out_x.append(along_x(join(ring_z[3], ring_z[5], last_b)))

    spot_shape = shape((PAT_DEV, columns), half)
    *places, queries = vmem_call(
        attend_kernel,
        (spot_shape,) * 5 + (shape((PCAP, columns), half),),
        in_specs=[smem] + [vmem] * 6 + [anywhere] * 9,
        out_specs=(vmem,) * 6,
        scratch_shapes=[
            pltpu.VMEM((width, 3 * columns), half),
            pltpu.VMEM((padded, columns), full),
            pltpu.VMEM((columns // HDIM, padded, 2 * HDIM), half),
            pltpu.SemaphoreType.DMA((3,)),
        ],
    )(place, normed, pooled, member, reader, chosen, segment_row, *blocks)
    places, queries, out_x[2][1::2] = barrier((places, queries, out_x[2][1::2]))

    def first_step(spread):
        return from_behind(spread[4], 1), from_behind(spread[0], -1)

    def second_step(spread, up, down):
        return [
            spread[2],
            from_behind(spread[3] + up, 1),
            from_behind(spread[1] + down, -1),
        ]

    up, down = first_step(places)
    out_x[2][2] = ring(out_x[2][1], "x", 1)
    asked = vmem_call(place_kernel, (spot_shape,) * 5)(chosen, queries)
    weights.append(unfold(out_x[1]))
    up, down, asked, weights = barrier((up, down, asked, weights))
    pieces = second_step(places, up, down)
    asked_up, asked_down = first_step(asked)
    weights.append(unfold(out_x[2]))
    pieces, weights, asked = barrier((pieces, weights, asked))

    def terms(partner):
        return vmem_call(
            functools.partial(term_kernel, partner),
            shape((4, PAT_DEV, columns), half),
            in_specs=[smem] + [vmem] * 3 + [anywhere] * 3,
            out_specs=vmem,
            scratch_shapes=[
                pltpu.VMEM((4, columns, columns), half),
                pltpu.SemaphoreType.DMA((4,)),
            ],
        )(place, *pieces, *weights)

    theirs = terms(True)
    theirs, asked_up, asked_down = barrier((theirs, asked_up, asked_down))
    arrived = ring(theirs, "c", 1)
    mine = terms(False)
    asked = second_step(asked, asked_up, asked_down)
    arrived, mine = barrier((arrived, mine))
    paired = [(mine[d].astype(full) + arrived[d].astype(full)).astype(half) for d in range(4)]
    mixed = [paired[0]] + [ring(paired[steps], "y", steps) for steps in (2, 1, 3)]
    asked, cot_other = barrier((asked, cot_other))
    gradient = vmem_call(
        gradient_kernel,
        shape((PAT_DEV, columns), full),
        in_specs=[smem, vmem, vmem] + [anywhere] * 3,
        out_specs=vmem,
        scratch_shapes=[
            pltpu.VMEM((8, columns, columns), half),
            pltpu.SemaphoreType.DMA((8,)),
        ],
    )(place, cot_mine, cot_other, *weights)
    mixed, gradient = barrier((mixed, gradient))
    queries = asked[0].astype(full) + asked[1].astype(full) + asked[2].astype(full)
    mixed = (mixed[0].astype(full) + mixed[1].astype(full)) + (
        mixed[2].astype(full) + mixed[3].astype(full)
    )
    patch_rows = (queries + mixed).astype(half)
    return (patch_rows, gradient)


def solution(mesh):
    fine = Mesh(mesh.devices.reshape(8, 4, 4, 2), DP + GRP)
    return jax.shard_map(
        per_device,
        mesh=fine,
        in_specs=(
            P(DP, None),
            P(),
            P(DP, None),
            P(DP, GRP),
            P(DP, GRP),
            P(DP, GRP),
            P(GRP, DP),
            P(DP, GRP),
        ),
        out_specs=(P(DP, GRP), P(DP, GRP)),
        check_vma=False,
    )
```

```python
import functools

import jax
import jax.numpy as jnp
from jax import lax
from jax.experimental import pallas as pl
from jax.experimental.pallas import tpu as pltpu
from jax.sharding import Mesh, PartitionSpec as P

HDIM = 128
MOST = 16
PAT_DEV = 256
PCAP = 640
OFFSETS = (-2, -1, 0, 1, 2)
EPSILON = 1e-05
DP = ("z", "x")
GRP = ("y", "c")
VMEM_BYTES = 52 * 1024 * 1024


def ring(value, axis, steps):
    count = lax.axis_size(axis)
    return lax.ppermute(value, axis, [(i, (i + steps) % count) for i in range(count)])


def from_behind(value, steps):
    count = lax.axis_size(DP)
    leading, last = (max(0, -steps), min(count, count - steps))
    return lax.ppermute(value, DP, [(source, source + steps) for source in range(leading, last)])


def vmem_call(kernel, out_shape, limit=VMEM_BYTES, **more):
    params = pltpu.CompilerParams(vmem_limit_bytes=limit)
    return pl.pallas_call(kernel, out_shape=out_shape, compiler_params=params, **more)


def one_hot(rows, columns):
    return jnp.where(rows == columns, 1.0, 0.0).astype(jnp.bfloat16)


def f32_dot(a, b, contract=((1,), (0,))):
    return lax.dot_general(a, b, (contract, ((), ())), preferred_element_type=jnp.float32)


def mask_kernel(place, segment_row, segment_col, member_out, read_out, land_out, size_out):
    member = jnp.where(
        lax.broadcasted_iota(jnp.int32, member_out.shape, 0) == segment_row[...], 1.0, 0.0
    )
    member_out[...] = member.astype(jnp.bfloat16)
    sizes = jnp.sum(member, axis=1, keepdims=True)
    size_out[...] = jnp.where(sizes > 0, sizes, 1.0)
    read_out[...] = one_hot(lax.broadcasted_iota(jnp.int32, read_out.shape, 1), segment_col[...])
    landing = lax.broadcasted_iota(jnp.int32, land_out.shape, 0) + place[4]
    land_out[...] = one_hot(landing, lax.broadcasted_iota(jnp.int32, land_out.shape, 1))


def prepare_kernel(before, states, gain, member, sizes, normed_out, pool_out):
    for source, start in ((before, 0), (states, MOST)):
        rows = source[...].astype(jnp.float32)
        mean_square = jnp.mean(rows * rows, axis=1, keepdims=True)
        normed = rows * lax.rsqrt(mean_square + EPSILON) * gain[...]
        normed_out[pl.ds(start, rows.shape[0]), :] = normed.astype(jnp.bfloat16)
    sums = f32_dot(member[:, : normed_out.shape[0]], normed_out[...])
    pool_out[...] = (sums / sizes[...]).astype(jnp.bfloat16)


def place_kernel(chosen, source, *places):
    for number, place in enumerate(places):
        rows = slice(number * PAT_DEV, (number + 1) * PAT_DEV)
        place[...] = f32_dot(chosen[rows, :], source[...]).astype(jnp.bfloat16)


def attend_kernel(place, normed, pooled, member, reader, chosen, segment_row, *rest):
    blocks, places, asked = rest[:9], rest[9:14], rest[14]
    weight, product, value_ext, sems = rest[15:]
    span = normed.shape[0]
    padded, columns = product.shape
    heads = columns // HDIM
    depth = weight.shape[0] // 8
    copies = []
    for steps in range(8):
        row = pl.multiple_of(((place[0] + 8 - steps) & 7) * depth, 16)
        for part in range(3):
            lanes = pl.ds(part * columns, columns)
            for block, first, start, count in block_parts(blocks, steps, part * depth, depth):
                source = block.at[pl.ds(first, count), :]
                target = weight.at[pl.ds(row + start, count), lanes]
                copies.append(pltpu.make_async_copy(source, target, sems.at[part]))
    for copy in copies:
        copy.start()
    value_ext[:, span:, :HDIM] = jnp.zeros((heads, padded - span, HDIM), jnp.bfloat16)
    value_ext[:, :, HDIM:] = jnp.ones((heads, padded, HDIM), jnp.bfloat16)
    product[pl.ds(span, padded - span), :] = jnp.zeros((padded - span, columns), jnp.float32)

    def arrive(part):
        whole = weight.at[:, pl.ds(part * columns, columns)]
        pltpu.make_async_copy(whole, whole, sems.at[part]).wait()

    arrive(0)
    queries = f32_dot(pooled[...], weight[:, :columns]).astype(jnp.bfloat16)
    asked[...] = queries
    arrive(1)
    wide = 2 * HDIM
    for start in range(0, columns, wide):
        lanes = slice(start, start + wide)
        keys = f32_dot(normed[...], weight[:, columns + start : columns + start + wide])
        read = f32_dot(reader[...], queries[:, lanes])
        product[:span, lanes] = read * keys.astype(jnp.bfloat16).astype(jnp.float32)
    arrive(2)
    for start in range(0, columns, wide):
        values = f32_dot(normed[...], weight[:, 2 * columns + start : 2 * columns + start + wide])
        values = values.astype(jnp.bfloat16)
        value_ext[start // HDIM, :span, :HDIM] = values[:, :HDIM]
        value_ext[start // HDIM + 1, :span, :HDIM] = values[:, HDIM:]
    lane = lax.broadcasted_iota(jnp.int32, (padded, HDIM), 1)
    scores = jnp.zeros((padded, HDIM), jnp.float32)
    for number in range(heads):
        total = jnp.sum(product[:, number * HDIM : (number + 1) * HDIM], axis=1, keepdims=True)
        scores = jnp.where(lane == number, total, scores)
    scores = scores.T[:8]
    scores = scores * HDIM ** (-0.5)
    segment = jnp.broadcast_to(segment_row[...], (8, padded))
    forward = backward = scores
    step = 1
    while step < span:
        same = pltpu.roll(segment, step, 1) == segment
        forward = jnp.maximum(forward, jnp.where(same, pltpu.roll(forward, step, 1), -1e30))
        same = pltpu.roll(segment, padded - step, 1) == segment
        backward = jnp.maximum(
            backward, jnp.where(same, pltpu.roll(backward, padded - step, 1), -1e30)
        )
        step *= 2
    weights = jnp.exp(scores - jnp.maximum(forward, backward)).astype(jnp.bfloat16)
    gathered = []
    for number in range(heads):
        spread = member[...] * weights[number : number + 1, :]
        total = f32_dot(spread, value_ext[number])
        divisor = total[:, HDIM:]
        gathered.append((total[:, :HDIM] / jnp.where(divisor > 0, divisor, 1.0)).astype(jnp.bfloat16))
    attended = jnp.concatenate(gathered, axis=1)
    for number in range(5):
        rows = slice(number * PAT_DEV, (number + 1) * PAT_DEV)
        places[number][...] = f32_dot(chosen[rows, :], attended).astype(jnp.bfloat16)


def block_parts(blocks, steps, first, count):
    if steps != 4:
        return [(blocks[steps + (steps > 4)], first, 0, count)]
    half = blocks[4].shape[0]
    parts = []
    if first < half:
        parts.append((blocks[4], first, 0, min(count, half - first)))
    if first + count > half:
        start = max(first, half)
        parts.append((blocks[5], start - half, start - first, first + count - start))
    return parts


def pack_kernel(query, key, value, out_rows, packed, folded, wide, *rest):
    landed, sems = rest[:4], rest[4]
    copies = [
        pltpu.make_async_copy(source, target, sems.at[i])
        for i, (source, target) in enumerate(zip((query, key, value, out_rows), landed))
    ]
    for copy in copies:
        copy.start()
    rows = query.shape[0]
    for number in range(3):
        copies[number].wait()
        wide[number * rows : (number + 1) * rows, :] = landed[number][...].astype(jnp.float32)
    packed[...] = wide[...].astype(jnp.bfloat16)
    copies[3].wait()
    tall = folded.shape[0]
    for number in range(folded.shape[1] // HDIM):
        piece = landed[3][number * tall : (number + 1) * tall, :]
        folded[:, number * HDIM : (number + 1) * HDIM] = piece


def order_kernel(place, *refs):
    turns, folded, block, wide = refs[:4], refs[4], refs[5], refs[6]
    rows = turns[0].shape[0] // 3
    for number, turn in enumerate(turns):
        at = (place[0] + 4 - number) & 3
        values = turn[...].astype(jnp.float32)
        for part in range(3):
            row = pl.multiple_of(part * 4 * rows + at * rows, 8)
            wide[pl.ds(row, rows), :] = values[part * rows : (part + 1) * rows, :]
    block[: 12 * rows, :] = wide[...].astype(jnp.bfloat16)
    block[12 * rows :, :] = folded[...]


def join_kernel(first, *refs):
    out = refs[-1]
    tall = out.shape[0] // (len(refs) - 1)
    for number, block in enumerate(refs[:-1]):
        start = min(first, block.shape[0] - tall)
        out[number * tall : (number + 1) * tall, :] = block[start : start + tall, :]


def unfold_kernel(place, *refs):
    sources, out = refs[:4], refs[4]
    count = out.shape[0]
    tall = sources[0].shape[0] // count
    for turn, source in enumerate(sources):
        lanes = pl.ds(pl.multiple_of(((place[1] + 4 - turn) & 3) * HDIM, HDIM), HDIM)
        for order in range(count):
            for piece in range(4):
                out[order, piece * tall : (piece + 1) * tall, lanes] = source[
                    order * tall : (order + 1) * tall, piece * HDIM : (piece + 1) * HDIM
                ]


ARRIVALS = ((0, 1, 7), (2, 6), (3, 5, 4))


def start_block(place, group, weights, target, sem):
    steps = (place[0] + 8 - group) & 7
    for part, weight in zip(ARRIVALS, weights):
        held = steps == part[0]
        index = 0
        for order, number in enumerate(part[1:], 1):
            held = held | (steps == number)
            index = jnp.where(steps == number, order, index)

        @pl.when(held)
        def _(weight=weight, index=index):
            pltpu.make_async_copy(weight.at[index], target, sem).start()


def term_kernel(partner, place, *refs):
    pieces, weights, out, buffer, sems = refs[:3], refs[3:6], *refs[6:]
    core = 1 - place[3] if partner else place[3]
    for i in range(4):
        group = 2 * ((place[2] + i) & 3) + core
        start_block(place, group, weights, buffer.at[i], sems.at[i])
    total = pieces[0][...].astype(jnp.float32)
    for piece in pieces[1:]:
        total = total + piece[...].astype(jnp.float32)
    landed = total.astype(jnp.bfloat16)
    for i in range(4):
        pltpu.make_async_copy(buffer.at[i], buffer.at[i], sems.at[i]).wait()
        out[i] = f32_dot(landed, buffer[i]).astype(out.dtype)


def gradient_kernel(place, mine, other, *refs):
    weights, out, buffer, sems = refs[:3], *refs[3:]
    for i in range(8):
        core = place[3] if i < 4 else 1 - place[3]
        group = 2 * ((place[2] + 4 - i % 4) & 3) + core
        start_block(place, group, weights, buffer.at[i], sems.at[i])
    total = jnp.zeros(out.shape, jnp.float32)
    for i in range(8):
        pltpu.make_async_copy(buffer.at[i], buffer.at[i], sems.at[i]).wait()
        picked = mine[i] if i < 4 else other[i - 4]
        total = total + f32_dot(picked, buffer[i], ((1,), (1,)))
    out[...] = total


def per_device(byte_states, norm_gain, patch_window, w_query, w_key, w_value, w_out, cotangent):
    byte_count, width = byte_states.shape
    rows, columns = w_query.shape
    span = byte_count + MOST
    padded = -(-span // HDIM) * HDIM
    my_z, my_x, my_y, my_c = (lax.axis_index(name) for name in DP + GRP)
    shape, half, full = jax.ShapeDtypeStruct, jnp.bfloat16, jnp.float32
    barrier = lax.optimization_barrier
    vmem = pl.BlockSpec(memory_space=pltpu.VMEM)
    smem = pl.BlockSpec(memory_space=pltpu.SMEM)
    anywhere = pl.BlockSpec(memory_space=pl.ANY)

    tall = w_out.shape[0] * HDIM // columns
    packed, folded = vmem_call(
        pack_kernel,
        (shape((3 * rows, columns), half), shape((tall, columns), half)),
        in_specs=[anywhere] * 4,
        out_specs=(vmem, vmem),
        limit=64 * 1024 * 1024 - 64 * 1024,
        scratch_shapes=[pltpu.VMEM((3 * rows, columns), full)]
        + [pltpu.VMEM((rows, columns), half)] * 3
        + [pltpu.VMEM(w_out.shape, half), pltpu.SemaphoreType.DMA((4,))],
    )(w_query, w_key, w_value, w_out)
    turns = [packed] + [ring(packed, "x", steps) for steps in (1, 2, 3)]
    turns, folded = barrier((turns, folded))
    deep = 12 * rows
    block = vmem_call(
        order_kernel,
        shape((deep + tall, columns), half),
        in_specs=[smem] + [vmem] * 5,
        out_specs=vmem,
        scratch_shapes=[pltpu.VMEM((deep, columns), full)],
    )(my_x.astype(jnp.int32).reshape(1), *turns, folded)
    block, last_rows, window = barrier((block, byte_states[byte_count - MOST :], patch_window))

    def join(*blocks):
        return vmem_call(functools.partial(join_kernel, deep), shape((len(blocks) * tall, columns), half))(
            *blocks
        )

    def along_x(piece):
        return [piece, ring(piece, "x", 1), None, ring(piece, "x", -1)]

    ring_z = {0: block, 1: ring(block, "z", 1), 7: ring(block, "z", -1)}
    before = from_behind(last_rows, 1)
    cot_y = [cotangent, ring(cotangent, "y", 1), None, ring(cotangent, "y", -1)]
    patch_ids = window[:, :span]
    first_patch = window[0, MOST]
    patch_total = window[0, span] - first_patch
    relative = patch_ids - first_patch
    owned = (relative >= 0) & (relative < patch_total)
    segment = jnp.where(owned, relative, PCAP)
    segment_row = jnp.pad(segment, ((0, 0), (0, padded - span)), constant_values=PCAP)
    segment_col = segment.reshape(span, 1)
    base = (lax.axis_index(DP) - 2) * PAT_DEV - first_patch
    place = jnp.stack([my_z, my_x, my_y, my_c, base]).astype(jnp.int32)
    gain = norm_gain[None, :]
    masks = vmem_call(
        mask_kernel,
        (
            shape((PCAP, padded), half),
            shape((span, PCAP), half),
            shape((5 * PAT_DEV, PCAP), half),
            shape((PCAP, 1), full),
        ),
        in_specs=[smem, vmem, vmem],
        out_specs=(vmem,) * 4,
    )(place, segment_row, segment_col)
    ring_z[1], ring_z[7], before, cot_y[1::2], place, segment_row, gain, masks, states = barrier(
        (ring_z[1], ring_z[7], before, cot_y[1::2], place, segment_row, gain, masks, byte_states)
    )
    member, reader, chosen, sizes = masks
    ring_z[2], ring_z[6] = ring(ring_z[1], "z", 1), ring(ring_z[7], "z", -1)
    out_x = [along_x(join(block, ring_z[1], ring_z[7]))]
    cot_y[2] = ring(cot_y[1], "y", 1)
    normed, pooled = vmem_call(
        prepare_kernel,
        (shape((span, width), half), shape((PCAP, width), half)),
        in_specs=[vmem] * 5,
        out_specs=(vmem,) * 2,
    )(before, states, gain, member, sizes)
    ring_z[2], ring_z[6], out_x[0][1::2], cot_y[2], normed, pooled = barrier(
        (ring_z[2], ring_z[6], out_x[0][1::2], cot_y[2], normed, pooled)
    )
    ring_z[3], ring_z[5] = ring(ring_z[2], "z", 1), ring(ring_z[6], "z", -1)
    out_x[0][2] = ring(out_x[0][1], "x", 1)
    out_x.append(along_x(join(ring_z[2], ring_z[6])))
    cot_mine = jnp.stack(cot_y)
    ring_z[3], ring_z[5], out_x[0][2], out_x[1][1::2], cot_mine = barrier(
        (ring_z[3], ring_z[5], out_x[0][2], out_x[1][1::2], cot_mine)
    )
    mid = (deep + tall) // 2
    last_a, last_b = ring(ring_z[3][:mid], "z", 1), ring(ring_z[5][mid:], "z", -1)
    out_x[1][2] = ring(out_x[1][1], "x", 1)
    cot_other = ring(cot_mine, "c", 1)

    def unfold(sources):
        return vmem_call(
            unfold_kernel,
            shape((sources[0].shape[0] // tall, columns, columns), half),
            in_specs=[smem] + [vmem] * 4,
            out_specs=vmem,
        )(place, *sources)

    weights = [unfold(out_x[0])]
    last_a, last_b, cot_other, ring_z[3], ring_z[5], weights = barrier(
        (last_a, last_b, cot_other, ring_z[3], ring_z[5], weights)
    )
    blocks = [ring_z[0], ring_z[1], ring_z[2], ring_z[3], last_a, last_b]
    blocks += [ring_z[5], ring_z[6], ring_z[7]]
    out_x.append(along_x(join(ring_z[3], ring_z[5], last_b)))

    spot_shape = shape((PAT_DEV, columns), half)
    *places, queries = vmem_call(
        attend_kernel,
        (spot_shape,) * 5 + (shape((PCAP, columns), half),),
        in_specs=[smem] + [vmem] * 6 + [anywhere] * 9,
        out_specs=(vmem,) * 6,
        scratch_shapes=[
            pltpu.VMEM((width, 3 * columns), half),
            pltpu.VMEM((padded, columns), full),
            pltpu.VMEM((columns // HDIM, padded, 2 * HDIM), half),
            pltpu.SemaphoreType.DMA((3,)),
        ],
    )(place, normed, pooled, member, reader, chosen, segment_row, *blocks)
    places, queries, out_x[1][2], out_x[2][1::2] = barrier(
        (places, queries, out_x[1][2], out_x[2][1::2])
    )

    def first_step(spread):
        return from_behind(spread[4], 1), from_behind(spread[0], -1)

    def second_step(spread, up, down):
        return [
            spread[2],
            from_behind(spread[3] + up, 1),
            from_behind(spread[1] + down, -1),
        ]

    up, down = first_step(places)
    asked = vmem_call(place_kernel, (spot_shape,) * 5)(chosen, queries)
    asked_up, asked_down = first_step(asked)
    up, down, onward = barrier((up, down, out_x[2][1]))
    pieces = second_step(places, up, down)
    out_x[2][2] = ring(onward, "x", 1)
    weights.append(unfold(out_x[1]))
    asked = second_step(asked, asked_up, asked_down)
    weights.append(unfold(out_x[2]))
    pieces, weights = barrier((pieces, weights))

    def terms(partner):
        return vmem_call(
            functools.partial(term_kernel, partner),
            shape((4, PAT_DEV, columns), half),
            in_specs=[smem] + [vmem] * 3 + [anywhere] * 3,
            out_specs=vmem,
            scratch_shapes=[
                pltpu.VMEM((4, columns, columns), half),
                pltpu.SemaphoreType.DMA((4,)),
            ],
        )(place, *pieces, *weights)

    theirs = terms(True)
    theirs, asked = barrier((theirs, asked))
    arrived = ring(theirs, "c", 1)
    mine = terms(False)
    arrived, mine = barrier((arrived, mine))
    paired = [(mine[d].astype(full) + arrived[d].astype(full)).astype(half) for d in range(4)]
    mixed = [paired[0]] + [ring(paired[steps], "y", steps) for steps in (2, 1, 3)]
    gradient = vmem_call(
        gradient_kernel,
        shape((PAT_DEV, columns), full),
        in_specs=[smem, vmem, vmem] + [anywhere] * 3,
        out_specs=vmem,
        scratch_shapes=[
            pltpu.VMEM((8, columns, columns), half),
            pltpu.SemaphoreType.DMA((8,)),
        ],
    )(place, cot_mine, cot_other, *weights)
    mixed, gradient = barrier((mixed, gradient))
    queries = asked[0].astype(full) + asked[1].astype(full) + asked[2].astype(full)
    mixed = (mixed[0].astype(full) + mixed[1].astype(full)) + (
        mixed[2].astype(full) + mixed[3].astype(full)
    )
    patch_rows = (queries + mixed).astype(half)
    return (patch_rows, gradient)


def solution(mesh):
    fine = Mesh(mesh.devices.reshape(8, 4, 4, 2), DP + GRP)
    return jax.shard_map(
        per_device,
        mesh=fine,
        in_specs=(
            P(DP, None),
            P(),
            P(DP, None),
            P(DP, GRP),
            P(DP, GRP),
            P(DP, GRP),
            P(GRP, DP),
            P(DP, GRP),
        ),
        out_specs=(P(DP, GRP), P(DP, GRP)),
        check_vma=False,
    )
```

```python
import functools

import jax
import jax.numpy as jnp
from jax import lax
from jax.experimental import pallas as pl
from jax.experimental.pallas import tpu as pltpu
from jax.sharding import Mesh, PartitionSpec as P

HDIM = 128
MOST = 16
PAT_DEV = 256
PCAP = 640
OFFSETS = (-2, -1, 0, 1, 2)
EPSILON = 1e-05
DP = ("z", "x")
GRP = ("y", "c")
VMEM_BYTES = 52 * 1024 * 1024


def ring(value, axis, steps):
    count = lax.axis_size(axis)
    return lax.ppermute(value, axis, [(i, (i + steps) % count) for i in range(count)])


def from_behind(value, steps):
    count = lax.axis_size(DP)
    leading, last = (max(0, -steps), min(count, count - steps))
    return lax.ppermute(value, DP, [(source, source + steps) for source in range(leading, last)])


def vmem_call(kernel, out_shape, limit=VMEM_BYTES, **more):
    params = pltpu.CompilerParams(vmem_limit_bytes=limit)
    return pl.pallas_call(kernel, out_shape=out_shape, compiler_params=params, **more)


def one_hot(rows, columns):
    return jnp.where(rows == columns, 1.0, 0.0).astype(jnp.bfloat16)


def f32_dot(a, b, contract=((1,), (0,))):
    return lax.dot_general(a, b, (contract, ((), ())), preferred_element_type=jnp.float32)


def mask_kernel(place, segment_row, segment_col, member_out, read_out, land_out, size_out):
    member = jnp.where(
        lax.broadcasted_iota(jnp.int32, member_out.shape, 0) == segment_row[...], 1.0, 0.0
    )
    member_out[...] = member.astype(jnp.bfloat16)
    sizes = jnp.sum(member, axis=1, keepdims=True)
    size_out[...] = jnp.where(sizes > 0, sizes, 1.0)
    read_out[...] = one_hot(lax.broadcasted_iota(jnp.int32, read_out.shape, 1), segment_col[...])
    landing = lax.broadcasted_iota(jnp.int32, land_out.shape, 0) + place[4]
    land_out[...] = one_hot(landing, lax.broadcasted_iota(jnp.int32, land_out.shape, 1))


def prepare_kernel(before, states, gain, member, sizes, normed_out, pool_out):
    for source, start in ((before, 0), (states, MOST)):
        rows = source[...].astype(jnp.float32)
        mean_square = jnp.mean(rows * rows, axis=1, keepdims=True)
        normed = rows * lax.rsqrt(mean_square + EPSILON) * gain[...]
        normed_out[pl.ds(start, rows.shape[0]), :] = normed.astype(jnp.bfloat16)
    sums = f32_dot(member[:, : normed_out.shape[0]], normed_out[...])
    pool_out[...] = (sums / sizes[...]).astype(jnp.bfloat16)


def place_kernel(chosen, source, *places):
    for number, place in enumerate(places):
        rows = slice(number * PAT_DEV, (number + 1) * PAT_DEV)
        place[...] = f32_dot(chosen[rows, :], source[...]).astype(jnp.bfloat16)


def attend_kernel(place, normed, pooled, member, reader, chosen, segment_row, *rest):
    blocks, places, asked = rest[:9], rest[9:14], rest[14]
    weight, product, value_ext, sems = rest[15:]
    span = normed.shape[0]
    padded, columns = product.shape
    heads = columns // HDIM
    depth = weight.shape[0] // 8
    copies = []
    for steps in range(8):
        row = pl.multiple_of(((place[0] + 8 - steps) & 7) * depth, 16)
        for part in range(3):
            lanes = pl.ds(part * columns, columns)
            for block, first, start, count in block_parts(blocks, steps, part * depth, depth):
                source = block.at[pl.ds(first, count), :]
                target = weight.at[pl.ds(row + start, count), lanes]
                copies.append(pltpu.make_async_copy(source, target, sems.at[part]))
    for copy in copies:
        copy.start()
    value_ext[:, span:, :HDIM] = jnp.zeros((heads, padded - span, HDIM), jnp.bfloat16)
    value_ext[:, :, HDIM:] = jnp.ones((heads, padded, HDIM), jnp.bfloat16)
    product[pl.ds(span, padded - span), :] = jnp.zeros((padded - span, columns), jnp.float32)

    def arrive(part):
        whole = weight.at[:, pl.ds(part * columns, columns)]
        pltpu.make_async_copy(whole, whole, sems.at[part]).wait()

    arrive(0)
    queries = f32_dot(pooled[...], weight[:, :columns]).astype(jnp.bfloat16)
    asked[...] = queries
    arrive(1)
    wide = 2 * HDIM
    for start in range(0, columns, wide):
        lanes = slice(start, start + wide)
        keys = f32_dot(normed[...], weight[:, columns + start : columns + start + wide])
        read = f32_dot(reader[...], queries[:, lanes])
        product[:span, lanes] = read * keys.astype(jnp.bfloat16).astype(jnp.float32)
    arrive(2)
    for start in range(0, columns, wide):
        values = f32_dot(normed[...], weight[:, 2 * columns + start : 2 * columns + start + wide])
        values = values.astype(jnp.bfloat16)
        value_ext[start // HDIM, :span, :HDIM] = values[:, :HDIM]
        value_ext[start // HDIM + 1, :span, :HDIM] = values[:, HDIM:]
    lane = lax.broadcasted_iota(jnp.int32, (padded, HDIM), 1)
    scores = jnp.zeros((padded, HDIM), jnp.float32)
    for number in range(heads):
        total = jnp.sum(product[:, number * HDIM : (number + 1) * HDIM], axis=1, keepdims=True)
        scores = jnp.where(lane == number, total, scores)
    scores = scores.T[:8]
    scores = scores * HDIM ** (-0.5)
    segment = jnp.broadcast_to(segment_row[...], (8, padded))
    forward = backward = scores
    step = 1
    while step < span:
        same = pltpu.roll(segment, step, 1) == segment
        forward = jnp.maximum(forward, jnp.where(same, pltpu.roll(forward, step, 1), -1e30))
        same = pltpu.roll(segment, padded - step, 1) == segment
        backward = jnp.maximum(
            backward, jnp.where(same, pltpu.roll(backward, padded - step, 1), -1e30)
        )
        step *= 2
    weights = jnp.exp(scores - jnp.maximum(forward, backward)).astype(jnp.bfloat16)
    gathered = []
    for number in range(heads):
        spread = member[...] * weights[number : number + 1, :]
        total = f32_dot(spread, value_ext[number])
        divisor = total[:, HDIM:]
        gathered.append((total[:, :HDIM] / jnp.where(divisor > 0, divisor, 1.0)).astype(jnp.bfloat16))
    attended = jnp.concatenate(gathered, axis=1)
    for number in range(5):
        rows = slice(number * PAT_DEV, (number + 1) * PAT_DEV)
        places[number][...] = f32_dot(chosen[rows, :], attended).astype(jnp.bfloat16)


def block_parts(blocks, steps, first, count):
    if steps != 4:
        return [(blocks[steps + (steps > 4)], first, 0, count)]
    half = blocks[4].shape[0]
    parts = []
    if first < half:
        parts.append((blocks[4], first, 0, min(count, half - first)))
    if first + count > half:
        start = max(first, half)
        parts.append((blocks[5], start - half, start - first, first + count - start))
    return parts


def pack_kernel(query, key, value, out_rows, packed, folded, wide, *rest):
    landed, sems = rest[:4], rest[4]
    copies = [
        pltpu.make_async_copy(source, target, sems.at[i])
        for i, (source, target) in enumerate(zip((query, key, value, out_rows), landed))
    ]
    for copy in copies:
        copy.start()
    rows = query.shape[0]
    for number in range(3):
        copies[number].wait()
        wide[number * rows : (number + 1) * rows, :] = landed[number][...].astype(jnp.float32)
    packed[...] = wide[...].astype(jnp.bfloat16)
    copies[3].wait()
    tall = folded.shape[0]
    for number in range(folded.shape[1] // HDIM):
        piece = landed[3][number * tall : (number + 1) * tall, :]
        folded[:, number * HDIM : (number + 1) * HDIM] = piece


def order_kernel(place, *refs):
    turns, folded, block, wide = refs[:4], refs[4], refs[5], refs[6]
    rows = turns[0].shape[0] // 3
    for number, turn in enumerate(turns):
        at = (place[0] + 4 - number) & 3
        values = turn[...].astype(jnp.float32)
        for part in range(3):
            row = pl.multiple_of(part * 4 * rows + at * rows, 8)
            wide[pl.ds(row, rows), :] = values[part * rows : (part + 1) * rows, :]
    block[: 12 * rows, :] = wide[...].astype(jnp.bfloat16)
    block[12 * rows :, :] = folded[...]


def join_kernel(first, *refs):
    out = refs[-1]
    tall = out.shape[0] // (len(refs) - 1)
    for number, block in enumerate(refs[:-1]):
        start = min(first, block.shape[0] - tall)
        out[number * tall : (number + 1) * tall, :] = block[start : start + tall, :]


def unfold_kernel(place, *refs):
    sources, out = refs[:4], refs[4]
    count = out.shape[0]
    tall = sources[0].shape[0] // count
    for turn, source in enumerate(sources):
        lanes = pl.ds(pl.multiple_of(((place[1] + 4 - turn) & 3) * HDIM, HDIM), HDIM)
        for order in range(count):
            for piece in range(4):
                out[order, piece * tall : (piece + 1) * tall, lanes] = source[
                    order * tall : (order + 1) * tall, piece * HDIM : (piece + 1) * HDIM
                ]


ARRIVALS = ((0, 1, 7), (2, 6), (3, 5, 4))


def start_block(place, group, weights, target, sem):
    steps = (place[0] + 8 - group) & 7
    for part, weight in zip(ARRIVALS, weights):
        held = steps == part[0]
        index = 0
        for order, number in enumerate(part[1:], 1):
            held = held | (steps == number)
            index = jnp.where(steps == number, order, index)

        @pl.when(held)
        def _(weight=weight, index=index):
            pltpu.make_async_copy(weight.at[index], target, sem).start()


def term_kernel(partner, place, *refs):
    pieces, weights, out, buffer, sems = refs[:3], refs[3:6], *refs[6:]
    core = 1 - place[3] if partner else place[3]
    for i in range(4):
        group = 2 * ((place[2] + i) & 3) + core
        start_block(place, group, weights, buffer.at[i], sems.at[i])
    total = pieces[0][...].astype(jnp.float32)
    for piece in pieces[1:]:
        total = total + piece[...].astype(jnp.float32)
    landed = total.astype(jnp.bfloat16)
    for i in range(4):
        pltpu.make_async_copy(buffer.at[i], buffer.at[i], sems.at[i]).wait()
        out[i] = f32_dot(landed, buffer[i]).astype(out.dtype)


def gradient_kernel(place, mine, other, *refs):
    weights, out, buffer, sems = refs[:3], *refs[3:]
    for i in range(8):
        core = place[3] if i < 4 else 1 - place[3]
        group = 2 * ((place[2] + 4 - i % 4) & 3) + core
        start_block(place, group, weights, buffer.at[i], sems.at[i])
    total = jnp.zeros(out.shape, jnp.float32)
    for i in range(8):
        pltpu.make_async_copy(buffer.at[i], buffer.at[i], sems.at[i]).wait()
        picked = mine[i] if i < 4 else other[i - 4]
        total = total + f32_dot(picked, buffer[i], ((1,), (1,)))
    out[...] = total


def per_device(byte_states, norm_gain, patch_window, w_query, w_key, w_value, w_out, cotangent):
    byte_count, width = byte_states.shape
    rows, columns = w_query.shape
    span = byte_count + MOST
    padded = -(-span // HDIM) * HDIM
    my_z, my_x, my_y, my_c = (lax.axis_index(name) for name in DP + GRP)
    shape, half, full = jax.ShapeDtypeStruct, jnp.bfloat16, jnp.float32
    barrier = lax.optimization_barrier
    vmem = pl.BlockSpec(memory_space=pltpu.VMEM)
    smem = pl.BlockSpec(memory_space=pltpu.SMEM)
    anywhere = pl.BlockSpec(memory_space=pl.ANY)

    tall = w_out.shape[0] * HDIM // columns
    packed, folded = vmem_call(
        pack_kernel,
        (shape((3 * rows, columns), half), shape((tall, columns), half)),
        in_specs=[anywhere] * 4,
        out_specs=(vmem, vmem),
        limit=64 * 1024 * 1024 - 64 * 1024,
        scratch_shapes=[pltpu.VMEM((3 * rows, columns), full)]
        + [pltpu.VMEM((rows, columns), half)] * 3
        + [pltpu.VMEM(w_out.shape, half), pltpu.SemaphoreType.DMA((4,))],
    )(w_query, w_key, w_value, w_out)
    turns = [packed] + [ring(packed, "x", steps) for steps in (1, 2, 3)]
    turns, folded = barrier((turns, folded))
    deep = 12 * rows
    block = vmem_call(
        order_kernel,
        shape((deep + tall, columns), half),
        in_specs=[smem] + [vmem] * 5,
        out_specs=vmem,
        scratch_shapes=[pltpu.VMEM((deep, columns), full)],
    )(my_x.astype(jnp.int32).reshape(1), *turns, folded)
    block, last_rows, window = barrier((block, byte_states[byte_count - MOST :], patch_window))

    def join(*blocks):
        return vmem_call(functools.partial(join_kernel, deep), shape((len(blocks) * tall, columns), half))(
            *blocks
        )

    def along_x(piece):
        return [piece, ring(piece, "x", 1), None, ring(piece, "x", -1)]

    ring_z = {0: block, 1: ring(block, "z", 1), 7: ring(block, "z", -1)}
    before = from_behind(last_rows, 1)
    cot_y = [cotangent, ring(cotangent, "y", 1), None, ring(cotangent, "y", -1)]
    patch_ids = window[:, :span]
    first_patch = window[0, MOST]
    patch_total = window[0, span] - first_patch
    relative = patch_ids - first_patch
    owned = (relative >= 0) & (relative < patch_total)
    segment = jnp.where(owned, relative, PCAP)
    segment_row = jnp.pad(segment, ((0, 0), (0, padded - span)), constant_values=PCAP)
    segment_col = segment.reshape(span, 1)
    base = (lax.axis_index(DP) - 2) * PAT_DEV - first_patch
    place = jnp.stack([my_z, my_x, my_y, my_c, base]).astype(jnp.int32)
    gain = norm_gain[None, :]
    masks = vmem_call(
        mask_kernel,
        (
            shape((PCAP, padded), half),
            shape((span, PCAP), half),
            shape((5 * PAT_DEV, PCAP), half),
            shape((PCAP, 1), full),
        ),
        in_specs=[smem, vmem, vmem],
        out_specs=(vmem,) * 4,
    )(place, segment_row, segment_col)
    ring_z[1], ring_z[7], before, cot_y[1::2], place, segment_row, gain, masks, states = barrier(
        (ring_z[1], ring_z[7], before, cot_y[1::2], place, segment_row, gain, masks, byte_states)
    )
    member, reader, chosen, sizes = masks
    ring_z[2], ring_z[6] = ring(ring_z[1], "z", 1), ring(ring_z[7], "z", -1)
    out_x = [along_x(join(block, ring_z[1], ring_z[7]))]
    cot_y[2] = ring(cot_y[1], "y", 1)
    normed, pooled = vmem_call(
        prepare_kernel,
        (shape((span, width), half), shape((PCAP, width), half)),
        in_specs=[vmem] * 5,
        out_specs=(vmem,) * 2,
    )(before, states, gain, member, sizes)
    ring_z[2], ring_z[6], out_x[0][1::2], cot_y[2], normed, pooled = barrier(
        (ring_z[2], ring_z[6], out_x[0][1::2], cot_y[2], normed, pooled)
    )
    ring_z[3], ring_z[5] = ring(ring_z[2], "z", 1), ring(ring_z[6], "z", -1)
    out_x[0][2] = ring(out_x[0][1], "x", 1)
    out_x.append(along_x(join(ring_z[2], ring_z[6])))
    cot_mine = jnp.stack(cot_y)
    ring_z[3], ring_z[5], out_x[0][2], out_x[1][1::2], cot_mine = barrier(
        (ring_z[3], ring_z[5], out_x[0][2], out_x[1][1::2], cot_mine)
    )
    mid = (deep + tall) // 2
    last_a, last_b = ring(ring_z[3][:mid], "z", 1), ring(ring_z[5][mid:], "z", -1)
    out_x[1][2] = ring(out_x[1][1], "x", 1)
    cot_other = ring(cot_mine, "c", 1)

    def unfold(sources):
        return vmem_call(
            unfold_kernel,
            shape((sources[0].shape[0] // tall, columns, columns), half),
            in_specs=[smem] + [vmem] * 4,
            out_specs=vmem,
        )(place, *sources)

    weights = [unfold(out_x[0])]
    last_a, last_b, cot_other, ring_z[3], ring_z[5], weights = barrier(
        (last_a, last_b, cot_other, ring_z[3], ring_z[5], weights)
    )
    blocks = [ring_z[0], ring_z[1], ring_z[2], ring_z[3], last_a, last_b]
    blocks += [ring_z[5], ring_z[6], ring_z[7]]
    out_x.append(along_x(join(ring_z[3], ring_z[5], last_b)))

    spot_shape = shape((PAT_DEV, columns), half)
    *places, queries = vmem_call(
        attend_kernel,
        (spot_shape,) * 5 + (shape((PCAP, columns), half),),
        in_specs=[smem] + [vmem] * 6 + [anywhere] * 9,
        out_specs=(vmem,) * 6,
        scratch_shapes=[
            pltpu.VMEM((width, 3 * columns), half),
            pltpu.VMEM((padded, columns), full),
            pltpu.VMEM((columns // HDIM, padded, 2 * HDIM), half),
            pltpu.SemaphoreType.DMA((3,)),
        ],
    )(place, normed, pooled, member, reader, chosen, segment_row, *blocks)
    places, queries, out_x[2][1::2] = barrier((places, queries, out_x[2][1::2]))

    def first_step(spread):
        return from_behind(spread[4], 1), from_behind(spread[0], -1)

    def second_step(spread, up, down):
        lower = from_behind(spread[1] + down, -1)
        return [spread[2], lower, from_behind(spread[3] + up, 1)]

    up, down = first_step(places)
    out_x[2][2] = ring(out_x[2][1], "x", 1)
    asked = vmem_call(place_kernel, (spot_shape,) * 5)(chosen, queries)
    weights.append(unfold(out_x[1]))
    up, down, asked, weights = barrier((up, down, asked, weights))
    pieces = second_step(places, up, down)
    asked_up, asked_down = first_step(asked)
    weights.append(unfold(out_x[2]))
    pieces, weights, asked = barrier((pieces, weights, asked))

    def terms(partner):
        return vmem_call(
            functools.partial(term_kernel, partner),
            shape((4, PAT_DEV, columns), half),
            in_specs=[smem] + [vmem] * 3 + [anywhere] * 3,
            out_specs=vmem,
            scratch_shapes=[
                pltpu.VMEM((4, columns, columns), half),
                pltpu.SemaphoreType.DMA((4,)),
            ],
        )(place, *pieces, *weights)

    theirs = terms(True)
    theirs, asked_up, asked_down = barrier((theirs, asked_up, asked_down))
    arrived = ring(theirs, "c", 1)
    mine = terms(False)
    asked = second_step(asked, asked_up, asked_down)
    arrived, mine = barrier((arrived, mine))
    paired = [(mine[d].astype(full) + arrived[d].astype(full)).astype(half) for d in range(4)]
    mixed = [paired[0]] + [ring(paired[steps], "y", steps) for steps in (2, 1, 3)]
    asked, cot_other = barrier((asked, cot_other))
    gradient = vmem_call(
        gradient_kernel,
        shape((PAT_DEV, columns), full),
        in_specs=[smem, vmem, vmem] + [anywhere] * 3,
        out_specs=vmem,
        scratch_shapes=[
            pltpu.VMEM((8, columns, columns), half),
            pltpu.SemaphoreType.DMA((8,)),
        ],
    )(place, cot_mine, cot_other, *weights)
    mixed, gradient = barrier((mixed, gradient))
    queries = asked[0].astype(full) + asked[1].astype(full) + asked[2].astype(full)
    mixed = (mixed[0].astype(full) + mixed[1].astype(full)) + (
        mixed[2].astype(full) + mixed[3].astype(full)
    )
    patch_rows = (queries + mixed).astype(half)
    return (patch_rows, gradient)


def solution(mesh):
    fine = Mesh(mesh.devices.reshape(8, 4, 4, 2), DP + GRP)
    return jax.shard_map(
        per_device,
        mesh=fine,
        in_specs=(
            P(DP, None),
            P(),
            P(DP, None),
            P(DP, GRP),
            P(DP, GRP),
            P(DP, GRP),
            P(GRP, DP),
            P(DP, GRP),
        ),
        out_specs=(P(DP, GRP), P(DP, GRP)),
        check_vma=False,
    )
```
